32 devices in a mesh: dp: 8 (over y, x, core), tensor: 4 (over z).
Axes of the slice: x: 2, y: 2, z: 4, core: 2. Of those that a mesh axis runs over, the one named last changes fastest.
Arguments:
- tokens: bfloat16 [4096, 768], P('dp'), may hold values from -6 to 6
- segments: int32 [16, 256], P('dp'), may hold values from 0 to 3, never falling along the last dimension, each value on 1 to 128 neighbouring positions
- cotangent: bfloat16 [4096, 768], P('dp'), may hold values from -6 to 6
- w_qkv: float32 [3, 768, 768], P(None, None, 'tensor'), may hold values from -0.21875 to 0.21875
- w_out: float32 [768, 768], P('tensor'), may hold values from -0.625 to 0.625
- w_up: float32 [768, 3072], P(None, 'tensor'), may hold values from -0.21875 to 0.21875
- w_down: float32 [3072, 768], P('tensor'), may hold values from -0.109375 to 0.109375
- head_bias: float32 [2, 768], P(None, 'tensor'), may hold values from -1.8 to 1.8
- ff_bias: float32 [3072], P('tensor'), may hold values from -1.8 to 1.8
- row_params: float32 [6, 768], replicated
- mom_qkv: float32 [3, 768, 768], P(None, None, 'tensor')
- mom_out: float32 [768, 768], P('tensor')
- mom_up: float32 [768, 3072], P(None, 'tensor')
- mom_down: float32 [3072, 768], P('tensor')
- mom_heads: float32 [2, 768], P(None, 'tensor')
- mom_ff: float32 [3072], P('tensor')
- mom_params: float32 [6, 768], replicated, may hold values from -192 to 192
Outputs:
- layer_out: bfloat16 [4096, 768], P('dp')
- grad_tokens: bfloat16 [4096, 768], P('dp')
- new_mom_qkv: float32 [3, 768, 768], P(None, None, 'tensor')
- new_qkv: float32 [3, 768, 768], P(None, None, 'tensor')
- low_qkv: bfloat16 [3, 768, 768], P(None, None, 'tensor')
- new_mom_out: float32 [768, 768], P('tensor')
- new_out: float32 [768, 768], P('tensor')
- low_out: bfloat16 [768, 768], P('tensor')
- new_mom_up: float32 [768, 3072], P(None, 'tensor')
- new_up: float32 [768, 3072], P(None, 'tensor')
- low_up: bfloat16 [768, 3072], P(None, 'tensor')
- new_mom_down: float32 [3072, 768], P('tensor')
- new_down: float32 [3072, 768], P('tensor')
- low_down: bfloat16 [3072, 768], P('tensor')
- new_mom_heads: float32 [2, 768], P(None, 'tensor')
- new_heads: float32 [2, 768], P(None, 'tensor')
- new_mom_ff: float32 [3072], P('tensor')
- new_ff: float32 [3072], P('tensor')
- new_mom_params: float32 [6, 768], replicated
- new_params: float32 [6, 768], replicated
The draws below stay inside these ranges and needn't reach their ends.
Inputs may be any that keep to these rules, and one draw needn't show every extreme that they name: `segments`: within each row of 256 positions the numbers never fall; each number present covers 1 to 128 positions, and one covers exactly 128.
All inputs are finite; a program needn't handle non-finite values.
Results may differ from the reference program's by a relative error of at most 0.024.
Values may be sent and summed in bfloat16 or wider, within the bound.
A program may use at most 192 MiB of HBM per device.

```python
import math
import jax
import jax.numpy as jnp
import numpy as np
from jax import lax

D = 768
H = 12
HD = 64
FF = 3072
LEN = 256
NS_STEPS = 5
SEQS = 16
TOKENS = 4096
N_TENSOR = 4


def rising(values, shape, axis, top, factor):
    count = shape[axis]
    ramp_shape = [1] * len(shape)
    ramp_shape[axis] = count
    ramp = 1.0 + (top - 1.0) * jnp.arange(count, dtype=jnp.float32) / max(count - 1, 1)
    return values * ramp.reshape(ramp_shape) * (factor * TOKENS ** 0.5)


def draw_mom_qkv(key, part):
    key = jax.random.fold_in(key, 11)
    shape = (3, D, D)
    values = jnp.clip(jax.random.normal(key, shape, jnp.float32), -3.0, 3.0)
    top = 3.0
    return rising(values, shape, 2, top, 0.1)


def draw_mom_out(key, part):
    key = jax.random.fold_in(key, 12)
    shape = (D, D)
    values = jnp.clip(jax.random.normal(key, shape, jnp.float32), -3.0, 3.0)
    top = 3.0
    return rising(values, shape, 0, top, 0.1)


def draw_mom_up(key, part):
    key = jax.random.fold_in(key, 13)
    shape = (D, FF)
    values = jnp.clip(jax.random.normal(key, shape, jnp.float32), -3.0, 3.0)
    top = 3.0
    return rising(values, shape, 1, top, 0.2)


def draw_mom_down(key, part):
    key = jax.random.fold_in(key, 14)
    shape = (FF, D)
    values = jnp.clip(jax.random.normal(key, shape, jnp.float32), -3.0, 3.0)
    top = 3.0
    return rising(values, shape, 0, top, 0.4)


def draw_mom_heads(key, part):
    key = jax.random.fold_in(key, 15)
    shape = (2, D)
    values = jnp.clip(jax.random.normal(key, shape, jnp.float32), -3.0, 3.0)
    top = 3.0
    return rising(values, shape, 1, top, 0.3)


def draw_mom_ff(key, part):
    key = jax.random.fold_in(key, 16)
    shape = (FF,)
    values = jnp.clip(jax.random.normal(key, shape, jnp.float32), -3.0, 3.0)
    top = 3.0
    return rising(values, shape, 0, top, 0.3)


def draw_row_params(key, part):
    key = jax.random.fold_in(key, 17)
    values = jnp.clip(jax.random.normal(key, (6, D), jnp.float32), -3.0, 3.0)
    row_ids = jnp.arange(6)[:, None]
    is_gain = (row_ids == 2) | (row_ids == 4)
    return jnp.where(is_gain, 1.0 + 0.15 * values, 0.3 * values)


def level_of(stream_key, shape, cuts, low, top_value):
    level = 1.0
    for axis_at, blocks in cuts:
        heights = jax.random.uniform(jax.random.fold_in(jax.random.fold_in(stream_key, 6), axis_at), (blocks,), jnp.float32, low / len(cuts), top_value / len(cuts))
        level = level * jnp.repeat(jnp.exp(heights), shape[axis_at] // blocks).reshape((-1,) + (1,) * (len(shape) - 1 - axis_at))
    return level


def split_up(number_of, total, bound, skew):
    weights = [(1 << 20) // math.isqrt(grade ** skew) + 1 for grade in range(2, number_of + 1)]
    rest, counts = total - bound - (number_of - 1), [1] * (number_of - 1)
    while rest > 0:
        movable = [i for i in range(number_of - 1) if counts[i] < bound]
        mass, remaining = sum([weights[i] for i in movable]), rest
        for i in movable:
            addition = min(bound - counts[i], max(1, remaining * weights[i] // mass), rest)
            counts[i] = counts[i] + addition
            rest = rest - addition
    return np.array([bound] + counts)


def ragged_sizes(rng, count, total, bound, slope):
    if count == 2:
        one = jax.random.randint(rng, (), max(1, total - bound), min(bound, total - 1) + 1)
        return jnp.stack([one, total - one])
    tallies = jnp.asarray(split_up(count, total, bound, slope), jnp.int32)
    couples = (count - 1) // 2
    source_of, receiver = tallies[1:1 + 2 * couples:2], tallies[2:2 + 2 * couples:2]
    room = jnp.minimum(source_of - 1, bound - receiver)
    shifted = jax.random.randint(jax.random.fold_in(rng, 1), (couples,), 0, 1 << 20) % (room + 1)
    tallies = tallies.at[1:1 + 2 * couples:2].set(source_of - shifted).at[2:2 + 2 * couples:2].set(receiver + shifted)
    return tallies[jax.random.permutation(jax.random.fold_in(rng, 2), count)]


def noise(stream_key, dims, spread, reach, shards=(), held_as=jnp.bfloat16):
    values = spread * jax.random.normal(stream_key, dims, jnp.float32)
    if shards:
        values = values * level_of(stream_key, dims, shards, -0.22, 0.18)
    return jnp.clip(values, -reach, reach).astype(held_as)


def setup_inputs(seed: int = 0) -> dict:
    key_list = jax.random.split(jax.random.key(seed), 18)
    tokens = noise(key_list[0], (TOKENS, D), 1.0, 6.0, ((0, 8),))
    segments = jax.vmap(lambda own: jnp.searchsorted(jnp.cumsum(ragged_sizes(own, 4, LEN, LEN // 2, 0)), jnp.arange(LEN), side="right"))(jax.random.split(key_list[1], SEQS)).reshape((SEQS, LEN)).astype(jnp.int32)
    cotangent = noise(key_list[2], (TOKENS, D), 1.0, 6.0, ((0, 8),))
    w_qkv = noise(key_list[3], (3, D, D), D ** -0.5, 0.21875, ((2, 4),), jnp.float32)
    w_out = noise(key_list[4], (D, D), (D // 8) ** -0.5, 0.625, ((0, 4),), jnp.float32)
    w_up = noise(key_list[5], (D, FF), D ** -0.5, 0.21875, ((1, 4),), jnp.float32)
    w_down = noise(key_list[6], (FF, D), FF ** -0.5, 0.109375, ((0, 4),), jnp.float32)
    head_bias = noise(key_list[7], (2, D), 0.3, 1.8, ((1, 4),), jnp.float32)
    ff_bias = noise(key_list[8], (FF,), 0.3, 1.8, ((0, 4),), jnp.float32)
    row_params = draw_row_params(jax.random.fold_in(key_list[17], 71), 0)
    mom_qkv = draw_mom_qkv(jax.random.fold_in(key_list[17], 71), 0)
    mom_out = draw_mom_out(jax.random.fold_in(key_list[17], 71), 0)
    mom_up = draw_mom_up(jax.random.fold_in(key_list[17], 71), 0)
    mom_down = draw_mom_down(jax.random.fold_in(key_list[17], 71), 0)
    mom_heads = draw_mom_heads(jax.random.fold_in(key_list[17], 71), 0)
    mom_ff = draw_mom_ff(jax.random.fold_in(key_list[17], 71), 0)
    mom_params = noise(key_list[16], (6, D), (0.5 * TOKENS ** 0.5), 192.0, (), jnp.float32)
    return {"tokens": tokens, "segments": segments, "cotangent": cotangent, "w_qkv": w_qkv, "w_out": w_out, "w_up": w_up, "w_down": w_down, "head_bias": head_bias, "ff_bias": ff_bias, "row_params": row_params, "mom_qkv": mom_qkv, "mom_out": mom_out, "mom_up": mom_up, "mom_down": mom_down, "mom_heads": mom_heads, "mom_ff": mom_ff, "mom_params": mom_params}


@jax.custom_vjp
def low(v):
    return lax.optimization_barrier(v.astype(jnp.bfloat16)).astype(jnp.float32)

@jax.custom_vjp
def low_back(v):
    return v

def low_keep(v):
    return (low(v), None)

def low_pass(kept, grad):
    return (grad,)

def back_keep(v):
    return (v, None)

def back_low(kept, grad):
    return (low(grad),)
low.defvjp(low_keep, low_pass)
low_back.defvjp(back_keep, back_low)
HIGHEST = lax.Precision.HIGHEST
EPS_NORM = 1e-05
coef_a = 3.4445
coef_b = -4.775
coef_c = 2.0315

def hdot(left, right):
    return jnp.dot(left, right, precision=HIGHEST)

def layer_norm(values, gain, shift):
    center = values - lax.optimization_barrier(jnp.mean(values, axis=-1, keepdims=True))
    inverse = lax.rsqrt(lax.optimization_barrier(jnp.mean(center * center, axis=-1, keepdims=True)) + EPS_NORM)
    return center * inverse * gain + shift

def layer(params, inputs, seg_rows):
    w_qkv, w_out, w_up, w_down, head_bias, ff_bias, row_params = params
    groups, length = seg_rows.shape
    query = low_back(low(hdot(inputs, low(w_qkv[0])) + head_bias[0]))
    keys = low_back(low(hdot(inputs, low(w_qkv[1]))))
    values = low_back(low(hdot(inputs, low(w_qkv[2])) + head_bias[1]))
    query = query.reshape(groups, length, H, HD)
    keys = keys.reshape(groups, length, H, HD)
    values = values.reshape(groups, length, H, HD)
    scores = jnp.einsum('gqhd,gkhd->ghqk', query, keys, precision=HIGHEST) / math.sqrt(HD)
    scores = low_back(scores)
    same_seg = (seg_rows[:, :, None] == seg_rows[:, None, :])[:, None]
    scores = jnp.where(same_seg, scores, -1e+30)
    probs = low(jax.nn.softmax(scores, axis=-1))
    context = jnp.einsum('ghqk,gkhd->gqhd', probs, values, precision=HIGHEST)
    context = low_back(low(context.reshape(groups * length, D)))
    attn = low_back(hdot(context, low(w_out)))
    hidden_one = layer_norm(inputs + attn + row_params[0], row_params[2], row_params[3])
    upward = low_back(hdot(low(hidden_one), low(w_up)) + ff_bias)
    activated = low(jax.nn.gelu(upward, approximate=False))
    mlp = low_back(hdot(activated, low(w_down)))
    return layer_norm(hidden_one + mlp + row_params[1], row_params[4], row_params[5])

def row_blocks(w_qkv, w_out, w_up, w_down):
    count = N_TENSOR
    cols = D // count
    part = FF // count
    blk_qkv = w_qkv.reshape(3, D, count, cols).transpose(2, 0, 3, 1).reshape(count, 3 * cols, D)
    blk_out = w_out.reshape(count, cols, D)
    blk_up = w_up.reshape(D, count, part).transpose(1, 2, 0)
    blk_down = w_down.reshape(count, part, D)
    return [blk_qkv, blk_out, blk_up, blk_down]

def orthogonal(block):
    total = jnp.sum(block * block)
    iterate = block / (jnp.sqrt(total) + 1e-07)
    for sweep in range(NS_STEPS):
        partial_grams = jnp.einsum('nrd,nre->nde', iterate, iterate, precision=HIGHEST)
        rounded = lax.optimization_barrier(partial_grams.astype(jnp.bfloat16)).astype(jnp.float32)
        gram_sum = lax.optimization_barrier(jnp.sum(rounded, axis=0))
        product = jnp.einsum('nrd,de->nre', iterate, gram_sum, precision=HIGHEST)
        second = jnp.einsum('nrd,de->nre', product, gram_sum, precision=HIGHEST)
        iterate = coef_a * iterate + coef_b * product + coef_c * second
    return iterate

def vector_step(param, moment):
    mean_sq = lax.optimization_barrier(jnp.mean(moment * moment, axis=-1, keepdims=True))
    return param - 0.1 * moment * lax.rsqrt(mean_sq + 1e-06)

def reference(tokens, segments, cotangent, w_qkv, w_out, w_up, w_down, head_bias, ff_bias, row_params, mom_qkv, mom_out, mom_up, mom_down, mom_heads, mom_ff, mom_params):
    params = (w_qkv, w_out, w_up, w_down, head_bias, ff_bias, row_params)
    group = math.gcd(SEQS, 16)
    count = SEQS // group
    tok_groups = tokens.astype(jnp.float32).reshape(count, group * LEN, D)
    seg_groups = segments.reshape(count, group, LEN)
    cot_groups = cotangent.astype(jnp.float32).reshape(count, group * LEN, D)

    def one_group(carry, item):
        inputs, seg_rows, cot_rows = item
        result, pullback = jax.vjp(lambda weights, rows: layer(weights, rows, seg_rows), params, inputs)
        grad_params, grad_rows = pullback(cot_rows)
        carry = jax.tree.map(lambda acc, new: acc + new, carry, grad_params)
        return (carry, (result.astype(jnp.bfloat16), grad_rows.astype(jnp.bfloat16)))
    zeros = jax.tree.map(jnp.zeros_like, params)
    grads, (outputs, grad_inputs) = lax.scan(one_group, zeros, (tok_groups, seg_groups, cot_groups))
    layer_out = outputs.reshape(TOKENS, D)
    grad_tokens = grad_inputs.reshape(TOKENS, D)
    g_qkv, g_out, g_up, g_down, g_heads, g_ff, g_params = grads
    new_mom_qkv = 0.5 * mom_qkv + g_qkv
    new_mom_out = 0.5 * mom_out + g_out
    new_mom_up = 0.5 * mom_up + g_up
    new_mom_down = 0.5 * mom_down + g_down
    new_mom_heads = 0.5 * mom_heads + g_heads
    new_mom_ff = 0.5 * mom_ff + g_ff
    new_mom_params = 0.5 * mom_params + g_params
    blocks = row_blocks(new_mom_qkv, new_mom_out, new_mom_up, new_mom_down)
    orth = [orthogonal(block) for block in blocks]
    cols = D // N_TENSOR
    part = FF // N_TENSOR
    orth_qkv = orth[0].reshape(N_TENSOR, 3, cols, D).transpose(1, 3, 0, 2).reshape(3, D, D)
    orth_out = orth[1].reshape(D, D)
    orth_up = orth[2].transpose(2, 0, 1).reshape(D, FF)
    orth_down = orth[3].reshape(FF, D)
    wide = math.sqrt(FF / D)
    new_qkv = w_qkv - 0.8 * math.sqrt(3.0) * orth_qkv
    new_out = w_out - 0.8 * orth_out
    new_up = w_up - 0.8 * wide * orth_up
    new_down = w_down - 0.8 * wide * orth_down
    new_heads = vector_step(head_bias, new_mom_heads)
    new_ff = vector_step(ff_bias, new_mom_ff)
    new_params = vector_step(row_params, new_mom_params)
    return (layer_out, grad_tokens, new_mom_qkv, new_qkv, new_qkv.astype(jnp.bfloat16), new_mom_out, new_out, new_out.astype(jnp.bfloat16), new_mom_up, new_up, new_up.astype(jnp.bfloat16), new_mom_down, new_down, new_down.astype(jnp.bfloat16), new_mom_heads, new_heads, new_mom_ff, new_ff, new_mom_params, new_params)
```

```python
import functools
import math

import jax
import jax.numpy as jnp
from jax import lax
from jax.experimental import pallas as pl
from jax.experimental.pallas import tpu as pltpu
from jax.sharding import PartitionSpec as P

HD = 64
EPS_NORM = 1e-05
coef_a = 3.4445
coef_b = -4.775
coef_c = 2.0315
BF = jnp.bfloat16
F32 = jnp.float32
MESH = pl.DeviceIdType.MESH
SUBS = 2
VMEM_LIMIT = 56 * 1024 * 1024


def remote(src, dst, send_sem, recv_sem, device):
    return pltpu.make_async_remote_copy(
        src_ref=src,
        dst_ref=dst,
        send_sem=send_sem,
        recv_sem=recv_sem,
        device_id=device,
        device_id_type=MESH,
    )


def greet(devices):
    barrier = pltpu.get_barrier_semaphore()
    for device in devices:
        pl.semaphore_signal(barrier, inc=1, device_id=device, device_id_type=MESH)
    pl.semaphore_wait(barrier, len(devices))


def z_peers(t):
    return [{"tensor": (t + k) % 4} for k in range(1, 4)]


def line_scratch(rows, width, dtype):
    part = rows // 4
    return [
        pltpu.VMEM((part, width), dtype),
        pltpu.VMEM((part, width), dtype),
        pltpu.VMEM((2 * part, width), dtype),
        pltpu.VMEM((2 * part, width), dtype),
        pltpu.SemaphoreType.DMA((8 * SUBS,)),
        pltpu.SemaphoreType.DMA((8 * SUBS,)),
    ]


def line_sum(t, x, o, scratch):
    raw, cmb, fwd, mix, ssem, rsem = scratch
    part = raw.shape[0]
    half = part // SUBS
    subs = range(SUBS)
    mate = t + 1 - 2 * (t % 2)
    outer = (t % 3) == 0
    inner = (t % 3) != 0

    def at(ref, chunk, s):
        return ref.at[pl.ds(pl.multiple_of(chunk * part + s * half, half), half)]

    def to(index, src, dst, recv, device):
        return remote(src, dst, ssem.at[index], rsem.at[recv], {"tensor": device})

    def ag_sem(chunk, s):
        return (4 + chunk) * SUBS + s

    def o_far(s):
        return to(s, at(x, 3 - t, s), at(fwd, 0, s), 2 * SUBS + s, mate)

    def o_near(s):
        return to(SUBS + s, at(x, 3 - mate, s), at(fwd, 1, s), 3 * SUBS + s, mate)

    def o_raw(s):
        return to(2 * SUBS + s, at(x, mate, s), at(raw, 0, s), s, mate)

    def o_own(s):
        return to(3 * SUBS + s, at(o, t, s), at(o, t, s), ag_sem(t, s), mate)

    def i_raw(s):
        return to(s, at(x, mate, s), at(raw, 0, s), s, mate)

    def i_far(s):
        return to(SUBS + s, at(mix, 0, s), at(cmb, 0, s), SUBS + s, 3 - mate)

    def i_near(s):
        return to(2 * SUBS + s, at(mix, 1, s), at(cmb, 0, s), SUBS + s, 3 - t)

    def i_ag(place, chunk, s, device):
        return to(place * SUBS + s, at(o, chunk, s), at(o, chunk, s), ag_sem(chunk, s), device)

    def got(dst, recv):
        remote(dst, dst, ssem.at[0], rsem.at[recv], {"tensor": mate}).wait_recv()

    def add(dst, *terms):
        total = terms[0][...].astype(F32)
        for term in terms[1:]:
            total = total + term[...].astype(F32)
        dst[...] = total.astype(dst.dtype)

    def start():
        @pl.when(outer)
        def _():
            for build in (o_far, o_near, o_raw):
                for s in subs:
                    build(s).start()

        @pl.when(inner)
        def _():
            for s in subs:
                i_raw(s).start()

    def combine():
        @pl.when(inner)
        def _():
            for slot, chunk, build in ((0, 3 - mate, i_far), (1, 3 - t, i_near)):
                for s in subs:
                    got(at(fwd, slot, s), (2 + slot) * SUBS + s)
                    add(at(mix, slot, s), at(fwd, slot, s), at(x, chunk, s))
                    build(s).start()

    def settle():
        for s in subs:
            got(at(raw, 0, s), s)
            got(at(cmb, 0, s), SUBS + s)
            add(at(o, t, s), at(x, t, s), at(raw, 0, s), at(cmb, 0, s))

            @pl.when(outer)
            def _(s=s):
                o_own(s).start()

            @pl.when(inner)
            def _(s=s):
                i_ag(3, t, s, 3 - t).start()
                i_ag(4, t, s, mate).start()

    def pass_on():
        @pl.when(inner)
        def _():
            for s in subs:
                got(at(o, mate, s), ag_sem(mate, s))
                i_ag(5, mate, s, 3 - t).start()
            for s in subs:
                got(at(o, 3 - t, s), ag_sem(3 - t, s))
                i_ag(6, 3 - t, s, mate).start()
            for s in subs:
                got(at(o, 3 - mate, s), ag_sem(3 - mate, s))
                i_ag(7, 3 - mate, s, mate).start()

    def finish():
        @pl.when(outer)
        def _():
            for chunk in (mate, 3 - mate, 3 - t):
                for s in subs:
                    got(at(o, chunk, s), ag_sem(chunk, s))
            for build in (o_far, o_near, o_raw, o_own):
                for s in subs:
                    build(s).wait_send()

        @pl.when(inner)
        def _():
            for s in subs:
                for build in (i_raw, i_far, i_near):
                    build(s).wait_send()
                i_ag(3, t, s, 3 - t).wait_send()
                i_ag(4, t, s, mate).wait_send()
                i_ag(5, mate, s, 3 - t).wait_send()
                i_ag(6, 3 - t, s, mate).wait_send()
                i_ag(7, 3 - mate, s, mate).wait_send()

    return [start, combine, settle, pass_on, finish]


def line_kernel(x, o, *scratch):
    t = lax.axis_index("tensor")
    greet(z_peers(t))
    for step in line_sum(t, x, o, scratch):
        step()


def params(collective_id):
    return pltpu.CompilerParams(
        collective_id=collective_id, has_side_effects=True, vmem_limit_bytes=VMEM_LIMIT
    )


IN_VMEM = pl.BlockSpec(memory_space=pltpu.VMEM)
IN_ANY = pl.BlockSpec(memory_space=pl.ANY)


def sum_tensor(partial, collective_id):
    rows, width = partial.shape
    return pl.pallas_call(
        line_kernel,
        out_shape=jax.ShapeDtypeStruct(partial.shape, partial.dtype),
        in_specs=[IN_VMEM],
        out_specs=IN_VMEM,
        scratch_shapes=line_scratch(rows, width, partial.dtype),
        compiler_params=params(collective_id),
        name="sum_tensor",
    )(partial)


def plane_scratch(count, rows, width):
    pairs = count // 2
    side = width // 2
    block = rows // pairs
    return [
        pltpu.VMEM((rows, side), BF),
        pltpu.VMEM((rows, side), BF),
        pltpu.VMEM((pairs, block, side), BF),
        pltpu.SemaphoreType.DMA((5, pairs)),
        pltpu.SemaphoreType.DMA((4, pairs)),
    ]


def plane_sum(count, p, x, o, scratch):
    from_mate, paired, slots, ssem, rsem = scratch
    pairs = count // 2
    side = from_mate.shape[1]
    block = slots.shape[1]
    pair = p // 2
    core = p % 2
    mate = {"dp": p + 1 - 2 * core}

    def rows_of(index):
        return pl.ds(pl.multiple_of(index * block, block), block)

    def cols_of(which):
        return pl.ds(pl.multiple_of(which * side, side), side)

    def after(k):
        return (pair + k) % pairs

    def before(k):
        return (pair + pairs - k) % pairs

    def give(k):
        spot = rows_of(after(k))
        return remote(
            x.at[spot, cols_of(1 - core)], from_mate.at[spot], ssem.at[0, k % pairs], rsem.at[0, k % pairs], mate
        )

    def hand(k):
        spot = rows_of(after(k))
        return remote(
            paired.at[spot], slots.at[k], ssem.at[1, k], rsem.at[1, k], {"dp": 2 * after(k) + core}
        )

    def spread(k):
        spot = o.at[rows_of(pair), cols_of(core)]
        return remote(spot, spot, ssem.at[2, k], rsem.at[2, k], {"dp": 2 * after(k) + core})

    def share(k):
        spot = o.at[rows_of(before(k)), cols_of(core)]
        return remote(spot, spot, ssem.at[3, k], rsem.at[3, k], mate)

    def start():
        for k in range(1, pairs + 1):
            give(k).start()

    def pair_up():
        for k in range(1, pairs + 1):
            spot = rows_of(after(k))
            give(k).wait_recv()
            total = x[spot, cols_of(core)].astype(F32) + from_mate[spot].astype(F32)
            paired[spot] = total.astype(BF)
            if k < pairs:
                hand(k).start()

    def settle():
        spot = rows_of(pair)
        total = paired[spot].astype(F32)
        for k in range(1, pairs):
            hand(k).wait_recv()
            total = total + slots[k].astype(F32)
        o[spot, cols_of(core)] = total.astype(BF)
        for k in range(1, pairs):
            spread(k).start()
        share(0).start()

    def pass_on():
        for k in range(1, pairs):
            spot = o.at[rows_of(before(k)), cols_of(core)]
            remote(spot, spot, ssem.at[2, k], rsem.at[2, k], mate).wait_recv()
            share(k).start()

    def finish():
        for k in range(pairs):
            spot = o.at[rows_of(before(k)), cols_of(1 - core)]
            remote(spot, spot, ssem.at[3, k], rsem.at[3, k], mate).wait_recv()
        for k in range(1, pairs + 1):
            give(k).wait_send()
        for k in range(1, pairs):
            hand(k).wait_send()
            spread(k).wait_send()
        for k in range(pairs):
            share(k).wait_send()

    return [start, pair_up, settle, pass_on, finish]


def vector_scratch(count, shape):
    return [
        pltpu.VMEM((count,) + shape, F32),
        pltpu.SemaphoreType.DMA((count,)),
        pltpu.SemaphoreType.DMA((count,)),
    ]


def vector_sum(axis, count, p, v, o, scratch):
    slots, ssem, rsem = scratch

    def send(k):
        return remote(v, slots.at[p], ssem.at[k], rsem.at[k], {axis: (p + k) % count})

    def start():
        slots[p] = v[...]
        for k in range(1, count):
            send(k).start()

    def finish():
        for k in range(1, count):
            spot = slots.at[(p + count - k) % count]
            remote(v, spot, ssem.at[k], rsem.at[k], {axis: (p + k) % count}).wait_recv()
        total = slots[0]
        for k in range(1, count):
            total = total + slots[k]
        o[...] = total
        for k in range(1, count):
            send(k).wait_send()

    return [start, finish]


def dp_kernel(count, x, v, o, vo, *scratch):
    p = lax.axis_index("dp")
    greet([{"dp": (p + k) % count} for k in range(1, count)])
    plane = plane_sum(count, p, x, o, scratch[:5])
    vector = vector_sum("dp", count, p, v, vo, scratch[5:])
    vector[0]()
    for step in plane:
        step()
    vector[1]()


def sum_dp(count, grads, vectors, collective_id):
    rows, width = grads.shape
    return pl.pallas_call(
        functools.partial(dp_kernel, count),
        out_shape=(
            jax.ShapeDtypeStruct(grads.shape, BF),
            jax.ShapeDtypeStruct(vectors.shape, F32),
        ),
        in_specs=[IN_VMEM, IN_VMEM],
        out_specs=(IN_VMEM, IN_VMEM),
        scratch_shapes=plane_scratch(count, rows, width) + vector_scratch(count, vectors.shape),
        compiler_params=params(collective_id),
        name="sum_dp",
    )(grads, vectors)


def dp_only_kernel(count, x, o, *scratch):
    p = lax.axis_index("dp")
    greet([{"dp": (p + k) % count} for k in range(1, count)])
    for step in plane_sum(count, p, x, o, scratch):
        step()


def sum_dp_only(count, grads, collective_id):
    rows, width = grads.shape
    return pl.pallas_call(
        functools.partial(dp_only_kernel, count),
        out_shape=jax.ShapeDtypeStruct(grads.shape, BF),
        in_specs=[IN_VMEM],
        out_specs=IN_VMEM,
        scratch_shapes=plane_scratch(count, rows, width),
        compiler_params=params(collective_id),
        name="sum_dp_only",
    )(grads)


def cut(values):
    high = values.astype(BF)
    return high, (values - high.astype(F32)).astype(BF)


def dot3(lh, ll, rh, rl, dims=(((1,), (0,)), ((), ()))):
    def dot(left, right):
        return lax.dot_general(left, right, dims, preferred_element_type=F32)

    return dot(lh, rh) + (dot(lh, rl) + dot(ll, rh))


def muon_kernel(
    count, sizes,
    mq, mo, mu, md, ga, gb, vs,
    xo, vt,
    zf, gf, zh, zl, gx, go, gp, af, ah, al, dh, dl, sf, sh, sl, xf, lsem, psem, asem_s, asem_r, *scratch,
):
    p = lax.axis_index("dp")
    t = lax.axis_index("tensor")
    width = zf.shape[1]
    group = count // 4
    which = p // group
    core = p % 2
    pairs = count // 2
    pair = p // 2
    mate = {"dp": p + 1 - 2 * core}
    share = xf.shape[0]
    tile = width // 3
    greet(z_peers(t) + [{"dp": (p + k) % count} for k in range(1, count)])
    vector = vector_sum("tensor", 4, t, vs, vt, scratch[6:])
    vector[0]()
    qkv_rows, out_rows, _, _ = sizes
    gsrc = (
        (ga, 0, qkv_rows), (ga, qkv_rows, out_rows), (gb, 0, width), (gb, width, width)
    )
    for index, moment in enumerate((mq, mo, mu, md)):
        grads, first, rows = gsrc[index]

        @pl.when(which == index)
        def _(moment=moment, grads=grads, first=first, rows=rows):
            one = pltpu.make_async_copy(moment, zf.at[pl.ds(0, rows)], lsem.at[0])
            two = pltpu.make_async_copy(
                grads.at[pl.ds(first, rows)], gf.at[pl.ds(0, rows)], lsem.at[1]
            )
            one.start()
            two.start()
            if rows < width:
                zf[pl.ds(rows, width - rows)] = jnp.zeros((width - rows, width), F32)
                gf[pl.ds(rows, width - rows)] = jnp.zeros((width - rows, width), BF)
            one.wait()
            two.wait()

    for i in range(3):
        spot = pl.ds(i * tile, tile)
        z = 0.5 * zf[spot] + gf[spot].astype(F32)
        zf[spot] = z
        zh[spot], zl[spot] = cut(z)

    def cols(index):
        return pl.ds(pl.multiple_of(index * tile, tile), tile)

    over_rows = (((0,), (0,)), ((), ()))
    for j, (row, col) in enumerate(((core, core), (core, core + 1), (2 * core, 2))):
        gx[:, pl.ds(j * tile, tile)] = dot3(
            zh[:, cols(row)], zl[:, cols(row)], zh[:, cols(col)], zl[:, cols(col)], over_rows
        )
    for step in line_sum(t, gx, go, scratch[:6]):
        step()
    swap = remote(go, gp, psem.at[0], psem.at[1], mate)
    swap.start()
    swap.wait()
    diagonal = lax.broadcasted_iota(jnp.int32, (tile, tile), 0) == lax.broadcasted_iota(
        jnp.int32, (tile, tile), 1
    )

    def upper(first, second):
        trace = jnp.float32(0.0)
        for block in (first[:, 0:tile], second[:, 0:tile], second[:, 2 * tile :]):
            trace = trace + jnp.sum(jnp.where(diagonal, block, 0.0))
        inverse = 1.0 / (jnp.sqrt(jnp.full((1, 1), trace, F32)) + 1e-07)
        scale = inverse * inverse
        blocks = (
            (0, 0, first, 0), (0, 1, first, 1), (0, 2, first, 2),
            (1, 1, second, 0), (1, 2, second, 1), (2, 2, second, 2),
        )
        for row, col, source, j in blocks:
            block = source[:, j * tile : (j + 1) * tile] * scale
            for r, c, value in ((row, col, block),) + (((col, row, block.T),) if row != col else ()):
                spot = (pl.ds(r * tile, tile), pl.ds(c * tile, tile))
                af[spot] = value
                ah[spot], al[spot] = cut(value)
        rank = p % group
        xf[...] = zf[pl.ds(pl.multiple_of(rank * share, share), share)] * inverse

    @pl.when(core == 0)
    def _():
        upper(go, gp)

    @pl.when(core == 1)
    def _():
        upper(gp, go)

    vector[1]()

    def make_d():
        for i in range(3):
            spot = pl.ds(i * tile, tile)
            value = coef_b * af[spot] + coef_c * dot3(ah[spot], al[spot], ah[...], al[...])
            dh[spot], dl[spot] = cut(value)

    def move_x():
        xh, xl = cut(xf[...])
        xf[...] = coef_a * xf[...] + dot3(xh, xl, dh[...], dl[...])

    def sweep(k, carry):
        make_d()
        move_x()
        for i in range(3):
            spot = pl.ds(i * tile, tile)
            value = coef_a * af[spot] + dot3(ah[spot], al[spot], dh[...], dl[...])
            sf[spot] = value
            sh[spot], sl[spot] = cut(value)
        for i in range(3):
            spot = pl.ds(i * tile, tile)
            value = coef_a * sf[spot] + dot3(sh[spot], sl[spot], dh[...], dl[...])
            af[spot] = value
            ah[spot], al[spot] = cut(value)
        return carry

    lax.fori_loop(0, 4, sweep, 0)
    make_d()
    move_x()

    def rows_of(device):
        return xo.at[pl.ds(pl.multiple_of(device * share, share), share)]

    def after(k):
        return 2 * ((pair + k) % pairs) + core

    def before(k):
        return 2 * ((pair + pairs - k) % pairs) + core

    def send(k):
        return remote(rows_of(p), rows_of(p), asem_s.at[0, k], asem_r.at[0, k], {"dp": after(k)})

    def hand(k):
        spot = rows_of(before(k))
        return remote(spot, spot, asem_s.at[1, k], asem_r.at[1, k], mate)

    xo[pl.ds(pl.multiple_of(p * share, share), share)] = xf[...].astype(BF)
    for k in range(1, pairs):
        send(k).start()
    hand(0).start()
    for k in range(1, pairs):
        spot = rows_of(before(k))
        remote(spot, spot, asem_s.at[0, k], asem_r.at[0, k], mate).wait_recv()
        hand(k).start()
    for k in range(pairs):
        spot = rows_of(before(k) + 1 - 2 * core)
        remote(spot, spot, asem_s.at[1, k], asem_r.at[1, k], mate).wait_recv()
    for k in range(1, pairs):
        send(k).wait_send()
    for k in range(pairs):
        hand(k).wait_send()


def muon(count, moments, ga, gb, squares, collective_id):
    width = ga.shape[1]
    tile = width // 3
    share = width // (count // 4)
    pairs = count // 2
    sizes = tuple(moment.shape[0] for moment in moments)

    def vmem(dtype, rows=width, columns=width):
        return pltpu.VMEM((rows, columns), dtype)

    scratch = (
        [vmem(F32), vmem(BF), vmem(BF), vmem(BF)]
        + [vmem(F32, tile)] * 3
        + [vmem(F32), vmem(BF), vmem(BF), vmem(BF), vmem(BF), vmem(F32), vmem(BF), vmem(BF)]
        + [vmem(F32, share)]
        + [pltpu.SemaphoreType.DMA((2,)), pltpu.SemaphoreType.DMA((2,))]
        + [pltpu.SemaphoreType.DMA((2, pairs)), pltpu.SemaphoreType.DMA((2, pairs))]
        + line_scratch(tile, width, F32)
        + vector_scratch(4, squares.shape)
    )
    return pl.pallas_call(
        functools.partial(muon_kernel, count, sizes),
        out_shape=(
            jax.ShapeDtypeStruct((4 * width, width), BF),
            jax.ShapeDtypeStruct(squares.shape, F32),
        ),
        in_specs=[IN_ANY] * 6 + [IN_VMEM],
        out_specs=(IN_VMEM, IN_VMEM),
        scratch_shapes=scratch,
        compiler_params=params(collective_id),
        name="muon",
    )(*moments, ga, gb, squares)


def layer_norm(values, gain, shift):
    center = values - jnp.mean(values, axis=-1, keepdims=True)
    inverse = lax.rsqrt(jnp.mean(center * center, axis=-1, keepdims=True) + EPS_NORM)
    normed = center * inverse
    return (normed * gain + shift, normed, inverse)


def norm_back(grad_out, normed, inverse, gain):
    scaled = grad_out * gain
    first_mean = jnp.mean(scaled, axis=-1, keepdims=True)
    second_mean = jnp.mean(scaled * normed, axis=-1, keepdims=True)
    return inverse * (scaled - first_mean - normed * second_mean)


def gelu_slope(upward):
    cdf_part = 0.5 * (1.0 + jax.scipy.special.erf(upward / math.sqrt(2.0)))
    return cdf_part + upward * jnp.exp(-0.5 * upward * upward) / math.sqrt(2.0 * math.pi)


def dot(left, right):
    return jnp.dot(left, right, preferred_element_type=F32)


def tdot(left, right):
    return lax.dot_general(left, right, (((0,), (0,)), ((), ())), preferred_element_type=F32)


def vector_step(param, moment, mean_sq):
    return param - 0.1 * moment * lax.rsqrt(mean_sq + 1e-06)


def local(
    tokens, segments, cotangent,
    w_qkv, w_out, w_up, w_down, head_bias, ff_bias, row_params,
    mom_qkv, mom_out, mom_up, mom_down, mom_heads, mom_ff, mom_params,
):
    tok_count, width = tokens.shape
    columns = w_qkv.shape[2]
    ff_cols = w_up.shape[1]
    local_heads = columns // HD
    seq_count, seq_len = segments.shape
    score_scale = 1.0 / math.sqrt(HD)
    tensor_size = lax.axis_size("tensor")
    count = lax.axis_size("dp")
    wq_low = w_qkv.astype(BF)
    wo_low = w_out.astype(BF)
    wu_low = w_up.astype(BF)
    wd_low = w_down.astype(BF)

    def split_heads(rows):
        return rows.reshape(seq_count, seq_len, local_heads, HD).transpose(0, 2, 1, 3)

    def join_heads(blocks):
        return blocks.transpose(0, 2, 1, 3).reshape(tok_count, columns)

    query_h = split_heads((dot(tokens, wq_low[0]) + head_bias[0]).astype(BF))
    keys_h = split_heads(dot(tokens, wq_low[1]).astype(BF))
    values_h = split_heads((dot(tokens, wq_low[2]) + head_bias[1]).astype(BF))
    same_seg = (segments[:, :, None] == segments[:, None, :])[:, None]
    scores = (
        jnp.einsum("shqd,shkd->shqk", query_h, keys_h, preferred_element_type=F32) * score_scale
    )
    scores = jnp.where(same_seg, scores, -1e30)
    row_max = jnp.max(scores, axis=-1, keepdims=True)
    expo = jnp.exp(scores - row_max)
    probs = expo / jnp.sum(expo, axis=-1, keepdims=True)
    probs_low = probs.astype(BF)
    context = jnp.einsum("shqk,shkd->shqd", probs_low, values_h, preferred_element_type=F32)
    context_low = join_heads(context.astype(BF))
    attn = sum_tensor(dot(context_low, wo_low).astype(BF), 1).astype(F32)
    first_in = tokens.astype(F32) + attn + row_params[0]
    hidden_one, normed_one, inverse_one = layer_norm(first_in, row_params[2], row_params[3])
    hidden_low = hidden_one.astype(BF)
    upward = dot(hidden_low, wu_low) + ff_bias
    activated_low = jax.nn.gelu(upward, approximate=False).astype(BF)
    mlp = sum_tensor(dot(activated_low, wd_low).astype(BF), 2).astype(F32)
    second_in = hidden_one + mlp + row_params[1]
    output_rows, normed_two, inverse_two = layer_norm(second_in, row_params[4], row_params[5])
    grad_out = cotangent.astype(F32)
    grad_second = norm_back(grad_out, normed_two, inverse_two, row_params[4])
    grad_mlp_low = grad_second.astype(BF)
    grad_act = dot(grad_mlp_low, wd_low.T)
    grad_up_low = (grad_act * gelu_slope(upward)).astype(BF)
    back_hidden = sum_tensor(dot(grad_up_low, wu_low.T).astype(BF), 3).astype(F32)
    grads_b = jnp.concatenate(
        [tdot(grad_up_low, hidden_low).astype(BF), tdot(activated_low, grad_mlp_low).astype(BF)]
    )
    sum_b = sum_dp_only(count, grads_b, 4)
    grad_hidden = back_hidden + grad_second
    grad_first = norm_back(grad_hidden, normed_one, inverse_one, row_params[2])
    grad_attn_low = grad_first.astype(BF)
    grad_context = split_heads(dot(grad_attn_low, wo_low.T).astype(BF))
    grad_values = jnp.einsum("shqk,shqd->shkd", probs_low, grad_context, preferred_element_type=F32)
    grad_probs = jnp.einsum("shqd,shkd->shqk", grad_context, values_h, preferred_element_type=F32)
    grad_scores = (
        probs * (grad_probs - jnp.sum(probs * grad_probs, axis=-1, keepdims=True))
    ).astype(BF)
    grad_query = (
        jnp.einsum("shqk,shkd->shqd", grad_scores, keys_h, preferred_element_type=F32) * score_scale
    )
    grad_keys = (
        jnp.einsum("shqk,shqd->shkd", grad_scores, query_h, preferred_element_type=F32)
        * score_scale
    )
    gq_low = join_heads(grad_query.astype(BF))
    gk_low = join_heads(grad_keys.astype(BF))
    gv_low = join_heads(grad_values.astype(BF))
    grads_a = jnp.concatenate(
        [
            tdot(jnp.concatenate([gq_low, gk_low, gv_low], axis=1), tokens).astype(BF),
            tdot(context_low, grad_attn_low).astype(BF),
        ]
    )

    def over_rows(values):
        return jnp.sum(values, axis=0)

    heads_part = jnp.concatenate(
        [
            over_rows(gq_low.astype(F32)),
            over_rows(gv_low.astype(F32)),
            jnp.zeros((width - 2 * columns,), F32),
        ]
    )
    vectors = jnp.stack(
        [
            over_rows(grad_first),
            over_rows(grad_second),
            over_rows(grad_hidden * normed_one),
            over_rows(grad_hidden),
            over_rows(grad_out * normed_two),
            over_rows(grad_out),
            over_rows(grad_up_low.astype(F32)),
            heads_part,
        ]
    )
    sum_a, vector_total = sum_dp(count, grads_a, vectors, 5)
    param_sum = vector_total[0:6]
    ff_own = vector_total[6]
    heads_own = vector_total[7, : 2 * columns].reshape(2, columns)
    new_mom_heads = 0.5 * mom_heads + heads_own
    new_mom_ff = 0.5 * mom_ff + ff_own
    new_mom_params = 0.5 * mom_params + param_sum
    squares = jnp.broadcast_to(
        jnp.concatenate(
            [
                jnp.sum(new_mom_heads * new_mom_heads, axis=1),
                jnp.sum(new_mom_ff * new_mom_ff)[None],
                jnp.zeros((5,), F32),
            ]
        )[:, None],
        (8, 128),
    )
    qkv_rows = 3 * columns
    moments = (
        mom_qkv.transpose(0, 2, 1).reshape(qkv_rows, width),
        mom_out,
        mom_up.T,
        mom_down,
    )
    steps, totals = muon(count, moments, sum_a, sum_b, squares, 6)
    back_terms = dot(gq_low, wq_low[0].T)
    back_terms = back_terms + dot(gk_low, wq_low[1].T)
    back_terms = back_terms + dot(gv_low, wq_low[2].T)
    grad_inputs = sum_tensor(back_terms.astype(BF), 7).astype(F32) + grad_first

    def to_qkv(rows):
        return rows.reshape(3, columns, width).transpose(0, 2, 1)

    new_mom_qkv = 0.5 * mom_qkv + to_qkv(sum_a[:qkv_rows].astype(F32))
    new_mom_out = 0.5 * mom_out + sum_a[qkv_rows:].astype(F32)
    new_mom_up = 0.5 * mom_up + sum_b[:ff_cols].astype(F32).T
    new_mom_down = 0.5 * mom_down + sum_b[ff_cols:].astype(F32)
    wide = math.sqrt(ff_cols * tensor_size / width)
    new_qkv = w_qkv - 0.8 * math.sqrt(3.0) * to_qkv(steps[:qkv_rows].astype(F32))
    new_out = w_out - 0.8 * steps[width : width + columns].astype(F32)
    new_up = w_up - 0.8 * wide * steps[2 * width : 3 * width].astype(F32).T
    new_down = w_down - 0.8 * wide * steps[3 * width :].astype(F32)
    new_heads = vector_step(head_bias, new_mom_heads, totals[0:2, 0:1] / (columns * tensor_size))
    new_ff = vector_step(ff_bias, new_mom_ff, totals[2, 0] / (ff_cols * tensor_size))
    new_params = vector_step(
        row_params,
        new_mom_params,
        jnp.mean(new_mom_params * new_mom_params, axis=-1, keepdims=True),
    )
    return (
        output_rows.astype(BF),
        grad_inputs.astype(BF),
        new_mom_qkv, new_qkv, new_qkv.astype(BF),
        new_mom_out, new_out, new_out.astype(BF),
        new_mom_up, new_up, new_up.astype(BF),
        new_mom_down, new_down, new_down.astype(BF),
        new_mom_heads, new_heads,
        new_mom_ff, new_ff,
        new_mom_params, new_params,
    )


def solution(mesh):
    placed = (
        P("dp", None), P("dp", None), P("dp", None),
        P(None, None, "tensor"), P("tensor", None), P(None, "tensor"), P("tensor", None),
        P(None, "tensor"), P("tensor"), P(),
        P(None, None, "tensor"), P("tensor", None), P(None, "tensor"), P("tensor", None),
        P(None, "tensor"), P("tensor"), P(),
    )
    triple = ((P(None, None, "tensor"),) * 3, (P("tensor", None),) * 3, (P(None, "tensor"),) * 3)
    return jax.shard_map(
        local,
        mesh=mesh,
        in_specs=placed,
        out_specs=(
            (P("dp", None), P("dp", None))
            + triple[0] + triple[1] + triple[2] + triple[1]
            + (P(None, "tensor"), P(None, "tensor"), P("tensor"), P("tensor"), P(), P())
        ),
        check_vma=False,
    )
```

```python
import functools
import math

import jax
import jax.numpy as jnp
from jax import lax
from jax.experimental import pallas as pl
from jax.experimental.pallas import tpu as pltpu
from jax.sharding import PartitionSpec as P

HD = 64
EPS_NORM = 1e-05
coef_a = 3.4445
coef_b = -4.775
coef_c = 2.0315
BF = jnp.bfloat16
F32 = jnp.float32
MESH = pl.DeviceIdType.MESH
SUBS = 2
VMEM_LIMIT = 56 * 1024 * 1024
PLACE = (1, 2, 0, 3)


def remote(src, dst, send_sem, recv_sem, device):
    return pltpu.make_async_remote_copy(
        src_ref=src,
        dst_ref=dst,
        send_sem=send_sem,
        recv_sem=recv_sem,
        device_id=device,
        device_id_type=MESH,
    )


def greet(devices):
    barrier = pltpu.get_barrier_semaphore()
    for device in devices:
        pl.semaphore_signal(barrier, inc=1, device_id=device, device_id_type=MESH)
    pl.semaphore_wait(barrier, len(devices))


def z_peers(t):
    return [{"tensor": (t + k) % 4} for k in range(1, 4)]


def line_scratch(rows, width, dtype):
    part = rows // 4
    return [
        pltpu.VMEM((part, width), dtype),
        pltpu.VMEM((part, width), dtype),
        pltpu.VMEM((2 * part, width), dtype),
        pltpu.VMEM((2 * part, width), dtype),
        pltpu.SemaphoreType.DMA((8 * SUBS,)),
        pltpu.SemaphoreType.DMA((8 * SUBS,)),
    ]


def line_sum(t, x, o, scratch):
    raw, cmb, fwd, mix, ssem, rsem = scratch
    part = raw.shape[0]
    half = part // SUBS
    subs = range(SUBS)
    mate = t + 1 - 2 * (t % 2)
    outer = (t % 3) == 0
    inner = (t % 3) != 0

    def at(ref, chunk, s):
        return ref.at[pl.ds(pl.multiple_of(chunk * part + s * half, half), half)]

    def to(index, src, dst, recv, device):
        return remote(src, dst, ssem.at[index], rsem.at[recv], {"tensor": device})

    def ag_sem(chunk, s):
        return (4 + chunk) * SUBS + s

    def o_far(s):
        return to(s, at(x, 3 - t, s), at(fwd, 0, s), 2 * SUBS + s, mate)

    def o_near(s):
        return to(SUBS + s, at(x, 3 - mate, s), at(fwd, 1, s), 3 * SUBS + s, mate)

    def o_raw(s):
        return to(2 * SUBS + s, at(x, mate, s), at(raw, 0, s), s, mate)

    def o_own(s):
        return to(3 * SUBS + s, at(o, t, s), at(o, t, s), ag_sem(t, s), mate)

    def i_raw(s):
        return to(s, at(x, mate, s), at(raw, 0, s), s, mate)

    def i_far(s):
        return to(SUBS + s, at(mix, 0, s), at(cmb, 0, s), SUBS + s, 3 - mate)

    def i_near(s):
        return to(2 * SUBS + s, at(mix, 1, s), at(cmb, 0, s), SUBS + s, 3 - t)

    def i_ag(place, chunk, s, device):
        return to(place * SUBS + s, at(o, chunk, s), at(o, chunk, s), ag_sem(chunk, s), device)

    def got(dst, recv):
        remote(dst, dst, ssem.at[0], rsem.at[recv], {"tensor": mate}).wait_recv()

    def add(dst, *terms):
        total = terms[0][...].astype(F32)
        for term in terms[1:]:
            total = total + term[...].astype(F32)
        dst[...] = total.astype(dst.dtype)

    def start():
        @pl.when(outer)
        def _():
            for build in (o_far, o_near, o_raw):
                for s in subs:
                    build(s).start()

        @pl.when(inner)
        def _():
            for s in subs:
                i_raw(s).start()

    def combine():
        @pl.when(inner)
        def _():
            for slot, chunk, build in ((0, 3 - mate, i_far), (1, 3 - t, i_near)):
                for s in subs:
                    got(at(fwd, slot, s), (2 + slot) * SUBS + s)
                    add(at(mix, slot, s), at(fwd, slot, s), at(x, chunk, s))
                    build(s).start()

    def settle():
        for s in subs:
            got(at(raw, 0, s), s)
            got(at(cmb, 0, s), SUBS + s)
            add(at(o, t, s), at(x, t, s), at(raw, 0, s), at(cmb, 0, s))

            @pl.when(outer)
            def _(s=s):
                o_own(s).start()

            @pl.when(inner)
            def _(s=s):
                i_ag(3, t, s, 3 - t).start()
                i_ag(4, t, s, mate).start()

    def pass_on():
        @pl.when(inner)
        def _():
            for s in subs:
                got(at(o, mate, s), ag_sem(mate, s))
                i_ag(5, mate, s, 3 - t).start()
            for s in subs:
                got(at(o, 3 - t, s), ag_sem(3 - t, s))
                i_ag(6, 3 - t, s, mate).start()
            for s in subs:
                got(at(o, 3 - mate, s), ag_sem(3 - mate, s))
                i_ag(7, 3 - mate, s, mate).start()

    def finish():
        @pl.when(outer)
        def _():
            for chunk in (mate, 3 - mate, 3 - t):
                for s in subs:
                    got(at(o, chunk, s), ag_sem(chunk, s))
            for build in (o_far, o_near, o_raw, o_own):
                for s in subs:
                    build(s).wait_send()

        @pl.when(inner)
        def _():
            for s in subs:
                for build in (i_raw, i_far, i_near):
                    build(s).wait_send()
                i_ag(3, t, s, 3 - t).wait_send()
                i_ag(4, t, s, mate).wait_send()
                i_ag(5, mate, s, 3 - t).wait_send()
                i_ag(6, 3 - t, s, mate).wait_send()
                i_ag(7, 3 - mate, s, mate).wait_send()

    return [start, combine, settle, pass_on, finish]


def line_kernel(x, o, *scratch):
    t = lax.axis_index("tensor")
    greet(z_peers(t))
    for step in line_sum(t, x, o, scratch):
        step()


def params(collective_id):
    return pltpu.CompilerParams(
        collective_id=collective_id, has_side_effects=True, vmem_limit_bytes=VMEM_LIMIT
    )


IN_VMEM = pl.BlockSpec(memory_space=pltpu.VMEM)
IN_ANY = pl.BlockSpec(memory_space=pl.ANY)


def sum_tensor(partial, collective_id):
    rows, width = partial.shape
    return pl.pallas_call(
        line_kernel,
        out_shape=jax.ShapeDtypeStruct(partial.shape, partial.dtype),
        in_specs=[IN_VMEM],
        out_specs=IN_VMEM,
        scratch_shapes=line_scratch(rows, width, partial.dtype),
        compiler_params=params(collective_id),
        name="sum_tensor",
    )(partial)


def plane_scratch(count, rows, width):
    pairs = count // 2
    side = width // 2
    block = rows // pairs
    return [
        pltpu.VMEM((rows, side), BF),
        pltpu.VMEM((rows, side), BF),
        pltpu.VMEM((pairs, block, side), BF),
        pltpu.SemaphoreType.DMA((5, pairs)),
        pltpu.SemaphoreType.DMA((4, pairs)),
    ]


def plane_sum(count, p, x, o, scratch):
    from_mate, paired, slots, ssem, rsem = scratch
    pairs = count // 2
    side = from_mate.shape[1]
    block = slots.shape[1]
    pair = p // 2
    core = p % 2
    mate = {"dp": p + 1 - 2 * core}

    def rows_of(index):
        return pl.ds(pl.multiple_of(index * block, block), block)

    def cols_of(which):
        return pl.ds(pl.multiple_of(which * side, side), side)

    def after(k):
        return (pair + k) % pairs

    def before(k):
        return (pair + pairs - k) % pairs

    def give(k):
        spot = rows_of(after(k))
        return remote(
            x.at[spot, cols_of(1 - core)], from_mate.at[spot], ssem.at[0, k % pairs], rsem.at[0, k % pairs], mate
        )

    def hand(k):
        spot = rows_of(after(k))
        return remote(
            paired.at[spot], slots.at[k], ssem.at[1, k], rsem.at[1, k], {"dp": 2 * after(k) + core}
        )

    def spread(k):
        spot = o.at[rows_of(pair), cols_of(core)]
        return remote(spot, spot, ssem.at[2, k], rsem.at[2, k], {"dp": 2 * after(k) + core})

    def share(k):
        spot = o.at[rows_of(before(k)), cols_of(core)]
        return remote(spot, spot, ssem.at[3, k], rsem.at[3, k], mate)

    def start():
        for k in range(1, pairs + 1):
            give(k).start()

    def pair_up():
        for k in range(1, pairs + 1):
            spot = rows_of(after(k))
            give(k).wait_recv()
            total = x[spot, cols_of(core)].astype(F32) + from_mate[spot].astype(F32)
            paired[spot] = total.astype(BF)
            if k < pairs:
                hand(k).start()

    def settle():
        spot = rows_of(pair)
        total = paired[spot].astype(F32)
        for k in range(1, pairs):
            hand(k).wait_recv()
            total = total + slots[k].astype(F32)
        o[spot, cols_of(core)] = total.astype(BF)
        for k in range(1, pairs):
            spread(k).start()
        share(0).start()

    def pass_on():
        for k in range(1, pairs):
            spot = o.at[rows_of(before(k)), cols_of(core)]
            remote(spot, spot, ssem.at[2, k], rsem.at[2, k], mate).wait_recv()
            share(k).start()

    def finish():
        for k in range(pairs):
            spot = o.at[rows_of(before(k)), cols_of(1 - core)]
            remote(spot, spot, ssem.at[3, k], rsem.at[3, k], mate).wait_recv()
        for k in range(1, pairs + 1):
            give(k).wait_send()
        for k in range(1, pairs):
            hand(k).wait_send()
            spread(k).wait_send()
        for k in range(pairs):
            share(k).wait_send()

    return [start, pair_up, settle, pass_on, finish]


def vector_scratch(count, shape):
    return [
        pltpu.VMEM((count,) + shape, F32),
        pltpu.SemaphoreType.DMA((count,)),
        pltpu.SemaphoreType.DMA((count,)),
    ]


def vector_sum(axis, count, p, v, o, scratch):
    slots, ssem, rsem = scratch

    def send(k):
        return remote(v, slots.at[p], ssem.at[k], rsem.at[k], {axis: (p + k) % count})

    def start():
        slots[p] = v[...]
        for k in range(1, count):
            send(k).start()

    def finish():
        for k in range(1, count):
            spot = slots.at[(p + count - k) % count]
            remote(v, spot, ssem.at[k], rsem.at[k], {axis: (p + k) % count}).wait_recv()
        total = slots[0]
        for k in range(1, count):
            total = total + slots[k]
        o[...] = total
        for k in range(1, count):
            send(k).wait_send()

    return [start, finish]


def dp_kernel(count, x, v, o, vo, *scratch):
    p = lax.axis_index("dp")
    greet([{"dp": (p + k) % count} for k in range(1, count)])
    plane = plane_sum(count, p, x, o, scratch[:5])
    vector = vector_sum("dp", count, p, v, vo, scratch[5:])
    vector[0]()
    for step in plane:
        step()
    vector[1]()


def sum_dp(count, grads, vectors, collective_id):
    rows, width = grads.shape
    return pl.pallas_call(
        functools.partial(dp_kernel, count),
        out_shape=(
            jax.ShapeDtypeStruct(grads.shape, BF),
            jax.ShapeDtypeStruct(vectors.shape, F32),
        ),
        in_specs=[IN_VMEM, IN_VMEM],
        out_specs=(IN_VMEM, IN_VMEM),
        scratch_shapes=plane_scratch(count, rows, width) + vector_scratch(count, vectors.shape),
        compiler_params=params(collective_id),
        name="sum_dp",
    )(grads, vectors)


def both_kernel(count, x, g, o, go, *scratch):
    p = lax.axis_index("dp")
    t = lax.axis_index("tensor")
    greet(z_peers(t) + [{"dp": (p + k) % count} for k in range(1, count)])
    line = line_sum(t, x, o, scratch[:6])
    plane = plane_sum(count, p, g, go, scratch[6:])
    for steps in zip(line, plane):
        for step in steps:
            step()


def sum_both(count, partial, grads, collective_id):
    return pl.pallas_call(
        functools.partial(both_kernel, count),
        out_shape=(
            jax.ShapeDtypeStruct(partial.shape, partial.dtype),
            jax.ShapeDtypeStruct(grads.shape, BF),
        ),
        in_specs=[IN_VMEM] * 2,
        out_specs=(IN_VMEM,) * 2,
        scratch_shapes=line_scratch(*partial.shape, partial.dtype)
        + plane_scratch(count, *grads.shape),
        compiler_params=params(collective_id),
        name="sum_both",
    )(partial, grads)


def cut(values):
    high = values.astype(BF)
    return high, (values - high.astype(F32)).astype(BF)


def dot3(lh, ll, rh, rl, dims=(((1,), (0,)), ((), ()))):
    def dot(left, right):
        return lax.dot_general(left, right, dims, preferred_element_type=F32)

    return dot(lh, rh) + (dot(lh, rl) + dot(ll, rh))


def muon_kernel(
    count, sizes,
    mq, mo, mu, md, ga, gb, vs, bx,
    xo, vt, bo,
    zf, gf, zh, zl, gx, go, gp, af, ah, al, dh, dl, sf, sh, sl, xf, lsem, psem, asem_s, asem_r, *scratch,
):
    p = lax.axis_index("dp")
    t = lax.axis_index("tensor")
    width = zf.shape[1]
    group = count // 4
    which = p // group
    core = p % 2
    pairs = count // 2
    pair = p // 2
    mate = {"dp": p + 1 - 2 * core}
    share = xf.shape[0]
    tile = width // 3
    greet(z_peers(t) + [{"dp": (p + k) % count} for k in range(1, count)])
    vector = vector_sum("tensor", 4, t, vs, vt, scratch[12:])
    back = line_sum(t, bx, bo, scratch[6:12])
    vector[0]()
    qkv_rows, out_rows, _, _ = sizes
    gsrc = (
        (ga, 0, qkv_rows), (ga, qkv_rows, out_rows), (gb, 0, width), (gb, width, width)
    )
    for index, moment in enumerate((mq, mo, mu, md)):
        grads, first, rows = gsrc[index]

        @pl.when(which == PLACE[index])
        def _(moment=moment, grads=grads, first=first, rows=rows):
            one = pltpu.make_async_copy(moment, zf.at[pl.ds(0, rows)], lsem.at[0])
            two = pltpu.make_async_copy(
                grads.at[pl.ds(first, rows)], gf.at[pl.ds(0, rows)], lsem.at[1]
            )
            one.start()
            two.start()
            if rows < width:
                zf[pl.ds(rows, width - rows)] = jnp.zeros((width - rows, width), F32)
                gf[pl.ds(rows, width - rows)] = jnp.zeros((width - rows, width), BF)
            one.wait()
            two.wait()

    for i in range(3):
        spot = pl.ds(i * tile, tile)
        z = 0.5 * zf[spot] + gf[spot].astype(F32)
        zf[spot] = z
        zh[spot], zl[spot] = cut(z)

    def cols(index):
        return pl.ds(pl.multiple_of(index * tile, tile), tile)

    over_rows = (((0,), (0,)), ((), ()))
    for j, (row, col) in enumerate(((core, core), (core, core + 1), (2 * core, 2))):
        gx[:, pl.ds(j * tile, tile)] = dot3(
            zh[:, cols(row)], zl[:, cols(row)], zh[:, cols(col)], zl[:, cols(col)], over_rows
        )
    for step in line_sum(t, gx, go, scratch[:6]):
        step()
    swap = remote(go, gp, psem.at[0], psem.at[1], mate)
    swap.start()
    back[0]()
    swap.wait()
    diagonal = lax.broadcasted_iota(jnp.int32, (tile, tile), 0) == lax.broadcasted_iota(
        jnp.int32, (tile, tile), 1
    )

    def upper(first, second):
        trace = jnp.float32(0.0)
        for block in (first[:, 0:tile], second[:, 0:tile], second[:, 2 * tile :]):
            trace = trace + jnp.sum(jnp.where(diagonal, block, 0.0))
        inverse = 1.0 / (jnp.sqrt(jnp.full((1, 1), trace, F32)) + 1e-07)
        scale = inverse * inverse
        blocks = (
            (0, 0, first, 0), (0, 1, first, 1), (0, 2, first, 2),
            (1, 1, second, 0), (1, 2, second, 1), (2, 2, second, 2),
        )
        for row, col, source, j in blocks:
            block = source[:, j * tile : (j + 1) * tile] * scale
            for r, c, value in ((row, col, block),) + (((col, row, block.T),) if row != col else ()):
                spot = (pl.ds(r * tile, tile), pl.ds(c * tile, tile))
                af[spot] = value
                ah[spot], al[spot] = cut(value)
        if group == 2:
            for index, rows in enumerate(sizes):

                @pl.when(which == PLACE[index])
                def _(half=rows // 2):
                    xf[0:half] = zf[pl.ds(pl.multiple_of(core * half, half), half)] * inverse
                    if half < share:
                        xf[half:share] = jnp.zeros((share - half, width), F32)

        else:
            rank = p % group
            xf[...] = zf[pl.ds(pl.multiple_of(rank * share, share), share)] * inverse

    @pl.when(core == 0)
    def _():
        upper(go, gp)

    @pl.when(core == 1)
    def _():
        upper(gp, go)

    vector[1]()

    def product(left, right, base, base_scale, scale, targets):
        (lh, ll), (rh, rl) = left, right
        for i in range(3):
            rows = pl.ds(i * tile, tile)
            for j in range(i, 3):
                columns = pl.ds(j * tile, tile)
                value = base_scale * base[rows, columns] + scale * dot3(
                    lh[rows], ll[rows], rh[:, columns], rl[:, columns]
                )
                for target, part in zip(targets, (*cut(value), value)):
                    target[rows, columns] = part
                    if i != j:
                        target[columns, rows] = part.T

    def make_d():
        product((ah, al), (ah, al), af, coef_b, coef_c, (dh, dl))

    def move_x():
        xh, xl = cut(xf[...])
        xf[...] = coef_a * xf[...] + dot3(xh, xl, dh[...], dl[...])

    def sweep(k, carry):
        make_d()
        move_x()
        product((ah, al), (dh, dl), af, coef_a, 1.0, (sh, sl, sf))
        product((sh, sl), (dh, dl), sf, coef_a, 1.0, (ah, al, af))
        for i in range(1, 4):
            pl.when(k == i - 1)(back[i])
        return carry

    lax.fori_loop(0, 4, sweep, 0)
    make_d()
    move_x()
    back[4]()

    if pairs == 4:
        gather_square(pair, core, mate, sizes, xf, xo, asem_s, asem_r)
    else:
        gather_any(p, core, pairs, mate, xf, xo, asem_s, asem_r)


def gather_square(pair, core, mate, sizes, xf, xo, ssem, rsem):
    width = xf.shape[1]

    def piece(index, side, part):
        half = sizes[index] // 4
        first = index * width + side * 2 * half + part * half
        return xo.at[pl.ds(pl.multiple_of(first, half), half)]

    def copy(index, part, route, device):
        spot = piece(index, core, part)
        return remote(spot, spot, ssem.at[index, part, route], rsem.at[index, part, route], device)

    def other(away):
        return {"dp": 2 * (pair + away * (1 - 2 * ((pair // away) % 2))) + core}

    def place_is(index, away):
        return pair == (PLACE[index] ^ away)

    def wait_in(index, part, route, side):
        spot = piece(index, side, part)
        remote(spot, spot, ssem.at[index, part, route], rsem.at[index, part, route], mate).wait_recv()

    for index, rows in enumerate(sizes):
        half = rows // 4

        @pl.when(place_is(index, 0))
        def _(index=index, half=half):
            for part in range(2):
                piece(index, core, part)[...] = xf[pl.ds(part * half, half)].astype(BF)
            for part in range(2):
                copy(index, part, 0, other(1)).start()
                copy(index, 1 - part, 1, other(2)).start()
            for part in range(2):
                copy(index, part, 3, mate).start()

    for index in range(4):
        for away, route, onward in ((1, 0, 2), (2, 1, 1)):

            @pl.when(place_is(index, away))
            def _(index=index, away=away, route=route, onward=onward):
                first = away - 1
                wait_in(index, first, route, core)
                copy(index, first, 2, other(onward)).start()
                copy(index, first, 3, mate).start()

    for index in range(4):
        for away, route, onward in ((1, 0, 2), (2, 1, 1)):

            @pl.when(place_is(index, away))
            def _(index=index, away=away, route=route):
                second = 2 - away
                wait_in(index, second, route, core)
                copy(index, second, 3, mate).start()

        @pl.when(place_is(index, 3))
        def _(index=index):
            for part in range(2):
                wait_in(index, part, 2, core)
                copy(index, part, 3, mate).start()

    for index in range(4):
        for part in range(2):
            wait_in(index, part, 3, 1 - core)
            copy(index, part, 3, mate).wait_send()

        @pl.when(place_is(index, 0))
        def _(index=index):
            for part in range(2):
                copy(index, part, 0, other(1)).wait_send()
                copy(index, part, 1, other(2)).wait_send()

        for away, onward in ((1, 2), (2, 1)):

            @pl.when(place_is(index, away))
            def _(index=index, away=away, onward=onward):
                copy(index, away - 1, 2, other(onward)).wait_send()


def gather_any(p, core, pairs, mate, xf, xo, asem_s, asem_r):
    pair = p // 2
    share = xf.shape[0]

    def rows_of(device):
        return xo.at[pl.ds(pl.multiple_of(device * share, share), share)]

    def after(k):
        return 2 * ((pair + k) % pairs) + core

    def before(k):
        return 2 * ((pair + pairs - k) % pairs) + core

    def send(k):
        return remote(rows_of(p), rows_of(p), asem_s.at[0, k], asem_r.at[0, k], {"dp": after(k)})

    def hand(k):
        spot = rows_of(before(k))
        return remote(spot, spot, asem_s.at[1, k], asem_r.at[1, k], mate)

    xo[pl.ds(pl.multiple_of(p * share, share), share)] = xf[...].astype(BF)
    for k in range(1, pairs):
        send(k).start()
    hand(0).start()
    for k in range(1, pairs):
        spot = rows_of(before(k))
        remote(spot, spot, asem_s.at[0, k], asem_r.at[0, k], mate).wait_recv()
        hand(k).start()
    for k in range(pairs):
        spot = rows_of(before(k) + 1 - 2 * core)
        remote(spot, spot, asem_s.at[1, k], asem_r.at[1, k], mate).wait_recv()
    for k in range(1, pairs):
        send(k).wait_send()
    for k in range(pairs):
        hand(k).wait_send()


def muon(count, moments, ga, gb, squares, back, collective_id):
    width = ga.shape[1]
    tile = width // 3
    share = width // (count // 4)
    pairs = count // 2
    sizes = tuple(moment.shape[0] for moment in moments)

    def vmem(dtype, rows=width, columns=width):
        return pltpu.VMEM((rows, columns), dtype)

    scratch = (
        [vmem(F32), vmem(BF), vmem(BF), vmem(BF)]
        + [vmem(F32, tile)] * 3
        + [vmem(F32), vmem(BF), vmem(BF), vmem(BF), vmem(BF), vmem(F32), vmem(BF), vmem(BF)]
        + [vmem(F32, share)]
        + [pltpu.SemaphoreType.DMA((2,)), pltpu.SemaphoreType.DMA((2,))]
        + [pltpu.SemaphoreType.DMA((4, 2, 4) if pairs == 4 else (2, pairs))] * 2
        + line_scratch(tile, width, F32)
        + line_scratch(*back.shape, BF)
        + vector_scratch(4, squares.shape)
    )
    return pl.pallas_call(
        functools.partial(muon_kernel, count, sizes),
        out_shape=(
            jax.ShapeDtypeStruct((4 * width, width), BF),
            jax.ShapeDtypeStruct(squares.shape, F32),
            jax.ShapeDtypeStruct(back.shape, BF),
        ),
        in_specs=[IN_ANY] * 6 + [IN_VMEM] * 2,
        out_specs=(IN_VMEM,) * 3,
        scratch_shapes=scratch,
        compiler_params=params(collective_id),
        name="muon",
    )(*moments, ga, gb, squares, back)


def layer_norm(values, gain, shift):
    center = values - jnp.mean(values, axis=-1, keepdims=True)
    inverse = lax.rsqrt(jnp.mean(center * center, axis=-1, keepdims=True) + EPS_NORM)
    normed = center * inverse
    return (normed * gain + shift, normed, inverse)


def norm_back(grad_out, normed, inverse, gain):
    scaled = grad_out * gain
    first_mean = jnp.mean(scaled, axis=-1, keepdims=True)
    second_mean = jnp.mean(scaled * normed, axis=-1, keepdims=True)
    return inverse * (scaled - first_mean - normed * second_mean)


def gelu_slope(upward):
    cdf_part = 0.5 * (1.0 + jax.scipy.special.erf(upward / math.sqrt(2.0)))
    return cdf_part + upward * jnp.exp(-0.5 * upward * upward) / math.sqrt(2.0 * math.pi)


def dot(left, right):
    return jnp.dot(left, right, preferred_element_type=F32)


def tdot(left, right):
    return lax.dot_general(left, right, (((0,), (0,)), ((), ())), preferred_element_type=F32)


def vector_step(param, moment, mean_sq):
    return param - 0.1 * moment * lax.rsqrt(mean_sq + 1e-06)


def local(
    tokens, segments, cotangent,
    w_qkv, w_out, w_up, w_down, head_bias, ff_bias, row_params,
    mom_qkv, mom_out, mom_up, mom_down, mom_heads, mom_ff, mom_params,
):
    tok_count, width = tokens.shape
    columns = w_qkv.shape[2]
    ff_cols = w_up.shape[1]
    local_heads = columns // HD
    seq_count, seq_len = segments.shape
    score_scale = 1.0 / math.sqrt(HD)
    tensor_size = lax.axis_size("tensor")
    count = lax.axis_size("dp")
    wq_low = w_qkv.astype(BF)
    wo_low = w_out.astype(BF)
    wu_low = w_up.astype(BF)
    wd_low = w_down.astype(BF)

    def split_heads(rows):
        return rows.reshape(seq_count, seq_len, local_heads, HD).transpose(0, 2, 1, 3)

    def join_heads(blocks):
        return blocks.transpose(0, 2, 1, 3).reshape(tok_count, columns)

    query_h = split_heads((dot(tokens, wq_low[0]) + head_bias[0]).astype(BF))
    keys_h = split_heads(dot(tokens, wq_low[1]).astype(BF))
    values_h = split_heads((dot(tokens, wq_low[2]) + head_bias[1]).astype(BF))
    same_seg = (segments[:, :, None] == segments[:, None, :])[:, None]
    scores = (
        jnp.einsum("shqd,shkd->shqk", query_h, keys_h, preferred_element_type=F32) * score_scale
    )
    scores = jnp.where(same_seg, scores, -1e30)
    row_max = jnp.max(scores, axis=-1, keepdims=True)
    expo = jnp.exp(scores - row_max)
    probs = expo / jnp.sum(expo, axis=-1, keepdims=True)
    probs_low = probs.astype(BF)
    context = jnp.einsum("shqk,shkd->shqd", probs_low, values_h, preferred_element_type=F32)
    context_low = join_heads(context.astype(BF))
    attn = sum_tensor(dot(context_low, wo_low).astype(BF), 1).astype(F32)
    first_in = tokens.astype(F32) + attn + row_params[0]
    hidden_one, normed_one, inverse_one = layer_norm(first_in, row_params[2], row_params[3])
    hidden_low = hidden_one.astype(BF)
    upward = dot(hidden_low, wu_low) + ff_bias
    activated_low = jax.nn.gelu(upward, approximate=False).astype(BF)
    mlp = sum_tensor(dot(activated_low, wd_low).astype(BF), 2).astype(F32)
    second_in = hidden_one + mlp + row_params[1]
    output_rows, normed_two, inverse_two = layer_norm(second_in, row_params[4], row_params[5])
    grad_out = cotangent.astype(F32)
    grad_second = norm_back(grad_out, normed_two, inverse_two, row_params[4])
    grad_mlp_low = grad_second.astype(BF)
    grad_act = dot(grad_mlp_low, wd_low.T)
    grad_up_low = (grad_act * gelu_slope(upward)).astype(BF)
    grads_b = jnp.concatenate(
        [tdot(grad_up_low, hidden_low).astype(BF), tdot(activated_low, grad_mlp_low).astype(BF)]
    )
    back_hidden, sum_b = sum_both(count, dot(grad_up_low, wu_low.T).astype(BF), grads_b, 3)
    grad_hidden = back_hidden.astype(F32) + grad_second
    grad_first = norm_back(grad_hidden, normed_one, inverse_one, row_params[2])
    grad_attn_low = grad_first.astype(BF)
    grad_context = split_heads(dot(grad_attn_low, wo_low.T).astype(BF))
    grad_values = jnp.einsum("shqk,shqd->shkd", probs_low, grad_context, preferred_element_type=F32)
    grad_probs = jnp.einsum("shqd,shkd->shqk", grad_context, values_h, preferred_element_type=F32)
    grad_scores = (
        probs * (grad_probs - jnp.sum(probs * grad_probs, axis=-1, keepdims=True))
    ).astype(BF)
    grad_query = (
        jnp.einsum("shqk,shkd->shqd", grad_scores, keys_h, preferred_element_type=F32) * score_scale
    )
    grad_keys = (
        jnp.einsum("shqk,shqd->shkd", grad_scores, query_h, preferred_element_type=F32)
        * score_scale
    )
    gq_low = join_heads(grad_query.astype(BF))
    gk_low = join_heads(grad_keys.astype(BF))
    gv_low = join_heads(grad_values.astype(BF))
    grads_a = jnp.concatenate(
        [
            tdot(jnp.concatenate([gq_low, gk_low, gv_low], axis=1), tokens).astype(BF),
            tdot(context_low, grad_attn_low).astype(BF),
        ]
    )

    def over_rows(values):
        return jnp.sum(values, axis=0)

    heads_part = jnp.concatenate(
        [
            over_rows(gq_low.astype(F32)),
            over_rows(gv_low.astype(F32)),
            jnp.zeros((width - 2 * columns,), F32),
        ]
    )
    vectors = jnp.stack(
        [
            over_rows(grad_first),
            over_rows(grad_second),
            over_rows(grad_hidden * normed_one),
            over_rows(grad_hidden),
            over_rows(grad_out * normed_two),
            over_rows(grad_out),
            over_rows(grad_up_low.astype(F32)),
            heads_part,
        ]
    )
    sum_a, vector_total = sum_dp(count, grads_a, vectors, 5)
    param_sum = vector_total[0:6]
    ff_own = vector_total[6]
    heads_own = vector_total[7, : 2 * columns].reshape(2, columns)
    new_mom_heads = 0.5 * mom_heads + heads_own
    new_mom_ff = 0.5 * mom_ff + ff_own
    new_mom_params = 0.5 * mom_params + param_sum
    squares = jnp.broadcast_to(
        jnp.concatenate(
            [
                jnp.sum(new_mom_heads * new_mom_heads, axis=1),
                jnp.sum(new_mom_ff * new_mom_ff)[None],
                jnp.zeros((5,), F32),
            ]
        )[:, None],
        (8, 128),
    )
    qkv_rows = 3 * columns
    moments = (
        mom_qkv.transpose(0, 2, 1).reshape(qkv_rows, width),
        mom_out,
        mom_up.T,
        mom_down,
    )
    back_terms = dot(gq_low, wq_low[0].T)
    back_terms = back_terms + dot(gk_low, wq_low[1].T)
    back_terms = back_terms + dot(gv_low, wq_low[2].T)
    steps, totals, back = muon(count, moments, sum_a, sum_b, squares, back_terms.astype(BF), 6)
    grad_inputs = back.astype(F32) + grad_first

    def to_qkv(rows):
        return rows.reshape(3, columns, width).transpose(0, 2, 1)

    new_mom_qkv = 0.5 * mom_qkv + to_qkv(sum_a[:qkv_rows].astype(F32))
    new_mom_out = 0.5 * mom_out + sum_a[qkv_rows:].astype(F32)
    new_mom_up = 0.5 * mom_up + sum_b[:ff_cols].astype(F32).T
    new_mom_down = 0.5 * mom_down + sum_b[ff_cols:].astype(F32)
    def step_of(index, rows):
        first = (index if count == 8 else PLACE[index]) * width
        return steps[first : first + rows].astype(F32)

    wide = math.sqrt(ff_cols * tensor_size / width)
    new_qkv = w_qkv - 0.8 * math.sqrt(3.0) * to_qkv(step_of(0, qkv_rows))
    new_out = w_out - 0.8 * step_of(1, columns)
    new_up = w_up - 0.8 * wide * step_of(2, ff_cols).T
    new_down = w_down - 0.8 * wide * step_of(3, ff_cols)
    new_heads = vector_step(head_bias, new_mom_heads, totals[0:2, 0:1] / (columns * tensor_size))
    new_ff = vector_step(ff_bias, new_mom_ff, totals[2, 0] / (ff_cols * tensor_size))
    new_params = vector_step(
        row_params,
        new_mom_params,
        jnp.mean(new_mom_params * new_mom_params, axis=-1, keepdims=True),
    )
    return (
        output_rows.astype(BF),
        grad_inputs.astype(BF),
        new_mom_qkv, new_qkv, new_qkv.astype(BF),
        new_mom_out, new_out, new_out.astype(BF),
        new_mom_up, new_up, new_up.astype(BF),
        new_mom_down, new_down, new_down.astype(BF),
        new_mom_heads, new_heads,
        new_mom_ff, new_ff,
        new_mom_params, new_params,
    )


def solution(mesh):
    placed = (
        P("dp", None), P("dp", None), P("dp", None),
        P(None, None, "tensor"), P("tensor", None), P(None, "tensor"), P("tensor", None),
        P(None, "tensor"), P("tensor"), P(),
        P(None, None, "tensor"), P("tensor", None), P(None, "tensor"), P("tensor", None),
        P(None, "tensor"), P("tensor"), P(),
    )
    triple = ((P(None, None, "tensor"),) * 3, (P("tensor", None),) * 3, (P(None, "tensor"),) * 3)
    return jax.shard_map(
        local,
        mesh=mesh,
        in_specs=placed,
        out_specs=(
            (P("dp", None), P("dp", None))
            + triple[0] + triple[1] + triple[2] + triple[1]
            + (P(None, "tensor"), P(None, "tensor"), P("tensor"), P("tensor"), P(), P())
        ),
        check_vma=False,
    )
```

```python
import functools
import math

import jax
import jax.numpy as jnp
from jax import lax
from jax.experimental import pallas as pl
from jax.experimental.pallas import tpu as pltpu
from jax.sharding import PartitionSpec as P

HD = 64
EPS_NORM = 1e-05
coef_a = 3.4445
coef_b = -4.775
coef_c = 2.0315
BF = jnp.bfloat16
F32 = jnp.float32
MESH = pl.DeviceIdType.MESH
SUBS = 2
VMEM_LIMIT = 56 * 1024 * 1024
PLACE = (1, 2, 0, 3)


def remote(src, dst, send_sem, recv_sem, device):
    return pltpu.make_async_remote_copy(
        src_ref=src,
        dst_ref=dst,
        send_sem=send_sem,
        recv_sem=recv_sem,
        device_id=device,
        device_id_type=MESH,
    )


def greet(devices):
    barrier = pltpu.get_barrier_semaphore()
    for device in devices:
        pl.semaphore_signal(barrier, inc=1, device_id=device, device_id_type=MESH)
    pl.semaphore_wait(barrier, len(devices))


def z_peers(t):
    return [{"tensor": (t + k) % 4} for k in range(1, 4)]


def line_scratch(rows, width, dtype):
    part = rows // 4
    return [
        pltpu.VMEM((part, width), dtype),
        pltpu.VMEM((part, width), dtype),
        pltpu.VMEM((2 * part, width), dtype),
        pltpu.VMEM((2 * part, width), dtype),
        pltpu.SemaphoreType.DMA((8 * SUBS,)),
        pltpu.SemaphoreType.DMA((8 * SUBS,)),
    ]


def line_sum(t, x, o, scratch):
    raw, cmb, fwd, mix, ssem, rsem = scratch
    part = raw.shape[0]
    half = part // SUBS
    subs = range(SUBS)
    mate = t + 1 - 2 * (t % 2)
    outer = (t % 3) == 0
    inner = (t % 3) != 0

    def at(ref, chunk, s):
        return ref.at[pl.ds(pl.multiple_of(chunk * part + s * half, half), half)]

    def to(index, src, dst, recv, device):
        return remote(src, dst, ssem.at[index], rsem.at[recv], {"tensor": device})

    def ag_sem(chunk, s):
        return (4 + chunk) * SUBS + s

    def o_far(s):
        return to(s, at(x, 3 - t, s), at(fwd, 0, s), 2 * SUBS + s, mate)

    def o_near(s):
        return to(SUBS + s, at(x, 3 - mate, s), at(fwd, 1, s), 3 * SUBS + s, mate)

    def o_raw(s):
        return to(2 * SUBS + s, at(x, mate, s), at(raw, 0, s), s, mate)

    def o_own(s):
        return to(3 * SUBS + s, at(o, t, s), at(o, t, s), ag_sem(t, s), mate)

    def i_raw(s):
        return to(s, at(x, mate, s), at(raw, 0, s), s, mate)

    def i_far(s):
        return to(SUBS + s, at(mix, 0, s), at(cmb, 0, s), SUBS + s, 3 - mate)

    def i_near(s):
        return to(2 * SUBS + s, at(mix, 1, s), at(cmb, 0, s), SUBS + s, 3 - t)

    def i_ag(place, chunk, s, device):
        return to(place * SUBS + s, at(o, chunk, s), at(o, chunk, s), ag_sem(chunk, s), device)

    def got(dst, recv):
        remote(dst, dst, ssem.at[0], rsem.at[recv], {"tensor": mate}).wait_recv()

    def add(dst, *terms):
        total = terms[0][...].astype(F32)
        for term in terms[1:]:
            total = total + term[...].astype(F32)
        dst[...] = total.astype(dst.dtype)

    def start():
        @pl.when(outer)
        def _():
            for build in (o_far, o_near, o_raw):
                for s in subs:
                    build(s).start()

        @pl.when(inner)
        def _():
            for s in subs:
                i_raw(s).start()

    def combine():
        @pl.when(inner)
        def _():
            for slot, chunk, build in ((0, 3 - mate, i_far), (1, 3 - t, i_near)):
                for s in subs:
                    got(at(fwd, slot, s), (2 + slot) * SUBS + s)
                    add(at(mix, slot, s), at(fwd, slot, s), at(x, chunk, s))
                    build(s).start()

    def settle():
        for s in subs:
            got(at(raw, 0, s), s)
            got(at(cmb, 0, s), SUBS + s)
            add(at(o, t, s), at(x, t, s), at(raw, 0, s), at(cmb, 0, s))

            @pl.when(outer)
            def _(s=s):
                o_own(s).start()

            @pl.when(inner)
            def _(s=s):
                i_ag(3, t, s, 3 - t).start()
                i_ag(4, t, s, mate).start()

    def pass_on():
        @pl.when(inner)
        def _():
            for s in subs:
                got(at(o, mate, s), ag_sem(mate, s))
                i_ag(5, mate, s, 3 - t).start()
            for s in subs:
                got(at(o, 3 - t, s), ag_sem(3 - t, s))
                i_ag(6, 3 - t, s, mate).start()
            for s in subs:
                got(at(o, 3 - mate, s), ag_sem(3 - mate, s))
                i_ag(7, 3 - mate, s, mate).start()

    def finish():
        @pl.when(outer)
        def _():
            for chunk in (mate, 3 - mate, 3 - t):
                for s in subs:
                    got(at(o, chunk, s), ag_sem(chunk, s))
            for build in (o_far, o_near, o_raw, o_own):
                for s in subs:
                    build(s).wait_send()

        @pl.when(inner)
        def _():
            for s in subs:
                for build in (i_raw, i_far, i_near):
                    build(s).wait_send()
                i_ag(3, t, s, 3 - t).wait_send()
                i_ag(4, t, s, mate).wait_send()
                i_ag(5, mate, s, 3 - t).wait_send()
                i_ag(6, 3 - t, s, mate).wait_send()
                i_ag(7, 3 - mate, s, mate).wait_send()

    return [start, combine, settle, pass_on, finish]


def params(collective_id):
    return pltpu.CompilerParams(
        collective_id=collective_id, has_side_effects=True, vmem_limit_bytes=VMEM_LIMIT
    )


IN_VMEM = pl.BlockSpec(memory_space=pltpu.VMEM)
IN_ANY = pl.BlockSpec(memory_space=pl.ANY)


def plane_scratch(count, rows, width):
    pairs = count // 2
    side = width // 2
    block = rows // pairs
    return [
        pltpu.VMEM((rows, side), BF),
        pltpu.VMEM((rows, side), BF),
        pltpu.VMEM((pairs, block, side), BF),
        pltpu.SemaphoreType.DMA((5, pairs)),
        pltpu.SemaphoreType.DMA((4, pairs)),
    ]


def plane_sum(count, p, x, o, scratch):
    from_mate, paired, slots, ssem, rsem = scratch
    pairs = count // 2
    side = from_mate.shape[1]
    block = slots.shape[1]
    pair = p // 2
    core = p % 2
    mate = {"dp": p + 1 - 2 * core}

    def rows_of(index):
        return pl.ds(pl.multiple_of(index * block, block), block)

    def cols_of(which):
        return pl.ds(pl.multiple_of(which * side, side), side)

    def after(k):
        return (pair + k) % pairs

    def before(k):
        return (pair + pairs - k) % pairs

    def give(k):
        spot = rows_of(after(k))
        return remote(
            x.at[spot, cols_of(1 - core)], from_mate.at[spot], ssem.at[0, k % pairs], rsem.at[0, k % pairs], mate
        )

    def hand(k):
        spot = rows_of(after(k))
        return remote(
            paired.at[spot], slots.at[k], ssem.at[1, k], rsem.at[1, k], {"dp": 2 * after(k) + core}
        )

    def spread(k):
        spot = o.at[rows_of(pair), cols_of(core)]
        return remote(spot, spot, ssem.at[2, k], rsem.at[2, k], {"dp": 2 * after(k) + core})

    def share(k):
        spot = o.at[rows_of(before(k)), cols_of(core)]
        return remote(spot, spot, ssem.at[3, k], rsem.at[3, k], mate)

    def start():
        for k in range(1, pairs + 1):
            give(k).start()

    def pair_up():
        for k in range(1, pairs + 1):
            spot = rows_of(after(k))
            give(k).wait_recv()
            total = x[spot, cols_of(core)].astype(F32) + from_mate[spot].astype(F32)
            paired[spot] = total.astype(BF)
            if k < pairs:
                hand(k).start()

    def settle():
        spot = rows_of(pair)
        total = paired[spot].astype(F32)
        for k in range(1, pairs):
            hand(k).wait_recv()
            total = total + slots[k].astype(F32)
        o[spot, cols_of(core)] = total.astype(BF)
        for k in range(1, pairs):
            spread(k).start()
        share(0).start()

    def pass_on():
        for k in range(1, pairs):
            spot = o.at[rows_of(before(k)), cols_of(core)]
            remote(spot, spot, ssem.at[2, k], rsem.at[2, k], mate).wait_recv()
            share(k).start()

    def finish():
        for k in range(pairs):
            spot = o.at[rows_of(before(k)), cols_of(1 - core)]
            remote(spot, spot, ssem.at[3, k], rsem.at[3, k], mate).wait_recv()
        for k in range(1, pairs + 1):
            give(k).wait_send()
        for k in range(1, pairs):
            hand(k).wait_send()
            spread(k).wait_send()
        for k in range(pairs):
            share(k).wait_send()

    return [start, pair_up, settle, pass_on, finish]


def vector_scratch(count, shape):
    return [
        pltpu.VMEM((count,) + shape, F32),
        pltpu.SemaphoreType.DMA((count,)),
        pltpu.SemaphoreType.DMA((count,)),
    ]


def vector_sum(axis, count, p, v, o, scratch):
    slots, ssem, rsem = scratch

    def send(k):
        return remote(v, slots.at[p], ssem.at[k], rsem.at[k], {axis: (p + k) % count})

    def start():
        slots[p] = v[...]
        for k in range(1, count):
            send(k).start()

    def finish():
        for k in range(1, count):
            spot = slots.at[(p + count - k) % count]
            remote(v, spot, ssem.at[k], rsem.at[k], {axis: (p + k) % count}).wait_recv()
        total = slots[0]
        for k in range(1, count):
            total = total + slots[k]
        o[...] = total
        for k in range(1, count):
            send(k).wait_send()

    return [start, finish]


ROW_STEP = 32


def tdot(left, right):
    return lax.dot_general(left, right, (((0,), (0,)), ((), ())), preferred_element_type=F32)


def dot(left, right):
    return jnp.dot(left, right, preferred_element_type=F32)


def dot_t(left, right):
    return lax.dot_general(left, right, (((1,), (1,)), ((), ())), preferred_element_type=F32)


def layer_kernel(
    count,
    x, cot, seg, rp, hb, fb, wq_hbm, wo_hbm, wu_hbm, wd_hbm,
    y, dz1, bt, ga, gb, vec,
    wq_f, wo_f, wu_f, wd_f, wq, wo, wu, wd,
    q_s, k_s, v_s, ctx_s, p_s, n1_s, inv1_s, h1l_s, u_s, act_s, slope_s, dz2_s, dm_s, du_s, da_s,
    dq_s, dk_s, dv_s, part_s, red_s, gap, gbp, vecp, wsem, *scratch,
):
    p = lax.axis_index("dp")
    t = lax.axis_index("tensor")
    tokens, width = x.shape
    half = tokens // 2
    columns = q_s.shape[1]
    heads = columns // HD
    scale = 1.0 / math.sqrt(HD)
    greet(z_peers(t) + [{"dp": (p + k) % count} for k in range(1, count)])
    loads = [
        pltpu.make_async_copy(source, target, wsem.at[i])
        for i, (source, target) in enumerate(
            ((wq_hbm, wq_f), (wo_hbm, wo_f), (wu_hbm, wu_f), (wd_hbm, wd_f))
        )
    ]
    for load in loads:
        load.start()
    sums = []
    for h in range(2):
        place = pl.ds(h * half, half)
        sums.append(
            line_sum(t, part_s.at[place], red_s.at[place], scratch[6 * h : 6 * h + 6])
        )
    plane_b = plane_sum(count, p, gbp, gb, scratch[12:17])
    plane_a = plane_sum(count, p, gap, ga, scratch[17:22])
    vector = vector_sum("dp", count, p, vecp, vec, scratch[22:25])
    vecp[...] = jnp.zeros_like(vecp)
    lane = lax.broadcasted_iota(jnp.int32, (1, columns), 1)

    def in_head(index):
        return (lane // HD) == index

    def rows_of(h):
        return pl.ds(h * half, half)

    def over_rows(h, body, init=0):
        def step(i, carry):
            first = h * half + i * ROW_STEP
            return body(pl.ds(pl.multiple_of(first, ROW_STEP), ROW_STEP), carry)

        return lax.fori_loop(0, half // ROW_STEP, step, init)

    def fold(values):
        return values.reshape(ROW_STEP // 8, 8, values.shape[1]).sum(axis=0)

    def add_vec(row, folded):
        vecp[row : row + 1, 0 : folded.shape[1]] += jnp.sum(folded, axis=0, keepdims=True)

    def narrow(index, source, target):
        loads[index].wait()
        if len(source.shape) == 3:
            for i in range(source.shape[0]):
                target[i] = source[i].astype(BF)
        else:
            target[...] = source[...].astype(BF)

    def attention(h):
        r = rows_of(h)
        xb = x[r]
        q = (dot(xb, wq[0]) + hb[0:1]).astype(BF)
        k = dot(xb, wq[1]).astype(BF)
        v = (dot(xb, wq[2]) + hb[1:2]).astype(BF)
        q_s[r], k_s[r], v_s[r] = q, k, v
        down = jnp.broadcast_to(seg[h : h + 1].astype(F32), (half, half))
        same = down == down.T
        context = jnp.zeros((half, columns), F32)
        for index in range(heads):
            mine = jnp.where(in_head(index), q, jnp.zeros_like(q))
            scores = jnp.where(same, dot_t(mine, k) * scale, -1e30)
            expo = jnp.exp(scores - jnp.max(scores, axis=-1, keepdims=True))
            probs = expo / jnp.sum(expo, axis=-1, keepdims=True)
            p_s[h * heads + index] = probs
            context = jnp.where(in_head(index), dot(probs.astype(BF), v), context)
        low = context.astype(BF)
        ctx_s[r] = low
        part_s[r] = dot(low, wo[...]).astype(BF)

    def up(h):
        def norm(r, carry):
            z = x[r].astype(F32) + red_s[r].astype(F32) + rp[0:1]
            center = z - jnp.mean(z, axis=-1, keepdims=True)
            inverse = lax.rsqrt(jnp.mean(center * center, axis=-1, keepdims=True) + EPS_NORM)
            normed = center * inverse
            n1_s[r] = normed
            inv1_s[r] = jnp.broadcast_to(inverse, (ROW_STEP, 128))
            h1l_s[r] = (normed * rp[2:3] + rp[3:4]).astype(BF)
            return carry

        over_rows(h, norm)
        u_s[rows_of(h)] = dot(h1l_s[rows_of(h)], wu[...])

        def gelu(r, carry):
            u = u_s[r] + fb[0:1]
            cdf = 0.5 * (1.0 + lax.erf(u * (1.0 / math.sqrt(2.0))))
            act_s[r] = (u * cdf).astype(BF)
            slope_s[r] = cdf + u * jnp.exp(-0.5 * u * u) * (1.0 / math.sqrt(2.0 * math.pi))
            return carry

        over_rows(h, gelu)

    def down(h):
        r = rows_of(h)
        part_s[r] = dot(act_s[r], wd[...]).astype(BF)

    def out_back(h):
        def norm(r, carry):
            s_dz2, s_dyn, s_dy = carry
            h1 = n1_s[r] * rp[2:3] + rp[3:4]
            z = h1 + red_s[r].astype(F32) + rp[1:2]
            center = z - jnp.mean(z, axis=-1, keepdims=True)
            inverse = lax.rsqrt(jnp.mean(center * center, axis=-1, keepdims=True) + EPS_NORM)
            normed = center * inverse
            y[r] = (normed * rp[4:5] + rp[5:6]).astype(BF)
            dy = cot[r].astype(F32)
            scaled = dy * rp[4:5]
            first = jnp.mean(scaled, axis=-1, keepdims=True)
            second = jnp.mean(scaled * normed, axis=-1, keepdims=True)
            dz2 = inverse * (scaled - first - normed * second)
            dz2_s[r] = dz2
            dm_s[r] = dz2.astype(BF)
            return s_dz2 + fold(dz2), s_dyn + fold(dy * normed), s_dy + fold(dy)

        zero = jnp.zeros((8, width), F32)
        for row, total in zip((1, 4, 5), over_rows(h, norm, (zero, zero, zero))):
            add_vec(row, total)
        u_s[rows_of(h)] = dot_t(dm_s[rows_of(h)], wd[...])

        def slope(r, carry):
            du = (u_s[r] * slope_s[r]).astype(BF)
            du_s[r] = du
            return carry + fold(du.astype(F32))

        add_vec(6, over_rows(h, slope, zero))

    def up_back(h):
        r = rows_of(h)
        part_s[r] = dot_t(du_s[r], wu[...]).astype(BF)

    def grads_b():
        gbp[0:width] = tdot(du_s[...], h1l_s[...]).astype(BF)
        gbp[width : 2 * width] = tdot(act_s[...], dm_s[...]).astype(BF)

    def attention_back(h):
        def norm(r, carry):
            s_dz1, s_dhn, s_dh = carry
            dh1 = red_s[r].astype(F32) + dz2_s[r]
            normed = n1_s[r]
            scaled = dh1 * rp[2:3]
            first = jnp.mean(scaled, axis=-1, keepdims=True)
            second = jnp.mean(scaled * normed, axis=-1, keepdims=True)
            grad = inv1_s[r][:, 0:1] * (scaled - first - normed * second)
            dz1[r] = grad
            da_s[r] = grad.astype(BF)
            return s_dz1 + fold(grad), s_dhn + fold(dh1 * normed), s_dh + fold(dh1)

        zero = jnp.zeros((8, width), F32)
        for row, total in zip((0, 2, 3), over_rows(h, norm, (zero, zero, zero))):
            add_vec(row, total)
        r = rows_of(h)
        dc = dot_t(da_s[r], wo[...]).astype(BF)
        q, k, v = q_s[r], k_s[r], v_s[r]
        dq = dk = dv = jnp.zeros((half, columns), F32)
        for index in range(heads):
            probs = p_s[h * heads + index]
            mine = jnp.where(in_head(index), dc, jnp.zeros_like(dc))
            dp = dot_t(mine, v)
            ds = (probs * (dp - jnp.sum(probs * dp, axis=-1, keepdims=True))).astype(BF)
            dv = jnp.where(in_head(index), tdot(probs.astype(BF), dc), dv)
            dq = jnp.where(in_head(index), dot(ds, k), dq)
            dk = jnp.where(in_head(index), tdot(ds, q), dk)
        dq = (dq * scale).astype(BF)
        dk = (dk * scale).astype(BF)
        dv = dv.astype(BF)
        dq_s[r], dk_s[r], dv_s[r] = dq, dk, dv
        add_vec(7, jnp.sum(dq.astype(F32), axis=0, keepdims=True))
        add_vec(8, jnp.sum(dv.astype(F32), axis=0, keepdims=True))

    def grads_a():
        for i, source in enumerate((dq_s, dk_s, dv_s)):
            gap[i * columns : (i + 1) * columns] = tdot(source[...], x[...]).astype(BF)
        gap[3 * columns : 4 * columns] = tdot(ctx_s[...], da_s[...]).astype(BF)

    def back_terms(h):
        r = rows_of(h)
        total = dot_t(dq_s[r], wq[0]) + dot_t(dk_s[r], wq[1]) + dot_t(dv_s[r], wq[2])
        bt[r] = total.astype(BF)

    (a_start, a_mix, a_settle, a_pass, a_end), (b_start, b_mix, b_settle, b_pass, b_end) = sums
    narrow(0, wq_f, wq)
    narrow(1, wo_f, wo)
    attention(0)
    a_start()
    attention(1)
    a_mix()
    b_start()
    narrow(2, wu_f, wu)
    a_settle()
    b_mix()
    a_pass()
    b_settle()
    narrow(3, wd_f, wd)
    a_end()
    up(0)
    b_pass()
    down(0)
    a_start()
    b_end()
    up(1)
    a_mix()
    down(1)
    b_start()
    a_settle()
    b_mix()
    a_pass()
    b_settle()
    a_end()
    out_back(0)
    b_pass()
    up_back(0)
    a_start()
    b_end()
    out_back(1)
    a_mix()
    up_back(1)
    b_start()
    grads_b()
    plane_b[0]()
    a_settle()
    b_mix()
    plane_b[1]()
    a_pass()
    b_settle()
    a_end()
    attention_back(0)
    b_pass()
    b_end()
    attention_back(1)
    grads_a()
    plane_a[0]()
    vector[0]()
    plane_b[2]()
    plane_a[1]()
    back_terms(0)
    back_terms(1)
    plane_b[3]()
    plane_a[2]()
    plane_b[4]()
    plane_a[3]()
    plane_a[4]()
    vector[1]()


def layer(count, tokens, cotangent, segments, row_params, head_bias, ff_bias, weights, collective_id):
    rows, width = tokens.shape
    w_qkv, w_out, w_up, w_down = weights
    columns = w_qkv.shape[2]
    heads = columns // HD
    half = rows // 2

    def low(*shape):
        return pltpu.VMEM(shape, BF)

    def full(*shape):
        return pltpu.VMEM(shape, F32)

    def out(shape, dtype):
        return jax.ShapeDtypeStruct(shape, dtype)

    scratch = (
        [full(*weight.shape) for weight in weights]
        + [low(*weight.shape) for weight in weights]
        + [low(rows, columns)] * 4
        + [full(2 * heads, half, half), full(rows, width), full(rows, 128), low(rows, width)]
        + [full(rows, width), low(rows, width), full(rows, width), full(rows, width)]
        + [low(rows, width)] * 3
        + [low(rows, columns)] * 3
        + [low(rows, width)] * 2
        + [low(4 * columns, width), low(2 * width, width), full(16, width)]
        + [pltpu.SemaphoreType.DMA((4,))]
        + line_scratch(half, width, BF) * 2
        + plane_scratch(count, 2 * width, width)
        + plane_scratch(count, 4 * columns, width)
        + vector_scratch(count, (16, width))
    )
    return pl.pallas_call(
        functools.partial(layer_kernel, count),
        out_shape=(
            out((rows, width), BF),
            out((rows, width), F32),
            out((rows, width), BF),
            out((4 * columns, width), BF),
            out((2 * width, width), BF),
            out((16, width), F32),
        ),
        in_specs=[IN_VMEM] * 6 + [IN_ANY] * 4,
        out_specs=(IN_VMEM,) * 6,
        scratch_shapes=scratch,
        compiler_params=params(collective_id),
        name="layer",
    )(tokens, cotangent, segments, row_params, head_bias, ff_bias, *weights)


def cut(values):
    high = values.astype(BF)
    return high, (values - high.astype(F32)).astype(BF)


def dot3(lh, ll, rh, rl, dims=(((1,), (0,)), ((), ()))):
    def dot(left, right):
        return lax.dot_general(left, right, dims, preferred_element_type=F32)

    return dot(lh, rh) + (dot(lh, rl) + dot(ll, rh))


def muon_kernel(
    count, sizes,
    mq, mo, mu, md, ga, gb, vs, bx,
    xo, vt, bo,
    zf, gf, zh, zl, gx, go, gp, af, ah, al, dh, dl, sf, sh, sl, xf, lsem, psem, asem_s, asem_r, *scratch,
):
    p = lax.axis_index("dp")
    t = lax.axis_index("tensor")
    width = zf.shape[1]
    group = count // 4
    which = p // group
    core = p % 2
    pairs = count // 2
    pair = p // 2
    mate = {"dp": p + 1 - 2 * core}
    share = xf.shape[0]
    tile = width // 3
    greet(z_peers(t) + [{"dp": (p + k) % count} for k in range(1, count)])
    vector = vector_sum("tensor", 4, t, vs, vt, scratch[12:])
    back = line_sum(t, bx, bo, scratch[6:12])
    vector[0]()
    qkv_rows, out_rows, _, _ = sizes
    gsrc = (
        (ga, 0, qkv_rows), (ga, qkv_rows, out_rows), (gb, 0, width), (gb, width, width)
    )
    for index, moment in enumerate((mq, mo, mu, md)):
        grads, first, rows = gsrc[index]

        @pl.when(which == PLACE[index])
        def _(moment=moment, grads=grads, first=first, rows=rows):
            one = pltpu.make_async_copy(moment, zf.at[pl.ds(0, rows)], lsem.at[0])
            two = pltpu.make_async_copy(
                grads.at[pl.ds(first, rows)], gf.at[pl.ds(0, rows)], lsem.at[1]
            )
            one.start()
            two.start()
            if rows < width:
                zf[pl.ds(rows, width - rows)] = jnp.zeros((width - rows, width), F32)
                gf[pl.ds(rows, width - rows)] = jnp.zeros((width - rows, width), BF)
            one.wait()
            two.wait()

    for i in range(3):
        spot = pl.ds(i * tile, tile)
        z = 0.5 * zf[spot] + gf[spot].astype(F32)
        zf[spot] = z
        zh[spot], zl[spot] = cut(z)

    def cols(index):
        return pl.ds(pl.multiple_of(index * tile, tile), tile)

    over_rows = (((0,), (0,)), ((), ()))
    for j, (row, col) in enumerate(((core, core), (core, core + 1), (2 * core, 2))):
        gx[:, pl.ds(j * tile, tile)] = dot3(
            zh[:, cols(row)], zl[:, cols(row)], zh[:, cols(col)], zl[:, cols(col)], over_rows
        )
    for step in line_sum(t, gx, go, scratch[:6]):
        step()
    swap = remote(go, gp, psem.at[0], psem.at[1], mate)
    swap.start()
    back[0]()
    swap.wait()
    diagonal = lax.broadcasted_iota(jnp.int32, (tile, tile), 0) == lax.broadcasted_iota(
        jnp.int32, (tile, tile), 1
    )

    def upper(first, second):
        trace = jnp.float32(0.0)
        for block in (first[:, 0:tile], second[:, 0:tile], second[:, 2 * tile :]):
            trace = trace + jnp.sum(jnp.where(diagonal, block, 0.0))
        inverse = 1.0 / (jnp.sqrt(jnp.full((1, 1), trace, F32)) + 1e-07)
        scale = inverse * inverse
        blocks = (
            (0, 0, first, 0), (0, 1, first, 1), (0, 2, first, 2),
            (1, 1, second, 0), (1, 2, second, 1), (2, 2, second, 2),
        )
        for row, col, source, j in blocks:
            block = source[:, j * tile : (j + 1) * tile] * scale
            for r, c, value in ((row, col, block),) + (((col, row, block.T),) if row != col else ()):
                spot = (pl.ds(r * tile, tile), pl.ds(c * tile, tile))
                af[spot] = value
                ah[spot], al[spot] = cut(value)
        if group == 2:
            for index, rows in enumerate(sizes):

                @pl.when(which == PLACE[index])
                def _(half=rows // 2):
                    xf[0:half] = zf[pl.ds(pl.multiple_of(core * half, half), half)] * inverse
                    if half < share:
                        xf[half:share] = jnp.zeros((share - half, width), F32)

        else:
            rank = p % group
            xf[...] = zf[pl.ds(pl.multiple_of(rank * share, share), share)] * inverse

    @pl.when(core == 0)
    def _():
        upper(go, gp)

    @pl.when(core == 1)
    def _():
        upper(gp, go)

    vector[1]()

    def product(left, right, base, base_scale, scale, targets):
        (lh, ll), (rh, rl) = left, right
        for i in range(3):
            rows = pl.ds(i * tile, tile)
            for j in range(i, 3):
                columns = pl.ds(j * tile, tile)
                value = base_scale * base[rows, columns] + scale * dot3(
                    lh[rows], ll[rows], rh[:, columns], rl[:, columns]
                )
                for target, part in zip(targets, (*cut(value), value)):
                    target[rows, columns] = part
                    if i != j:
                        target[columns, rows] = part.T

    def make_d():
        product((ah, al), (ah, al), af, coef_b, coef_c, (dh, dl))

    def move_x():
        xh, xl = cut(xf[...])
        xf[...] = coef_a * xf[...] + dot3(xh, xl, dh[...], dl[...])

    def sweep(k, carry):
        make_d()
        move_x()
        product((ah, al), (dh, dl), af, coef_a, 1.0, (sh, sl, sf))
        product((sh, sl), (dh, dl), sf, coef_a, 1.0, (ah, al, af))
        for i in range(1, 4):
            pl.when(k == i - 1)(back[i])
        return carry

    lax.fori_loop(0, 4, sweep, 0)
    make_d()
    move_x()
    back[4]()

    if pairs == 4:
        gather_square(pair, core, mate, sizes, xf, xo, asem_s, asem_r)
    else:
        gather_any(p, core, pairs, mate, xf, xo, asem_s, asem_r)


def gather_square(pair, core, mate, sizes, xf, xo, ssem, rsem):
    width = xf.shape[1]

    def piece(index, side, part):
        half = sizes[index] // 4
        first = index * width + side * 2 * half + part * half
        return xo.at[pl.ds(pl.multiple_of(first, half), half)]

    def copy(index, part, route, device):
        spot = piece(index, core, part)
        return remote(spot, spot, ssem.at[index, part, route], rsem.at[index, part, route], device)

    def other(away):
        return {"dp": 2 * (pair + away * (1 - 2 * ((pair // away) % 2))) + core}

    def place_is(index, away):
        return pair == (PLACE[index] ^ away)

    def wait_in(index, part, route, side):
        spot = piece(index, side, part)
        remote(spot, spot, ssem.at[index, part, route], rsem.at[index, part, route], mate).wait_recv()

    for index, rows in enumerate(sizes):
        half = rows // 4

        @pl.when(place_is(index, 0))
        def _(index=index, half=half):
            for part in range(2):
                piece(index, core, part)[...] = xf[pl.ds(part * half, half)].astype(BF)
            for part in range(2):
                copy(index, part, 0, other(1)).start()
                copy(index, 1 - part, 1, other(2)).start()
            for part in range(2):
                copy(index, part, 3, mate).start()

    for index in range(4):
        for away, route, onward in ((1, 0, 2), (2, 1, 1)):

            @pl.when(place_is(index, away))
            def _(index=index, away=away, route=route, onward=onward):
                first = away - 1
                wait_in(index, first, route, core)
                copy(index, first, 2, other(onward)).start()
                copy(index, first, 3, mate).start()

    for index in range(4):
        for away, route, onward in ((1, 0, 2), (2, 1, 1)):

            @pl.when(place_is(index, away))
            def _(index=index, away=away, route=route):
                second = 2 - away
                wait_in(index, second, route, core)
                copy(index, second, 3, mate).start()

        @pl.when(place_is(index, 3))
        def _(index=index):
            for part in range(2):
                wait_in(index, part, 2, core)
                copy(index, part, 3, mate).start()

    for index in range(4):
        for part in range(2):
            wait_in(index, part, 3, 1 - core)
            copy(index, part, 3, mate).wait_send()

        @pl.when(place_is(index, 0))
        def _(index=index):
            for part in range(2):
                copy(index, part, 0, other(1)).wait_send()
                copy(index, part, 1, other(2)).wait_send()

        for away, onward in ((1, 2), (2, 1)):

            @pl.when(place_is(index, away))
            def _(index=index, away=away, onward=onward):
                copy(index, away - 1, 2, other(onward)).wait_send()


def gather_any(p, core, pairs, mate, xf, xo, asem_s, asem_r):
    pair = p // 2
    share = xf.shape[0]

    def rows_of(device):
        return xo.at[pl.ds(pl.multiple_of(device * share, share), share)]

    def after(k):
        return 2 * ((pair + k) % pairs) + core

    def before(k):
        return 2 * ((pair + pairs - k) % pairs) + core

    def send(k):
        return remote(rows_of(p), rows_of(p), asem_s.at[0, k], asem_r.at[0, k], {"dp": after(k)})

    def hand(k):
        spot = rows_of(before(k))
        return remote(spot, spot, asem_s.at[1, k], asem_r.at[1, k], mate)

    xo[pl.ds(pl.multiple_of(p * share, share), share)] = xf[...].astype(BF)
    for k in range(1, pairs):
        send(k).start()
    hand(0).start()
    for k in range(1, pairs):
        spot = rows_of(before(k))
        remote(spot, spot, asem_s.at[0, k], asem_r.at[0, k], mate).wait_recv()
        hand(k).start()
    for k in range(pairs):
        spot = rows_of(before(k) + 1 - 2 * core)
        remote(spot, spot, asem_s.at[1, k], asem_r.at[1, k], mate).wait_recv()
    for k in range(1, pairs):
        send(k).wait_send()
    for k in range(pairs):
        hand(k).wait_send()


def muon(count, moments, ga, gb, squares, back, collective_id):
    width = ga.shape[1]
    tile = width // 3
    share = width // (count // 4)
    pairs = count // 2
    sizes = tuple(moment.shape[0] for moment in moments)

    def vmem(dtype, rows=width, columns=width):
        return pltpu.VMEM((rows, columns), dtype)

    scratch = (
        [vmem(F32), vmem(BF), vmem(BF), vmem(BF)]
        + [vmem(F32, tile)] * 3
        + [vmem(F32), vmem(BF), vmem(BF), vmem(BF), vmem(BF), vmem(F32), vmem(BF), vmem(BF)]
        + [vmem(F32, share)]
        + [pltpu.SemaphoreType.DMA((2,)), pltpu.SemaphoreType.DMA((2,))]
        + [pltpu.SemaphoreType.DMA((4, 2, 4) if pairs == 4 else (2, pairs))] * 2
        + line_scratch(tile, width, F32)
        + line_scratch(*back.shape, BF)
        + vector_scratch(4, squares.shape)
    )
    return pl.pallas_call(
        functools.partial(muon_kernel, count, sizes),
        out_shape=(
            jax.ShapeDtypeStruct((4 * width, width), BF),
            jax.ShapeDtypeStruct(squares.shape, F32),
            jax.ShapeDtypeStruct(back.shape, BF),
        ),
        in_specs=[IN_ANY] * 6 + [IN_VMEM] * 2,
        out_specs=(IN_VMEM,) * 3,
        scratch_shapes=scratch,
        compiler_params=params(collective_id),
        name="muon",
    )(*moments, ga, gb, squares, back)


def vector_step(param, moment, mean_sq):
    return param - 0.1 * moment * lax.rsqrt(mean_sq + 1e-06)


def local(
    tokens, segments, cotangent,
    w_qkv, w_out, w_up, w_down, head_bias, ff_bias, row_params,
    mom_qkv, mom_out, mom_up, mom_down, mom_heads, mom_ff, mom_params,
):
    width = tokens.shape[1]
    columns = w_qkv.shape[2]
    ff_cols = w_up.shape[1]
    tensor_size = lax.axis_size("tensor")
    count = lax.axis_size("dp")
    output_rows, grad_first, back_terms, sum_a, sum_b, vector_total = layer(
        count, tokens, cotangent, segments, row_params, head_bias, ff_bias.reshape(1, ff_cols),
        (w_qkv, w_out, w_up, w_down), 1,
    )
    param_sum = vector_total[0:6]
    ff_own = vector_total[6]
    heads_own = vector_total[7:9, :columns]
    new_mom_heads = 0.5 * mom_heads + heads_own
    new_mom_ff = 0.5 * mom_ff + ff_own
    new_mom_params = 0.5 * mom_params + param_sum
    squares = jnp.broadcast_to(
        jnp.concatenate(
            [
                jnp.sum(new_mom_heads * new_mom_heads, axis=1),
                jnp.sum(new_mom_ff * new_mom_ff)[None],
                jnp.zeros((5,), F32),
            ]
        )[:, None],
        (8, 128),
    )
    qkv_rows = 3 * columns
    moments = (
        mom_qkv.transpose(0, 2, 1).reshape(qkv_rows, width),
        mom_out,
        mom_up.T,
        mom_down,
    )
    steps, totals, back = muon(count, moments, sum_a, sum_b, squares, back_terms, 2)
    grad_inputs = back.astype(F32) + grad_first

    def to_qkv(rows):
        return rows.reshape(3, columns, width).transpose(0, 2, 1)

    new_mom_qkv = 0.5 * mom_qkv + to_qkv(sum_a[:qkv_rows].astype(F32))
    new_mom_out = 0.5 * mom_out + sum_a[qkv_rows:].astype(F32)
    new_mom_up = 0.5 * mom_up + sum_b[:ff_cols].astype(F32).T
    new_mom_down = 0.5 * mom_down + sum_b[ff_cols:].astype(F32)
    def step_of(index, rows):
        first = (index if count == 8 else PLACE[index]) * width
        return steps[first : first + rows].astype(F32)

    wide = math.sqrt(ff_cols * tensor_size / width)
    new_qkv = w_qkv - 0.8 * math.sqrt(3.0) * to_qkv(step_of(0, qkv_rows))
    new_out = w_out - 0.8 * step_of(1, columns)
    new_up = w_up - 0.8 * wide * step_of(2, ff_cols).T
    new_down = w_down - 0.8 * wide * step_of(3, ff_cols)
    new_heads = vector_step(head_bias, new_mom_heads, totals[0:2, 0:1] / (columns * tensor_size))
    new_ff = vector_step(ff_bias, new_mom_ff, totals[2, 0] / (ff_cols * tensor_size))
    new_params = vector_step(
        row_params,
        new_mom_params,
        jnp.mean(new_mom_params * new_mom_params, axis=-1, keepdims=True),
    )
    return (
        output_rows,
        grad_inputs.astype(BF),
        new_mom_qkv, new_qkv, new_qkv.astype(BF),
        new_mom_out, new_out, new_out.astype(BF),
        new_mom_up, new_up, new_up.astype(BF),
        new_mom_down, new_down, new_down.astype(BF),
        new_mom_heads, new_heads,
        new_mom_ff, new_ff,
        new_mom_params, new_params,
    )


def solution(mesh):
    placed = (
        P("dp", None), P("dp", None), P("dp", None),
        P(None, None, "tensor"), P("tensor", None), P(None, "tensor"), P("tensor", None),
        P(None, "tensor"), P("tensor"), P(),
        P(None, None, "tensor"), P("tensor", None), P(None, "tensor"), P("tensor", None),
        P(None, "tensor"), P("tensor"), P(),
    )
    triple = ((P(None, None, "tensor"),) * 3, (P("tensor", None),) * 3, (P(None, "tensor"),) * 3)
    return jax.shard_map(
        local,
        mesh=mesh,
        in_specs=placed,
        out_specs=(
            (P("dp", None), P("dp", None))
            + triple[0] + triple[1] + triple[2] + triple[1]
            + (P(None, "tensor"), P(None, "tensor"), P("tensor"), P("tensor"), P(), P())
        ),
        check_vma=False,
    )
```

```python
import functools
import math

import jax
import jax.numpy as jnp
from jax import lax
from jax.experimental import pallas as pl
from jax.experimental.pallas import tpu as pltpu
from jax.sharding import PartitionSpec as P

HD = 64
EPS_NORM = 1e-05
coef_a = 3.4445
coef_b = -4.775
coef_c = 2.0315
BF = jnp.bfloat16
F32 = jnp.float32
MESH = pl.DeviceIdType.MESH
SUBS = 2
PLACE = (1, 2, 0, 3)


def remote(src, dst, send_sem, recv_sem, device):
    return pltpu.make_async_remote_copy(
        src_ref=src,
        dst_ref=dst,
        send_sem=send_sem,
        recv_sem=recv_sem,
        device_id=device,
        device_id_type=MESH,
    )


def greet(devices):
    barrier = pltpu.get_barrier_semaphore()
    for device in devices:
        pl.semaphore_signal(barrier, inc=1, device_id=device, device_id_type=MESH)
    pl.semaphore_wait(barrier, len(devices))


def z_peers(t):
    return [{"tensor": (t + k) % 4} for k in range(1, 4)]


def line_scratch(rows, width, dtype):
    part = rows // 4
    return [
        pltpu.VMEM((part, width), dtype),
        pltpu.VMEM((part, width), dtype),
        pltpu.VMEM((2 * part, width), dtype),
        pltpu.VMEM((2 * part, width), dtype),
        pltpu.SemaphoreType.DMA((8 * SUBS,)),
        pltpu.SemaphoreType.DMA((8 * SUBS,)),
    ]


def line_sum(t, x, o, scratch):
    raw, cmb, fwd, mix, ssem, rsem = scratch
    part = raw.shape[0]
    half = part // SUBS
    subs = range(SUBS)
    mate = t + 1 - 2 * (t % 2)
    outer = (t % 3) == 0
    inner = (t % 3) != 0

    def at(ref, chunk, s):
        return ref.at[pl.ds(pl.multiple_of(chunk * part + s * half, half), half)]

    def to(index, src, dst, recv, device):
        return remote(src, dst, ssem.at[index], rsem.at[recv], {"tensor": device})

    def ag_sem(chunk, s):
        return (4 + chunk) * SUBS + s

    def o_far(s):
        return to(s, at(x, 3 - t, s), at(fwd, 0, s), 2 * SUBS + s, mate)

    def o_near(s):
        return to(SUBS + s, at(x, 3 - mate, s), at(fwd, 1, s), 3 * SUBS + s, mate)

    def o_raw(s):
        return to(2 * SUBS + s, at(x, mate, s), at(raw, 0, s), s, mate)

    def o_own(s):
        return to(3 * SUBS + s, at(o, t, s), at(o, t, s), ag_sem(t, s), mate)

    def i_raw(s):
        return to(s, at(x, mate, s), at(raw, 0, s), s, mate)

    def i_far(s):
        return to(SUBS + s, at(mix, 0, s), at(cmb, 0, s), SUBS + s, 3 - mate)

    def i_near(s):
        return to(2 * SUBS + s, at(mix, 1, s), at(cmb, 0, s), SUBS + s, 3 - t)

    def i_ag(place, chunk, s, device):
        return to(place * SUBS + s, at(o, chunk, s), at(o, chunk, s), ag_sem(chunk, s), device)

    def got(dst, recv):
        remote(dst, dst, ssem.at[0], rsem.at[recv], {"tensor": mate}).wait_recv()

    def add(dst, *terms):
        total = terms[0][...].astype(F32)
        for term in terms[1:]:
            total = total + term[...].astype(F32)
        dst[...] = total.astype(dst.dtype)

    def start():
        @pl.when(outer)
        def _():
            for build in (o_far, o_near, o_raw):
                for s in subs:
                    build(s).start()

        @pl.when(inner)
        def _():
            for s in subs:
                i_raw(s).start()

    def combine():
        @pl.when(inner)
        def _():
            for slot, chunk, build in ((0, 3 - mate, i_far), (1, 3 - t, i_near)):
                for s in subs:
                    got(at(fwd, slot, s), (2 + slot) * SUBS + s)
                    add(at(mix, slot, s), at(fwd, slot, s), at(x, chunk, s))
                    build(s).start()

    def settle():
        for s in subs:
            got(at(raw, 0, s), s)
            got(at(cmb, 0, s), SUBS + s)
            add(at(o, t, s), at(x, t, s), at(raw, 0, s), at(cmb, 0, s))

            @pl.when(outer)
            def _(s=s):
                o_own(s).start()

            @pl.when(inner)
            def _(s=s):
                i_ag(3, t, s, 3 - t).start()
                i_ag(4, t, s, mate).start()

    def pass_on():
        @pl.when(inner)
        def _():
            for s in subs:
                got(at(o, mate, s), ag_sem(mate, s))
                i_ag(5, mate, s, 3 - t).start()
            for s in subs:
                got(at(o, 3 - t, s), ag_sem(3 - t, s))
                i_ag(6, 3 - t, s, mate).start()
            for s in subs:
                got(at(o, 3 - mate, s), ag_sem(3 - mate, s))
                i_ag(7, 3 - mate, s, mate).start()

    def finish():
        @pl.when(outer)
        def _():
            for chunk in (mate, 3 - mate, 3 - t):
                for s in subs:
                    got(at(o, chunk, s), ag_sem(chunk, s))
            for build in (o_far, o_near, o_raw, o_own):
                for s in subs:
                    build(s).wait_send()

        @pl.when(inner)
        def _():
            for s in subs:
                for build in (i_raw, i_far, i_near):
                    build(s).wait_send()
                i_ag(3, t, s, 3 - t).wait_send()
                i_ag(4, t, s, mate).wait_send()
                i_ag(5, mate, s, 3 - t).wait_send()
                i_ag(6, 3 - t, s, mate).wait_send()
                i_ag(7, 3 - mate, s, mate).wait_send()

    return [start, combine, settle, pass_on, finish]


def params(collective_id, mebibytes):
    return pltpu.CompilerParams(
        collective_id=collective_id,
        has_side_effects=True,
        vmem_limit_bytes=mebibytes * 1024 * 1024,
    )


IN_VMEM = pl.BlockSpec(memory_space=pltpu.VMEM)
IN_ANY = pl.BlockSpec(memory_space=pl.ANY)


def plane_scratch(count, rows, width):
    pairs = count // 2
    side = width // 2
    block = rows // pairs
    return [
        pltpu.VMEM((rows, side), BF),
        pltpu.VMEM((rows, side), BF),
        pltpu.VMEM((pairs, block, side), BF),
        pltpu.SemaphoreType.DMA((5, pairs)),
        pltpu.SemaphoreType.DMA((4, pairs)),
    ]


def plane_sum(count, p, x, o, scratch):
    from_mate, paired, slots, ssem, rsem = scratch
    pairs = count // 2
    side = from_mate.shape[1]
    block = slots.shape[1]
    pair = p // 2
    core = p % 2
    mate = {"dp": p + 1 - 2 * core}

    def rows_of(index):
        return pl.ds(pl.multiple_of(index * block, block), block)

    def cols_of(which):
        return pl.ds(pl.multiple_of(which * side, side), side)

    def after(k):
        return (pair + k) % pairs

    def before(k):
        return (pair + pairs - k) % pairs

    def give(k):
        spot = rows_of(after(k))
        return remote(
            x.at[spot, cols_of(1 - core)], from_mate.at[spot], ssem.at[0, k % pairs], rsem.at[0, k % pairs], mate
        )

    def hand(k):
        spot = rows_of(after(k))
        return remote(
            paired.at[spot], slots.at[k], ssem.at[1, k], rsem.at[1, k], {"dp": 2 * after(k) + core}
        )

    def spread(k):
        spot = o.at[rows_of(pair), cols_of(core)]
        return remote(spot, spot, ssem.at[2, k], rsem.at[2, k], {"dp": 2 * after(k) + core})

    def share(k):
        spot = o.at[rows_of(before(k)), cols_of(core)]
        return remote(spot, spot, ssem.at[3, k], rsem.at[3, k], mate)

    def start():
        for k in range(1, pairs + 1):
            give(k).start()

    def pair_up():
        for k in range(1, pairs + 1):
            spot = rows_of(after(k))
            give(k).wait_recv()
            total = x[spot, cols_of(core)].astype(F32) + from_mate[spot].astype(F32)
            paired[spot] = total.astype(BF)
            if k < pairs:
                hand(k).start()

    def settle():
        spot = rows_of(pair)
        total = paired[spot].astype(F32)
        for k in range(1, pairs):
            hand(k).wait_recv()
            total = total + slots[k].astype(F32)
        o[spot, cols_of(core)] = total.astype(BF)
        for k in range(1, pairs):
            spread(k).start()
        share(0).start()

    def pass_on():
        for k in range(1, pairs):
            spot = o.at[rows_of(before(k)), cols_of(core)]
            remote(spot, spot, ssem.at[2, k], rsem.at[2, k], mate).wait_recv()
            share(k).start()

    def finish():
        for k in range(pairs):
            spot = o.at[rows_of(before(k)), cols_of(1 - core)]
            remote(spot, spot, ssem.at[3, k], rsem.at[3, k], mate).wait_recv()
        for k in range(1, pairs + 1):
            give(k).wait_send()
        for k in range(1, pairs):
            hand(k).wait_send()
            spread(k).wait_send()
        for k in range(pairs):
            share(k).wait_send()

    return [start, pair_up, settle, pass_on, finish]


def reduce_scratch(rows, width):
    side = width // 2
    return [
        pltpu.VMEM((rows, side), BF),
        pltpu.VMEM((rows, side), BF),
        pltpu.VMEM((2 * rows, side), BF),
        pltpu.SemaphoreType.DMA((2, 8)),
        pltpu.SemaphoreType.DMA((2, 8)),
    ]


def square_reduce(p, x, kept, matrices, scratch):
    from_mate, paired, taken, ssem, rsem = scratch
    side = from_mate.shape[1]
    pair = p // 2
    core = p % 2
    mate = {"dp": p + 1 - 2 * core}

    def away_from(place, away):
        return {"dp": 2 * (place ^ away) + core}

    def cols_of(which):
        return pl.ds(pl.multiple_of(which * side, side), side)

    def give(m):
        _, first, rows = matrices[m]
        spot = pl.ds(first, rows)
        return remote(x.at[spot, cols_of(1 - core)], from_mate.at[spot], ssem.at[m, 0], rsem.at[m, 0], mate)

    def part_of(m, part):
        _, first, rows = matrices[m]
        return pl.ds(first + part * (rows // 2), rows // 2)

    def slot(m, near, part):
        _, first, rows = matrices[m]
        return pl.ds(2 * first + near * rows + part * (rows // 2), rows // 2)

    def opposite_send(m, part):
        place = matrices[m][0]
        return remote(
            paired.at[part_of(m, part)], taken.at[slot(m, 0, part)],
            ssem.at[m, 1 + part], rsem.at[m, 1], away_from(place, 1 + part),
        )

    def near_raw(m, near):
        part = 1 - near
        return remote(
            paired.at[part_of(m, part)], taken.at[slot(m, near, part)],
            ssem.at[m, 1], rsem.at[m, 2 + 2 * near], away_from(matrices[m][0], 0),
        )

    def near_mixed(m, near):
        part = near
        return remote(
            paired.at[part_of(m, part)], taken.at[slot(m, near, part)],
            ssem.at[m, 2], rsem.at[m, 3 + 2 * near], away_from(matrices[m][0], 0),
        )

    def swap(m):
        spot = kept.at[pl.ds(0, matrices[m][2]), cols_of(core)]
        return remote(spot, spot, ssem.at[m, 6], rsem.at[m, 6], mate)

    def arrived(ref, m, index):
        remote(ref, ref, ssem.at[m, 0], rsem.at[m, index], mate).wait_recv()

    def role(m, away):
        return pl.when(pair == (matrices[m][0] ^ away))

    every = range(len(matrices))

    def start():
        for m in every:
            give(m).start()

    def pair_up():
        for m in every:
            _, first, rows = matrices[m]
            spot = pl.ds(first, rows)
            give(m).wait_recv()
            total = x[spot, cols_of(core)].astype(F32) + from_mate[spot].astype(F32)
            paired[spot] = total.astype(BF)

            @role(m, 3)
            def _(m=m):
                for part in range(2):
                    opposite_send(m, part).start()

            for near in range(2):

                @role(m, 1 + near)
                def _(m=m, near=near):
                    near_raw(m, near).start()

    def mix():
        for m in every:
            for near in range(2):

                @role(m, 1 + near)
                def _(m=m, near=near):
                    piece = slot(m, 0, near)
                    arrived(taken.at[piece], m, 1)
                    spot = part_of(m, near)
                    total = paired[spot].astype(F32) + taken[piece].astype(F32)
                    paired[spot] = total.astype(BF)
                    near_mixed(m, near).start()

    def settle():
        for m in every:

            @role(m, 0)
            def _(m=m):
                _, first, rows = matrices[m]
                for near in range(2):
                    arrived(taken.at[slot(m, near, 1 - near)], m, 2 + 2 * near)
                    arrived(taken.at[slot(m, near, near)], m, 3 + 2 * near)
                spot = pl.ds(first, rows)
                total = x[spot, cols_of(core)].astype(F32) + from_mate[spot].astype(F32)
                for near in range(2):
                    total = total + taken[pl.ds(2 * first + near * rows, rows)].astype(F32)
                kept[pl.ds(0, rows), cols_of(core)] = total.astype(BF)
                swap(m).start()

    def finish():
        for m in every:
            rows = matrices[m][2]
            give(m).wait_send()

            @role(m, 0)
            def _(m=m, rows=rows):
                arrived(kept.at[pl.ds(0, rows), cols_of(1 - core)], m, 6)
                swap(m).wait_send()

            @role(m, 3)
            def _(m=m):
                for part in range(2):
                    opposite_send(m, part).wait_send()

            for near in range(2):

                @role(m, 1 + near)
                def _(m=m, near=near):
                    near_raw(m, near).wait_send()
                    near_mixed(m, near).wait_send()

    return [start, pair_up, mix, settle, finish]


def gather_scratch():
    return [pltpu.SemaphoreType.DMA((4, 2, 4))] * 2


def square_gather(p, sizes, out, own, scratch):
    ssem, rsem = scratch
    width = out.shape[1]
    pair = p // 2
    core = p % 2
    mate = {"dp": p + 1 - 2 * core}
    firsts = [sum(sizes[:index]) for index in range(4)]

    def piece(index, side, part):
        rows = sizes[index]
        if index == 2:
            across = pl.ds(pl.multiple_of(side * (width // 2), width // 2), width // 2)
            return out.at[pl.ds(firsts[index] + part * (rows // 2), rows // 2), across]
        quarter = rows // 4
        first = firsts[index] + side * 2 * quarter + part * quarter
        return out.at[pl.ds(pl.multiple_of(first, quarter), quarter)]

    def copy(index, part, route, device):
        spot = piece(index, core, part)
        return remote(spot, spot, ssem.at[index, part, route], rsem.at[index, part, route], device)

    def other(away):
        return {"dp": 2 * (pair + away * (1 - 2 * ((pair // away) % 2))) + core}

    def role(index, away):
        return pl.when(pair == (PLACE[index] ^ away))

    def wait_in(index, part, route, side):
        spot = piece(index, side, part)
        remote(spot, spot, ssem.at[index, part, route], rsem.at[index, part, route], mate).wait_recv()

    ways = ((1, 0, 2), (2, 1, 1))

    def start():
        for index in range(4):

            @role(index, 0)
            def _(index=index):
                for part in range(2):
                    piece(index, core, part)[...] = own(index, part)
                for part in range(2):
                    copy(index, part, 0, other(1)).start()
                    copy(index, 1 - part, 1, other(2)).start()
                for part in range(2):
                    copy(index, part, 3, mate).start()

    def pass_on():
        for index in range(4):
            for away, route, onward in ways:

                @role(index, away)
                def _(index=index, away=away, route=route, onward=onward):
                    wait_in(index, away - 1, route, core)
                    copy(index, away - 1, 2, other(onward)).start()
                    copy(index, away - 1, 3, mate).start()

    def rest():
        for index in range(4):
            for away, route, _ in ways:

                @role(index, away)
                def _(index=index, away=away, route=route):
                    wait_in(index, 2 - away, route, core)
                    copy(index, 2 - away, 3, mate).start()

            @role(index, 3)
            def _(index=index):
                for part in range(2):
                    wait_in(index, part, 2, core)
                    copy(index, part, 3, mate).start()

    def finish():
        for index in range(4):
            for part in range(2):
                wait_in(index, part, 3, 1 - core)
                copy(index, part, 3, mate).wait_send()

            @role(index, 0)
            def _(index=index):
                for part in range(2):
                    copy(index, part, 0, other(1)).wait_send()
                    copy(index, part, 1, other(2)).wait_send()

            for away, _, onward in ways:

                @role(index, away)
                def _(index=index, away=away, onward=onward):
                    copy(index, away - 1, 2, other(onward)).wait_send()

    return [start, pass_on, rest, finish]


def vector_scratch(count, shape):
    return [
        pltpu.VMEM((count,) + shape, F32),
        pltpu.SemaphoreType.DMA((count,)),
        pltpu.SemaphoreType.DMA((count,)),
    ]


def vector_sum(axis, count, p, v, o, scratch):
    slots, ssem, rsem = scratch

    def send(k):
        return remote(v, slots.at[p], ssem.at[k], rsem.at[k], {axis: (p + k) % count})

    def start():
        slots[p] = v[...]
        for k in range(1, count):
            send(k).start()

    def finish():
        for k in range(1, count):
            spot = slots.at[(p + count - k) % count]
            remote(v, spot, ssem.at[k], rsem.at[k], {axis: (p + k) % count}).wait_recv()
        total = slots[0]
        for k in range(1, count):
            total = total + slots[k]
        o[...] = total
        for k in range(1, count):
            send(k).wait_send()

    return [start, finish]


ROW_STEP = 32


def tdot(left, right):
    return lax.dot_general(left, right, (((0,), (0,)), ((), ())), preferred_element_type=F32)


def dot(left, right):
    return jnp.dot(left, right, preferred_element_type=F32)


def dot_t(left, right):
    return lax.dot_general(left, right, (((1,), (1,)), ((), ())), preferred_element_type=F32)


def layer_kernel(
    count,
    x, cot, seg, rp, hb, fb, mh, mf, wq_hbm, wo_hbm, wu_hbm, wd_hbm,
    y, dz1, bt, grads, vec, squares,
    wq_f, wo_f, wu_f, wd_f, wq, wo, wu, wd,
    q_s, k_s, v_s, ctx_s, p_s, n1_s, inv1_s, h1l_s, u_s, act_s, slope_s, dz2_s, dm_s, du_s, da_s,
    dq_s, dk_s, dv_s, part_s, red_s, gap, gbp, vecp, wsem, *scratch,
):
    p = lax.axis_index("dp")
    t = lax.axis_index("tensor")
    tokens, width = x.shape
    half = tokens // 2
    columns = q_s.shape[1]
    heads = columns // HD
    scale = 1.0 / math.sqrt(HD)
    greet(z_peers(t) + [{"dp": (p + k) % count} for k in range(1, count)])
    loads = [
        pltpu.make_async_copy(source, target, wsem.at[i])
        for i, (source, target) in enumerate(
            ((wq_hbm, wq_f), (wo_hbm, wo_f), (wu_hbm, wu_f), (wd_hbm, wd_f))
        )
    ]
    for load in loads:
        load.start()
    sums = []
    for h in range(2):
        place = pl.ds(h * half, half)
        sums.append(
            line_sum(t, part_s.at[place], red_s.at[place], scratch[6 * h : 6 * h + 6])
        )
    top = 4 * columns
    if count == 8:
        ends = [(PLACE[2], 0, width), (PLACE[3], width, width)]
        plane_b = square_reduce(p, gbp, grads, ends, scratch[12:17])
        ends = [(PLACE[0], 0, 3 * columns), (PLACE[1], 3 * columns, columns)]
        plane_a = square_reduce(p, gap, grads, ends, scratch[17:22])
    else:
        plane_b = plane_sum(count, p, gbp, grads.at[pl.ds(top, 2 * width)], scratch[12:17])
        plane_a = plane_sum(count, p, gap, grads.at[pl.ds(0, top)], scratch[17:22])
    vector = vector_sum("dp", count, p, vecp, vec, scratch[22:25])
    vecp[...] = jnp.zeros_like(vecp)
    lane = lax.broadcasted_iota(jnp.int32, (1, columns), 1)

    def in_head(index):
        return (lane // HD) == index

    def rows_of(h):
        return pl.ds(h * half, half)

    def over_rows(h, body, init=0):
        def step(i, carry):
            first = h * half + i * ROW_STEP
            return body(pl.ds(pl.multiple_of(first, ROW_STEP), ROW_STEP), carry)

        return lax.fori_loop(0, half // ROW_STEP, step, init)

    def fold(values):
        return values.reshape(ROW_STEP // 8, 8, values.shape[1]).sum(axis=0)

    def add_vec(row, folded):
        vecp[row : row + 1, 0 : folded.shape[1]] += jnp.sum(folded, axis=0, keepdims=True)

    def narrow(index, source, target):
        loads[index].wait()
        if len(source.shape) == 3:
            for i in range(source.shape[0]):
                target[i] = source[i].astype(BF)
        else:
            target[...] = source[...].astype(BF)

    def attention(h):
        r = rows_of(h)
        xb = x[r]
        q = (dot_t(xb, wq[0]) + hb[0:1]).astype(BF)
        k = dot_t(xb, wq[1]).astype(BF)
        v = (dot_t(xb, wq[2]) + hb[1:2]).astype(BF)
        q_s[r], k_s[r], v_s[r] = q, k, v
        down = jnp.broadcast_to(seg[h : h + 1].astype(F32), (half, half))
        same = down == down.T
        context = jnp.zeros((half, columns), F32)
        for index in range(heads):
            mine = jnp.where(in_head(index), q, jnp.zeros_like(q))
            scores = jnp.where(same, dot_t(mine, k) * scale, -1e30)
            expo = jnp.exp(scores - jnp.max(scores, axis=-1, keepdims=True))
            probs = expo / jnp.sum(expo, axis=-1, keepdims=True)
            p_s[h * heads + index] = probs
            context = jnp.where(in_head(index), dot(probs.astype(BF), v), context)
        low = context.astype(BF)
        ctx_s[r] = low
        part_s[r] = dot(low, wo[...]).astype(BF)

    def up(h):
        def norm(r, carry):
            z = x[r].astype(F32) + red_s[r].astype(F32) + rp[0:1]
            center = z - jnp.mean(z, axis=-1, keepdims=True)
            inverse = lax.rsqrt(jnp.mean(center * center, axis=-1, keepdims=True) + EPS_NORM)
            normed = center * inverse
            n1_s[r] = normed
            inv1_s[r] = jnp.broadcast_to(inverse, (ROW_STEP, 128))
            h1l_s[r] = (normed * rp[2:3] + rp[3:4]).astype(BF)
            return carry

        over_rows(h, norm)
        u_s[rows_of(h)] = dot(h1l_s[rows_of(h)], wu[...])

        def gelu(r, carry):
            u = u_s[r] + fb[0:1]
            cdf = 0.5 * (1.0 + lax.erf(u * (1.0 / math.sqrt(2.0))))
            act_s[r] = (u * cdf).astype(BF)
            slope_s[r] = cdf + u * jnp.exp(-0.5 * u * u) * (1.0 / math.sqrt(2.0 * math.pi))
            return carry

        over_rows(h, gelu)

    def down(h):
        r = rows_of(h)
        part_s[r] = dot(act_s[r], wd[...]).astype(BF)

    def out_back(h):
        def norm(r, carry):
            s_dz2, s_dyn, s_dy = carry
            h1 = n1_s[r] * rp[2:3] + rp[3:4]
            z = h1 + red_s[r].astype(F32) + rp[1:2]
            center = z - jnp.mean(z, axis=-1, keepdims=True)
            inverse = lax.rsqrt(jnp.mean(center * center, axis=-1, keepdims=True) + EPS_NORM)
            normed = center * inverse
            y[r] = (normed * rp[4:5] + rp[5:6]).astype(BF)
            dy = cot[r].astype(F32)
            scaled = dy * rp[4:5]
            first = jnp.mean(scaled, axis=-1, keepdims=True)
            second = jnp.mean(scaled * normed, axis=-1, keepdims=True)
            dz2 = inverse * (scaled - first - normed * second)
            dz2_s[r] = dz2
            dm_s[r] = dz2.astype(BF)
            return s_dz2 + fold(dz2), s_dyn + fold(dy * normed), s_dy + fold(dy)

        zero = jnp.zeros((8, width), F32)
        for row, total in zip((1, 4, 5), over_rows(h, norm, (zero, zero, zero))):
            add_vec(row, total)
        u_s[rows_of(h)] = dot_t(dm_s[rows_of(h)], wd[...])

        def slope(r, carry):
            du = (u_s[r] * slope_s[r]).astype(BF)
            du_s[r] = du
            return carry + fold(du.astype(F32))

        add_vec(6, over_rows(h, slope, zero))

    def up_back(h):
        r = rows_of(h)
        part_s[r] = dot_t(du_s[r], wu[...]).astype(BF)

    def grads_b():
        gbp[0:width] = tdot(h1l_s[...], du_s[...]).astype(BF)
        gbp[width : 2 * width] = tdot(act_s[...], dm_s[...]).astype(BF)

    def attention_back(h):
        def norm(r, carry):
            s_dz1, s_dhn, s_dh = carry
            dh1 = red_s[r].astype(F32) + dz2_s[r]
            normed = n1_s[r]
            scaled = dh1 * rp[2:3]
            first = jnp.mean(scaled, axis=-1, keepdims=True)
            second = jnp.mean(scaled * normed, axis=-1, keepdims=True)
            grad = inv1_s[r][:, 0:1] * (scaled - first - normed * second)
            dz1[r] = grad
            da_s[r] = grad.astype(BF)
            return s_dz1 + fold(grad), s_dhn + fold(dh1 * normed), s_dh + fold(dh1)

        zero = jnp.zeros((8, width), F32)
        for row, total in zip((0, 2, 3), over_rows(h, norm, (zero, zero, zero))):
            add_vec(row, total)
        r = rows_of(h)
        dc = dot_t(da_s[r], wo[...]).astype(BF)
        q, k, v = q_s[r], k_s[r], v_s[r]
        dq = dk = dv = jnp.zeros((half, columns), F32)
        for index in range(heads):
            probs = p_s[h * heads + index]
            mine = jnp.where(in_head(index), dc, jnp.zeros_like(dc))
            dp = dot_t(mine, v)
            ds = (probs * (dp - jnp.sum(probs * dp, axis=-1, keepdims=True))).astype(BF)
            dv = jnp.where(in_head(index), tdot(probs.astype(BF), dc), dv)
            dq = jnp.where(in_head(index), dot(ds, k), dq)
            dk = jnp.where(in_head(index), tdot(ds, q), dk)
        dq = (dq * scale).astype(BF)
        dk = (dk * scale).astype(BF)
        dv = dv.astype(BF)
        dq_s[r], dk_s[r], dv_s[r] = dq, dk, dv
        add_vec(7, jnp.sum(dq.astype(F32), axis=0, keepdims=True))
        add_vec(8, jnp.sum(dv.astype(F32), axis=0, keepdims=True))

    def grads_a():
        for i, source in enumerate((dq_s, dk_s, dv_s)):
            gap[i * columns : (i + 1) * columns] = tdot(source[...], x[...]).astype(BF)
        gap[3 * columns : 4 * columns] = tdot(ctx_s[...], da_s[...]).astype(BF)

    def back_terms(h):
        r = rows_of(h)
        total = dot(dq_s[r], wq[0]) + dot(dk_s[r], wq[1]) + dot(dv_s[r], wq[2])
        bt[r] = total.astype(BF)

    (a_start, a_mix, a_settle, a_pass, a_end), (b_start, b_mix, b_settle, b_pass, b_end) = sums
    narrow(0, wq_f, wq)
    narrow(1, wo_f, wo)
    attention(0)
    a_start()
    attention(1)
    a_mix()
    b_start()
    narrow(2, wu_f, wu)
    a_settle()
    b_mix()
    a_pass()
    b_settle()
    narrow(3, wd_f, wd)
    a_end()
    up(0)
    b_pass()
    down(0)
    a_start()
    b_end()
    up(1)
    a_mix()
    down(1)
    b_start()
    a_settle()
    b_mix()
    a_pass()
    b_settle()
    a_end()
    out_back(0)
    b_pass()
    up_back(0)
    a_start()
    b_end()
    out_back(1)
    a_mix()
    up_back(1)
    b_start()
    grads_b()
    plane_b[0]()
    a_settle()
    b_mix()
    plane_b[1]()
    a_pass()
    b_settle()
    a_end()
    if count == 8:
        plane_b[2]()
    attention_back(0)
    b_pass()
    b_end()
    attention_back(1)
    grads_a()
    plane_a[0]()
    vector[0]()
    if count != 8:
        plane_b[2]()
    plane_a[1]()
    back_terms(0)
    back_terms(1)
    plane_b[3]()
    plane_a[2]()
    vector[1]()
    moved = 0.5 * mh[...] + vec[7:9, 0:columns]
    squares[0:2] = jnp.broadcast_to(jnp.sum(moved * moved, axis=1, keepdims=True), (2, 128))
    moved = 0.5 * mf[...] + vec[6:7]
    squares[2:3] = jnp.broadcast_to(jnp.sum(moved * moved, axis=1, keepdims=True), (1, 128))
    squares[3:8] = jnp.zeros((5, 128), F32)
    plane_a[3]()
    plane_b[4]()
    plane_a[4]()


def layer(count, tokens, cotangent, segments, small, weights, collective_id):
    rows, width = tokens.shape
    w_qkv, w_out, w_up, w_down = weights
    columns = w_qkv.shape[1]
    heads = columns // HD
    half = rows // 2
    grads = width if count == 8 else 4 * columns + 2 * width

    def low(*shape):
        return pltpu.VMEM(shape, BF)

    def full(*shape):
        return pltpu.VMEM(shape, F32)

    def out(shape, dtype):
        return jax.ShapeDtypeStruct(shape, dtype)

    scratch = (
        [full(*weight.shape) for weight in weights]
        + [low(*weight.shape) for weight in weights]
        + [low(rows, columns)] * 4
        + [full(2 * heads, half, half), full(rows, width), full(rows, 128), low(rows, width)]
        + [full(rows, width), low(rows, width), full(rows, width), full(rows, width)]
        + [low(rows, width)] * 3
        + [low(rows, columns)] * 3
        + [low(rows, width)] * 2
        + [low(4 * columns, width), low(2 * width, width), full(16, width)]
        + [pltpu.SemaphoreType.DMA((4,))]
        + line_scratch(half, width, BF) * 2
        + (reduce_scratch(2 * width, width) if count == 8 else plane_scratch(count, 2 * width, width))
        + (
            reduce_scratch(4 * columns, width)
            if count == 8
            else plane_scratch(count, 4 * columns, width)
        )
        + vector_scratch(count, (16, width))
    )
    return pl.pallas_call(
        functools.partial(layer_kernel, count),
        out_shape=(
            out((rows, width), BF),
            out((rows, width), F32),
            out((rows, width), BF),
            out((grads, width), BF),
            out((16, width), F32),
            out((8, 128), F32),
        ),
        in_specs=[IN_VMEM] * 8 + [IN_ANY] * 4,
        out_specs=(IN_VMEM,) * 6,
        scratch_shapes=scratch,
        compiler_params=params(collective_id, 56),
        name="layer",
    )(tokens, cotangent, segments, *small, *weights)


def cut(values):
    high = values.astype(BF)
    return high, (values - high.astype(F32)).astype(BF)


def dot3(lh, ll, rh, rl, dims=(((1,), (0,)), ((), ()))):
    def dot(left, right):
        return lax.dot_general(left, right, dims, preferred_element_type=F32)

    return dot(lh, rh) + (dot(lh, rl) + dot(ll, rh))


def muon_kernel(
    count, sizes,
    mq, mo, mu, md, grads, vs, bx, dz1,
    xo, gall, vt, bo,
    zf, gf, zh, zl, gx, go, gp, af, ah, al, dh, dl, sf, sh, sl, xf, bs, lsem, psem, *scratch,
):
    p = lax.axis_index("dp")
    t = lax.axis_index("tensor")
    width = zf.shape[1]
    group = count // 4
    which = p // group
    core = p % 2
    mate = {"dp": p + 1 - 2 * core}
    share = xf.shape[0]
    tile = width // 3
    greet(z_peers(t) + [{"dp": (p + k) % count} for k in range(1, count)])
    vector = vector_sum("tensor", 4, t, vs, vt, scratch[12:15])
    back = line_sum(t, bx, bs, scratch[6:12])
    vector[0]()
    firsts = [sum(sizes[:index]) for index in range(4)]
    for index, moment in enumerate((mq, mo, mu, md)):
        rows = sizes[index]
        first = 0 if count == 8 else firsts[index]

        @pl.when(which == PLACE[index])
        def _(index=index, moment=moment, first=first, rows=rows):
            one = pltpu.make_async_copy(moment, sf.at[pl.ds(0, rows)], lsem.at[0])
            two = pltpu.make_async_copy(
                grads.at[pl.ds(first, rows)], gf.at[pl.ds(0, rows)], lsem.at[1]
            )
            one.start()
            two.start()
            one.wait()
            two.wait()
            for i in range(3):
                spot = pl.ds(i * (rows // 3), rows // 3)
                z = 0.5 * sf[spot] + gf[spot].astype(F32)
                if index == 2:
                    z = z.T
                    spot = (pl.ds(0, width), spot)
                zf[spot] = z
                zh[spot], zl[spot] = cut(z)
            if rows < width:
                spot = pl.ds(rows, width - rows)
                zf[spot] = jnp.zeros((width - rows, width), F32)
                zh[spot] = jnp.zeros((width - rows, width), BF)
                zl[spot] = jnp.zeros((width - rows, width), BF)

    if count == 8:

        def own_gradient(index, part):
            if index == 2:
                across = pl.ds(pl.multiple_of(core * (width // 2), width // 2), width // 2)
                return gf[pl.ds(part * (width // 2), width // 2), across]
            quarter = sizes[index] // 4
            first = pl.multiple_of((2 * core + part) * quarter, quarter)
            return gf[pl.ds(first, quarter)]

        def own_step(index, part):
            if index == 2:
                return xf[:, pl.ds(part * (width // 2), width // 2)].T.astype(BF)
            quarter = sizes[index] // 4
            return xf[pl.ds(part * quarter, quarter)].astype(BF)

        spread = square_gather(p, sizes, gall, own_gradient, scratch[15:17])
        spread[0]()

    def cols(index):
        return pl.ds(pl.multiple_of(index * tile, tile), tile)

    over_rows = (((0,), (0,)), ((), ()))
    for j, (row, col) in enumerate(((core, core), (core, core + 1), (2 * core, 2))):
        gx[:, pl.ds(j * tile, tile)] = dot3(
            zh[:, cols(row)], zl[:, cols(row)], zh[:, cols(col)], zl[:, cols(col)], over_rows
        )
    for step in line_sum(t, gx, go, scratch[:6]):
        step()
    swap = remote(go, gp, psem.at[0], psem.at[1], mate)
    swap.start()
    back[0]()
    swap.wait()
    diagonal = lax.broadcasted_iota(jnp.int32, (tile, tile), 0) == lax.broadcasted_iota(
        jnp.int32, (tile, tile), 1
    )

    def upper(first, second):
        trace = jnp.float32(0.0)
        for block in (first[:, 0:tile], second[:, 0:tile], second[:, 2 * tile :]):
            trace = trace + jnp.sum(jnp.where(diagonal, block, 0.0))
        inverse = 1.0 / (jnp.sqrt(jnp.full((1, 1), trace, F32)) + 1e-07)
        scale = inverse * inverse
        blocks = (
            (0, 0, first, 0), (0, 1, first, 1), (0, 2, first, 2),
            (1, 1, second, 0), (1, 2, second, 1), (2, 2, second, 2),
        )
        for row, col, source, j in blocks:
            block = source[:, j * tile : (j + 1) * tile] * scale
            for r, c, value in ((row, col, block),) + (((col, row, block.T),) if row != col else ()):
                spot = (pl.ds(r * tile, tile), pl.ds(c * tile, tile))
                af[spot] = value
                ah[spot], al[spot] = cut(value)
        if group == 2:
            for index, rows in enumerate(sizes):

                @pl.when(which == PLACE[index])
                def _(half=rows // 2):
                    xf[0:half] = zf[pl.ds(pl.multiple_of(core * half, half), half)] * inverse
                    if half < share:
                        xf[half:share] = jnp.zeros((share - half, width), F32)

        else:
            rank = p % group
            xf[...] = zf[pl.ds(pl.multiple_of(rank * share, share), share)] * inverse

    @pl.when(core == 0)
    def _():
        upper(go, gp)

    @pl.when(core == 1)
    def _():
        upper(gp, go)

    vector[1]()

    def product(left, right, base, base_scale, scale, targets):
        (lh, ll), (rh, rl) = left, right
        for i in range(3):
            rows = pl.ds(i * tile, tile)
            for j in range(i, 3):
                columns = pl.ds(j * tile, tile)
                value = base_scale * base[rows, columns] + scale * dot3(
                    lh[rows], ll[rows], rh[:, columns], rl[:, columns]
                )
                for target, part in zip(targets, (*cut(value), value)):
                    target[rows, columns] = part
                    if i != j:
                        target[columns, rows] = part.T

    def make_d():
        product((ah, al), (ah, al), af, coef_b, coef_c, (dh, dl))

    def move_x():
        xh, xl = cut(xf[...])
        xf[...] = coef_a * xf[...] + dot3(xh, xl, dh[...], dl[...])

    def sweep(k, carry):
        make_d()
        move_x()
        product((ah, al), (dh, dl), af, coef_a, 1.0, (sh, sl, sf))
        product((sh, sl), (dh, dl), sf, coef_a, 1.0, (ah, al, af))
        for i in range(1, 4):
            pl.when(k == i - 1)(back[i])
            if count == 8 and i < 3:
                pl.when(k == i - 1)(spread[i])
        return carry

    lax.fori_loop(0, 4, sweep, 0)
    make_d()
    move_x()
    back[4]()
    bo[...] = (bs[...].astype(F32) + dz1[...]).astype(BF)
    if count == 8:
        spread[3]()
        for step in square_gather(p, sizes, xo, own_step, scratch[17:19]):
            step()
    else:
        gall[...] = jnp.zeros_like(gall)
        gather_any(p, core, count // 2, mate, xf, xo, scratch[15], scratch[16])


def gather_any(p, core, pairs, mate, xf, xo, asem_s, asem_r):
    pair = p // 2
    share = xf.shape[0]

    def rows_of(device):
        return xo.at[pl.ds(pl.multiple_of(device * share, share), share)]

    def after(k):
        return 2 * ((pair + k) % pairs) + core

    def before(k):
        return 2 * ((pair + pairs - k) % pairs) + core

    def send(k):
        return remote(rows_of(p), rows_of(p), asem_s.at[0, k], asem_r.at[0, k], {"dp": after(k)})

    def hand(k):
        spot = rows_of(before(k))
        return remote(spot, spot, asem_s.at[1, k], asem_r.at[1, k], mate)

    xo[pl.ds(pl.multiple_of(p * share, share), share)] = xf[...].astype(BF)
    for k in range(1, pairs):
        send(k).start()
    hand(0).start()
    for k in range(1, pairs):
        spot = rows_of(before(k))
        remote(spot, spot, asem_s.at[0, k], asem_r.at[0, k], mate).wait_recv()
        hand(k).start()
    for k in range(pairs):
        spot = rows_of(before(k) + 1 - 2 * core)
        remote(spot, spot, asem_s.at[1, k], asem_r.at[1, k], mate).wait_recv()
    for k in range(1, pairs):
        send(k).wait_send()
    for k in range(pairs):
        hand(k).wait_send()


def muon(count, moments, grads, squares, back, grad_first, collective_id):
    width = grads.shape[1]
    tile = width // 3
    share = width // (count // 4)
    sizes = tuple(moment.shape[0] for moment in moments)
    square = count == 8

    def vmem(dtype, rows=width, columns=width):
        return pltpu.VMEM((rows, columns), dtype)

    def out(shape, dtype):
        return jax.ShapeDtypeStruct(shape, dtype)

    pair_sems = [pltpu.SemaphoreType.DMA((2, count // 2))] * 2
    scratch = (
        [vmem(F32), vmem(BF), vmem(BF), vmem(BF)]
        + [vmem(F32, tile)] * 3
        + [vmem(F32), vmem(BF), vmem(BF), vmem(BF), vmem(BF), vmem(F32), vmem(BF), vmem(BF)]
        + [vmem(F32, share), vmem(BF, back.shape[0])]
        + [pltpu.SemaphoreType.DMA((2,)), pltpu.SemaphoreType.DMA((2,))]
        + line_scratch(tile, width, F32)
        + line_scratch(*back.shape, BF)
        + vector_scratch(4, squares.shape)
        + (gather_scratch() * 2 if square else pair_sems)
    )
    return pl.pallas_call(
        functools.partial(muon_kernel, count, sizes),
        out_shape=(
            out((sum(sizes) if square else 4 * width, width), BF),
            out((sum(sizes), width) if square else (16, width), BF),
            out(squares.shape, F32),
            out(back.shape, BF),
        ),
        in_specs=[IN_ANY] * 5 + [IN_VMEM] * 3,
        out_specs=(IN_VMEM,) * 4,
        scratch_shapes=scratch,
        compiler_params=params(collective_id, 44),
        name="muon",
    )(*moments, grads, squares, back, grad_first)


def vector_step(param, moment, mean_sq):
    return param - 0.1 * moment * lax.rsqrt(mean_sq + 1e-06)


def local(
    tokens, segments, cotangent,
    w_qkv, w_out, w_up, w_down, head_bias, ff_bias, row_params,
    mom_qkv, mom_out, mom_up, mom_down, mom_heads, mom_ff, mom_params,
):
    width = tokens.shape[1]
    columns = w_qkv.shape[2]
    ff_cols = w_up.shape[1]
    tensor_size = lax.axis_size("tensor")
    count = lax.axis_size("dp")
    qkv_rows = 3 * columns
    wq_rows = w_qkv.transpose(0, 2, 1)
    output_rows, grad_first, back_terms, grads, vector_total, squares = layer(
        count, tokens, cotangent, segments,
        (row_params, head_bias, ff_bias.reshape(1, ff_cols), mom_heads, mom_ff.reshape(1, ff_cols)),
        (wq_rows, w_out, w_up, w_down), 1,
    )
    new_mom_heads = 0.5 * mom_heads + vector_total[7:9, :columns]
    new_mom_ff = 0.5 * mom_ff + vector_total[6]
    new_mom_params = 0.5 * mom_params + vector_total[0:6]
    moments = (mom_qkv.transpose(0, 2, 1).reshape(qkv_rows, width), mom_out, mom_up, mom_down)
    steps, gathered, totals, grad_inputs = muon(
        count, moments, grads, squares, back_terms, grad_first, 2
    )
    if count == 8:
        grads = gathered

    def to_qkv(rows):
        return rows.reshape(3, columns, width).transpose(0, 2, 1)

    bounds = (0, qkv_rows, qkv_rows + columns, qkv_rows + columns + width)

    def grad_of(index, rows):
        return grads[bounds[index] : bounds[index] + rows].astype(F32)

    def step_of(index, rows):
        first = bounds[index] if count == 8 else PLACE[index] * width
        part = steps[first : first + rows].astype(F32)
        return part.T if index == 2 and count != 8 else part

    new_mom_qkv = 0.5 * mom_qkv + to_qkv(grad_of(0, qkv_rows))
    new_mom_out = 0.5 * mom_out + grad_of(1, columns)
    new_mom_up = 0.5 * mom_up + grad_of(2, width)
    new_mom_down = 0.5 * mom_down + grad_of(3, ff_cols)
    wide = math.sqrt(ff_cols * tensor_size / width)
    new_qkv = w_qkv - 0.8 * math.sqrt(3.0) * to_qkv(step_of(0, qkv_rows))
    new_out = w_out - 0.8 * step_of(1, columns)
    new_up = w_up - 0.8 * wide * step_of(2, width)
    new_down = w_down - 0.8 * wide * step_of(3, ff_cols)
    new_heads = vector_step(head_bias, new_mom_heads, totals[0:2, 0:1] / (columns * tensor_size))
    new_ff = vector_step(ff_bias, new_mom_ff, totals[2, 0] / (ff_cols * tensor_size))
    new_params = vector_step(
        row_params,
        new_mom_params,
        jnp.mean(new_mom_params * new_mom_params, axis=-1, keepdims=True),
    )
    return (
        output_rows,
        grad_inputs,
        new_mom_qkv, new_qkv, new_qkv.astype(BF),
        new_mom_out, new_out, new_out.astype(BF),
        new_mom_up, new_up, new_up.astype(BF),
        new_mom_down, new_down, new_down.astype(BF),
        new_mom_heads, new_heads,
        new_mom_ff, new_ff,
        new_mom_params, new_params,
    )


def solution(mesh):
    placed = (
        P("dp", None), P("dp", None), P("dp", None),
        P(None, None, "tensor"), P("tensor", None), P(None, "tensor"), P("tensor", None),
        P(None, "tensor"), P("tensor"), P(),
        P(None, None, "tensor"), P("tensor", None), P(None, "tensor"), P("tensor", None),
        P(None, "tensor"), P("tensor"), P(),
    )
    triple = ((P(None, None, "tensor"),) * 3, (P("tensor", None),) * 3, (P(None, "tensor"),) * 3)
    return jax.shard_map(
        local,
        mesh=mesh,
        in_specs=placed,
        out_specs=(
            (P("dp", None), P("dp", None))
            + triple[0] + triple[1] + triple[2] + triple[1]
            + (P(None, "tensor"), P(None, "tensor"), P("tensor"), P("tensor"), P(), P())
        ),
        check_vma=False,
    )
```

```python
import functools
import math

import jax
import jax.numpy as jnp
from jax import lax
from jax.experimental import pallas as pl
from jax.experimental.pallas import tpu as pltpu
from jax.sharding import PartitionSpec as P

HD = 64
EPS_NORM = 1e-05
coef_a = 3.4445
coef_b = -4.775
coef_c = 2.0315
BF = jnp.bfloat16
F32 = jnp.float32
MESH = pl.DeviceIdType.MESH
SUBS = 2
PLACE = (1, 2, 0, 3)


def remote(src, dst, send_sem, recv_sem, device):
    return pltpu.make_async_remote_copy(
        src_ref=src,
        dst_ref=dst,
        send_sem=send_sem,
        recv_sem=recv_sem,
        device_id=device,
        device_id_type=MESH,
    )


def greet(devices):
    barrier = pltpu.get_barrier_semaphore()
    for device in devices:
        pl.semaphore_signal(barrier, inc=1, device_id=device, device_id_type=MESH)
    pl.semaphore_wait(barrier, len(devices))


def z_peers(t):
    return [{"tensor": (t + k) % 4} for k in range(1, 4)]


def line_scratch(rows, width, dtype):
    part = rows // 4
    return [
        pltpu.VMEM((part, width), dtype),
        pltpu.VMEM((part, width), dtype),
        pltpu.VMEM((2 * part, width), dtype),
        pltpu.VMEM((2 * part, width), dtype),
        pltpu.SemaphoreType.DMA((8 * SUBS,)),
        pltpu.SemaphoreType.DMA((8 * SUBS,)),
    ]


def line_sum(t, x, o, scratch):
    raw, cmb, fwd, mix, ssem, rsem = scratch
    part = raw.shape[0]
    half = part // SUBS
    subs = range(SUBS)
    mate = t + 1 - 2 * (t % 2)
    outer = (t % 3) == 0
    inner = (t % 3) != 0

    def at(ref, chunk, s):
        return ref.at[pl.ds(pl.multiple_of(chunk * part + s * half, half), half)]

    def to(index, src, dst, recv, device):
        return remote(src, dst, ssem.at[index], rsem.at[recv], {"tensor": device})

    def ag_sem(chunk, s):
        return (4 + chunk) * SUBS + s

    def o_far(s):
        return to(s, at(x, 3 - t, s), at(fwd, 0, s), 2 * SUBS + s, mate)

    def o_near(s):
        return to(SUBS + s, at(x, 3 - mate, s), at(fwd, 1, s), 3 * SUBS + s, mate)

    def o_raw(s):
        return to(2 * SUBS + s, at(x, mate, s), at(raw, 0, s), s, mate)

    def o_own(s):
        return to(3 * SUBS + s, at(o, t, s), at(o, t, s), ag_sem(t, s), mate)

    def i_raw(s):
        return to(s, at(x, mate, s), at(raw, 0, s), s, mate)

    def i_far(s):
        return to(SUBS + s, at(mix, 0, s), at(cmb, 0, s), SUBS + s, 3 - mate)

    def i_near(s):
        return to(2 * SUBS + s, at(mix, 1, s), at(cmb, 0, s), SUBS + s, 3 - t)

    def i_ag(place, chunk, s, device):
        return to(place * SUBS + s, at(o, chunk, s), at(o, chunk, s), ag_sem(chunk, s), device)

    def got(dst, recv):
        remote(dst, dst, ssem.at[0], rsem.at[recv], {"tensor": mate}).wait_recv()

    def add(dst, *terms):
        total = terms[0][...].astype(F32)
        for term in terms[1:]:
            total = total + term[...].astype(F32)
        dst[...] = total.astype(dst.dtype)

    def start():
        @pl.when(outer)
        def _():
            for build in (o_far, o_near, o_raw):
                for s in subs:
                    build(s).start()

        @pl.when(inner)
        def _():
            for s in subs:
                i_raw(s).start()

    def combine():
        @pl.when(inner)
        def _():
            for slot, chunk, build in ((0, 3 - mate, i_far), (1, 3 - t, i_near)):
                for s in subs:
                    got(at(fwd, slot, s), (2 + slot) * SUBS + s)
                    add(at(mix, slot, s), at(fwd, slot, s), at(x, chunk, s))
                    build(s).start()

    def settle():
        for s in subs:
            got(at(raw, 0, s), s)
            got(at(cmb, 0, s), SUBS + s)
            add(at(o, t, s), at(x, t, s), at(raw, 0, s), at(cmb, 0, s))

            @pl.when(outer)
            def _(s=s):
                o_own(s).start()

            @pl.when(inner)
            def _(s=s):
                i_ag(3, t, s, 3 - t).start()
                i_ag(4, t, s, mate).start()

    def pass_on():
        @pl.when(inner)
        def _():
            for s in subs:
                got(at(o, mate, s), ag_sem(mate, s))
                i_ag(5, mate, s, 3 - t).start()
            for s in subs:
                got(at(o, 3 - t, s), ag_sem(3 - t, s))
                i_ag(6, 3 - t, s, mate).start()
            for s in subs:
                got(at(o, 3 - mate, s), ag_sem(3 - mate, s))
                i_ag(7, 3 - mate, s, mate).start()

    def finish():
        @pl.when(outer)
        def _():
            for chunk in (mate, 3 - mate, 3 - t):
                for s in subs:
                    got(at(o, chunk, s), ag_sem(chunk, s))
            for build in (o_far, o_near, o_raw, o_own):
                for s in subs:
                    build(s).wait_send()

        @pl.when(inner)
        def _():
            for s in subs:
                for build in (i_raw, i_far, i_near):
                    build(s).wait_send()
                i_ag(3, t, s, 3 - t).wait_send()
                i_ag(4, t, s, mate).wait_send()
                i_ag(5, mate, s, 3 - t).wait_send()
                i_ag(6, 3 - t, s, mate).wait_send()
                i_ag(7, 3 - mate, s, mate).wait_send()

    return [start, combine, settle, pass_on, finish]


def relay_scratch(rows, width, dtype):
    part = rows // 2
    return [
        pltpu.VMEM((2 * part, width), dtype),
        pltpu.VMEM((part, width), dtype),
        pltpu.VMEM((part, width), dtype),
        pltpu.SemaphoreType.DMA((5 * SUBS,)),
        pltpu.SemaphoreType.DMA((5 * SUBS,)),
    ]


def relay_sum(t, x, o, scratch):
    taken, mixed, mix, ssem, rsem = scratch
    part = mixed.shape[0]
    piece = part // SUBS
    subs = range(SUBS)
    mate = t + 1 - 2 * (t % 2)
    facing = 3 - t
    outer = (t % 3) == 0
    inner = (t % 3) != 0
    near = t // 2
    far = 1 - near

    def at(ref, chunk, s):
        return ref.at[pl.ds(pl.multiple_of(chunk * part + s * piece, piece), piece)]

    def to(index, src, dst, recv, device):
        return remote(
            src, dst, ssem.at[index], rsem.at[recv], {"tensor": device}
        )

    def give_far(s):
        return to(s, at(x, far, s), at(taken, 0, s), s, mate)

    def give_near(s):
        return to(SUBS + s, at(x, near, s), at(taken, 1, s), SUBS + s, mate)

    def cross(s):
        return to(s, at(mix, 0, s), at(mixed, 0, s), 2 * SUBS + s, facing)

    def own_across(s):
        return to(SUBS + s, at(o, near, s), at(o, near, s), (3 + near) * SUBS + s, facing)

    def own_out(s):
        return to(2 * SUBS + s, at(o, near, s), at(o, near, s), (3 + near) * SUBS + s, mate)

    def far_out(s):
        return to(3 * SUBS + s, at(o, far, s), at(o, far, s), (3 + far) * SUBS + s, mate)

    def got(dst, recv):
        remote(dst, dst, ssem.at[0], rsem.at[recv], {"tensor": mate}).wait_recv()

    def add(dst, *terms):
        total = terms[0][...].astype(F32)
        for term in terms[1:]:
            total = total + term[...].astype(F32)
        dst[...] = total.astype(dst.dtype)

    def start():
        @pl.when(outer)
        def _():
            for build in (give_far, give_near):
                for s in subs:
                    build(s).start()

    def combine():
        @pl.when(inner)
        def _():
            for s in subs:
                got(at(taken, 0, s), s)
                add(at(mix, 0, s), at(taken, 0, s), at(x, far, s))
                cross(s).start()

    def settle():
        @pl.when(inner)
        def _():
            for s in subs:
                got(at(taken, 1, s), SUBS + s)
                got(at(mixed, 0, s), 2 * SUBS + s)
                add(at(o, near, s), at(x, near, s), at(taken, 1, s), at(mixed, 0, s))
                own_across(s).start()
                own_out(s).start()

    def pass_on():
        @pl.when(inner)
        def _():
            for s in subs:
                got(at(o, far, s), (3 + far) * SUBS + s)
                far_out(s).start()

    def finish():
        @pl.when(outer)
        def _():
            for chunk in (near, far):
                for s in subs:
                    got(at(o, chunk, s), (3 + chunk) * SUBS + s)
            for build in (give_far, give_near):
                for s in subs:
                    build(s).wait_send()

        @pl.when(inner)
        def _():
            for build in (cross, own_across, own_out, far_out):
                for s in subs:
                    build(s).wait_send()

    return [start, combine, settle, pass_on, finish]


def params(collective_id, mebibytes):
    return pltpu.CompilerParams(
        collective_id=collective_id,
        has_side_effects=True,
        vmem_limit_bytes=mebibytes * 1024 * 1024,
    )


IN_VMEM = pl.BlockSpec(memory_space=pltpu.VMEM)
IN_HBM = pl.BlockSpec(memory_space=pltpu.HBM)


def plane_scratch(count, rows, width):
    pairs = count // 2
    side = width // 2
    block = rows // pairs
    return [
        pltpu.VMEM((rows, side), BF),
        pltpu.VMEM((rows, side), BF),
        pltpu.VMEM((pairs, block, side), BF),
        pltpu.SemaphoreType.DMA((5, pairs)),
        pltpu.SemaphoreType.DMA((4, pairs)),
    ]


def plane_sum(count, p, x, o, scratch):
    from_mate, paired, slots, ssem, rsem = scratch
    pairs = count // 2
    side = from_mate.shape[1]
    block = slots.shape[1]
    pair = p // 2
    core = p % 2
    mate = {"dp": p + 1 - 2 * core}

    def rows_of(index):
        return pl.ds(pl.multiple_of(index * block, block), block)

    def cols_of(which):
        return pl.ds(pl.multiple_of(which * side, side), side)

    def after(k):
        return (pair + k) % pairs

    def before(k):
        return (pair + pairs - k) % pairs

    def give(k):
        spot = rows_of(after(k))
        return remote(
            x.at[spot, cols_of(1 - core)], from_mate.at[spot], ssem.at[0, k % pairs], rsem.at[0, k % pairs], mate
        )

    def hand(k):
        spot = rows_of(after(k))
        return remote(
            paired.at[spot], slots.at[k], ssem.at[1, k], rsem.at[1, k], {"dp": 2 * after(k) + core}
        )

    def spread(k):
        spot = o.at[rows_of(pair), cols_of(core)]
        return remote(spot, spot, ssem.at[2, k], rsem.at[2, k], {"dp": 2 * after(k) + core})

    def share(k):
        spot = o.at[rows_of(before(k)), cols_of(core)]
        return remote(spot, spot, ssem.at[3, k], rsem.at[3, k], mate)

    def start():
        for k in range(1, pairs + 1):
            give(k).start()

    def pair_up():
        for k in range(1, pairs + 1):
            spot = rows_of(after(k))
            give(k).wait_recv()
            total = x[spot, cols_of(core)].astype(F32) + from_mate[spot].astype(F32)
            paired[spot] = total.astype(BF)
            if k < pairs:
                hand(k).start()

    def settle():
        spot = rows_of(pair)
        total = paired[spot].astype(F32)
        for k in range(1, pairs):
            hand(k).wait_recv()
            total = total + slots[k].astype(F32)
        o[spot, cols_of(core)] = total.astype(BF)
        for k in range(1, pairs):
            spread(k).start()
        share(0).start()

    def pass_on():
        for k in range(1, pairs):
            spot = o.at[rows_of(before(k)), cols_of(core)]
            remote(spot, spot, ssem.at[2, k], rsem.at[2, k], mate).wait_recv()
            share(k).start()

    def finish():
        for k in range(pairs):
            spot = o.at[rows_of(before(k)), cols_of(1 - core)]
            remote(spot, spot, ssem.at[3, k], rsem.at[3, k], mate).wait_recv()
        for k in range(1, pairs + 1):
            give(k).wait_send()
        for k in range(1, pairs):
            hand(k).wait_send()
            spread(k).wait_send()
        for k in range(pairs):
            share(k).wait_send()

    return [start, pair_up, settle, pass_on, finish]


def reduce_scratch(rows, width):
    side = width // 2
    return [
        pltpu.VMEM((rows, side), BF),
        pltpu.VMEM((rows, side), BF),
        pltpu.VMEM((2 * rows, side), BF),
        pltpu.SemaphoreType.DMA((2, 8)),
        pltpu.SemaphoreType.DMA((2, 8)),
    ]


def square_reduce(p, x, kept, matrices, scratch):
    from_mate, paired, taken, ssem, rsem = scratch
    side = from_mate.shape[1]
    pair = p // 2
    core = p % 2
    mate = {"dp": p + 1 - 2 * core}

    def away_from(place, away):
        return {"dp": 2 * (place ^ away) + core}

    def cols_of(which):
        return pl.ds(pl.multiple_of(which * side, side), side)

    def give(m):
        _, first, rows = matrices[m]
        spot = pl.ds(first, rows)
        return remote(x.at[spot, cols_of(1 - core)], from_mate.at[spot], ssem.at[m, 0], rsem.at[m, 0], mate)

    def part_of(m, part):
        _, first, rows = matrices[m]
        return pl.ds(first + part * (rows // 2), rows // 2)

    def slot(m, near, part):
        _, first, rows = matrices[m]
        return pl.ds(2 * first + near * rows + part * (rows // 2), rows // 2)

    def opposite_send(m, part):
        place = matrices[m][0]
        return remote(
            paired.at[part_of(m, part)], taken.at[slot(m, 0, part)],
            ssem.at[m, 1 + part], rsem.at[m, 1], away_from(place, 1 + part),
        )

    def near_raw(m, near):
        part = 1 - near
        return remote(
            paired.at[part_of(m, part)], taken.at[slot(m, near, part)],
            ssem.at[m, 1], rsem.at[m, 2 + 2 * near], away_from(matrices[m][0], 0),
        )

    def near_mixed(m, near):
        part = near
        return remote(
            paired.at[part_of(m, part)], taken.at[slot(m, near, part)],
            ssem.at[m, 2], rsem.at[m, 3 + 2 * near], away_from(matrices[m][0], 0),
        )

    def swap(m):
        spot = kept.at[pl.ds(0, matrices[m][2]), cols_of(core)]
        return remote(spot, spot, ssem.at[m, 6], rsem.at[m, 6], mate)

    def arrived(ref, m, index):
        remote(ref, ref, ssem.at[m, 0], rsem.at[m, index], mate).wait_recv()

    def role(m, away):
        return pl.when(pair == (matrices[m][0] ^ away))

    every = range(len(matrices))

    def start():
        for m in every:
            give(m).start()

    def pair_up():
        for m in every:
            _, first, rows = matrices[m]
            spot = pl.ds(first, rows)
            give(m).wait_recv()
            total = x[spot, cols_of(core)].astype(F32) + from_mate[spot].astype(F32)
            paired[spot] = total.astype(BF)

            @role(m, 3)
            def _(m=m):
                for part in range(2):
                    opposite_send(m, part).start()

            for near in range(2):

                @role(m, 1 + near)
                def _(m=m, near=near):
                    near_raw(m, near).start()

    def mix():
        for m in every:
            for near in range(2):

                @role(m, 1 + near)
                def _(m=m, near=near):
                    piece = slot(m, 0, near)
                    arrived(taken.at[piece], m, 1)
                    spot = part_of(m, near)
                    total = paired[spot].astype(F32) + taken[piece].astype(F32)
                    paired[spot] = total.astype(BF)
                    near_mixed(m, near).start()

    def settle():
        for m in every:

            @role(m, 0)
            def _(m=m):
                _, first, rows = matrices[m]
                for near in range(2):
                    arrived(taken.at[slot(m, near, 1 - near)], m, 2 + 2 * near)
                    arrived(taken.at[slot(m, near, near)], m, 3 + 2 * near)
                spot = pl.ds(first, rows)
                total = x[spot, cols_of(core)].astype(F32) + from_mate[spot].astype(F32)
                for near in range(2):
                    total = total + taken[pl.ds(2 * first + near * rows, rows)].astype(F32)
                kept[pl.ds(0, rows), cols_of(core)] = total.astype(BF)
                swap(m).start()

    def finish():
        for m in every:
            rows = matrices[m][2]
            give(m).wait_send()

            @role(m, 0)
            def _(m=m, rows=rows):
                arrived(kept.at[pl.ds(0, rows), cols_of(1 - core)], m, 6)
                swap(m).wait_send()

            @role(m, 3)
            def _(m=m):
                for part in range(2):
                    opposite_send(m, part).wait_send()

            for near in range(2):

                @role(m, 1 + near)
                def _(m=m, near=near):
                    near_raw(m, near).wait_send()
                    near_mixed(m, near).wait_send()

    return [start, pair_up, mix, settle, finish]


def gather_scratch():
    return [pltpu.SemaphoreType.DMA((4, 2, 4))] * 2


def square_gather(p, sizes, out, own, scratch):
    ssem, rsem = scratch
    width = out.shape[1]
    pair = p // 2
    core = p % 2
    mate = {"dp": p + 1 - 2 * core}
    firsts = [sum(sizes[:index]) for index in range(4)]

    def piece(index, side, part):
        rows = sizes[index]
        if index == 2:
            across = pl.ds(pl.multiple_of(side * (width // 2), width // 2), width // 2)
            return out.at[pl.ds(firsts[index] + part * (rows // 2), rows // 2), across]
        quarter = rows // 4
        first = firsts[index] + side * 2 * quarter + part * quarter
        return out.at[pl.ds(pl.multiple_of(first, quarter), quarter)]

    def copy(index, part, route, device):
        spot = piece(index, core, part)
        return remote(spot, spot, ssem.at[index, part, route], rsem.at[index, part, route], device)

    def other(away):
        return {"dp": 2 * (pair + away * (1 - 2 * ((pair // away) % 2))) + core}

    def role(index, away):
        return pl.when(pair == (PLACE[index] ^ away))

    def wait_in(index, part, route, side):
        spot = piece(index, side, part)
        remote(spot, spot, ssem.at[index, part, route], rsem.at[index, part, route], mate).wait_recv()

    ways = ((1, 0, 2), (2, 1, 1))

    def start():
        for index in range(4):

            @role(index, 0)
            def _(index=index):
                for part in range(2):
                    piece(index, core, part)[...] = own(index, part)
                for part in range(2):
                    copy(index, part, 0, other(1)).start()
                    copy(index, 1 - part, 1, other(2)).start()
                for part in range(2):
                    copy(index, part, 3, mate).start()

    def pass_on():
        for index in range(4):
            for away, route, onward in ways:

                @role(index, away)
                def _(index=index, away=away, route=route, onward=onward):
                    wait_in(index, away - 1, route, core)
                    copy(index, away - 1, 2, other(onward)).start()
                    copy(index, away - 1, 3, mate).start()

    def rest():
        for index in range(4):
            for away, route, _ in ways:

                @role(index, away)
                def _(index=index, away=away, route=route):
                    wait_in(index, 2 - away, route, core)
                    copy(index, 2 - away, 3, mate).start()

            @role(index, 3)
            def _(index=index):
                for part in range(2):
                    wait_in(index, part, 2, core)
                    copy(index, part, 3, mate).start()

    def finish():
        for index in range(4):
            for part in range(2):
                wait_in(index, part, 3, 1 - core)
                copy(index, part, 3, mate).wait_send()

            @role(index, 0)
            def _(index=index):
                for part in range(2):
                    copy(index, part, 0, other(1)).wait_send()
                    copy(index, part, 1, other(2)).wait_send()

            for away, _, onward in ways:

                @role(index, away)
                def _(index=index, away=away, onward=onward):
                    copy(index, away - 1, 2, other(onward)).wait_send()

    return [start, pass_on, rest, finish]


def vector_scratch(count, shape):
    return [
        pltpu.VMEM((count,) + shape, F32),
        pltpu.SemaphoreType.DMA((count,)),
        pltpu.SemaphoreType.DMA((count,)),
    ]


def vector_sum(axis, count, p, v, o, scratch):
    slots, ssem, rsem = scratch

    def send(k):
        return remote(v, slots.at[p], ssem.at[k], rsem.at[k], {axis: (p + k) % count})

    def start():
        slots[p] = v[...]
        for k in range(1, count):
            send(k).start()

    def finish():
        for k in range(1, count):
            spot = slots.at[(p + count - k) % count]
            remote(v, spot, ssem.at[k], rsem.at[k], {axis: (p + k) % count}).wait_recv()
        total = slots[0]
        for k in range(1, count):
            total = total + slots[k]
        o[...] = total
        for k in range(1, count):
            send(k).wait_send()

    return [start, finish]


ROW_STEP = 32


def tdot(left, right):
    return lax.dot_general(left, right, (((0,), (0,)), ((), ())), preferred_element_type=F32)


def dot(left, right):
    return jnp.dot(left, right, preferred_element_type=F32)


def dot_t(left, right):
    return lax.dot_general(left, right, (((1,), (1,)), ((), ())), preferred_element_type=F32)


def layer_kernel(
    count,
    seg, rp, hb, fb, mh, mf, x_hbm, cot_hbm, wq_hbm, wo_hbm, wu_hbm, wd_hbm,
    y, dz1, bt, grads, vec, squares,
    x, cot, wq_f, wo_f, wu_f, wd_f, wq, wo, wu, wd,
    q_s, k_s, v_s, ctx_s, p_s, n1_s, inv1_s, h1l_s, u_s, act_s, slope_s, dz2_s, dm_s, du_s, da_s,
    dq_s, dk_s, dv_s, part_s, red_s, gap, gbp, vecp, wsem, *scratch,
):
    p = lax.axis_index("dp")
    t = lax.axis_index("tensor")
    tokens, width = x.shape
    half = tokens // 2
    columns = q_s.shape[1]
    heads = columns // HD
    scale = 1.0 / math.sqrt(HD)
    loads = [
        pltpu.make_async_copy(source, target, wsem.at[i])
        for i, (source, target) in enumerate(
            (
                (wq_hbm, wq_f), (wo_hbm, wo_f), (wu_hbm, wu_f), (wd_hbm, wd_f),
                (x_hbm, x), (cot_hbm, cot),
            )
        )
    ]
    for place in (0, 4, 1, 2, 3, 5):
        loads[place].start()
    greet(z_peers(t) + [{"dp": (p + k) % count} for k in range(1, count)])
    quarter = tokens // 4
    sums = []
    for q in range(4):
        place = pl.ds(q * quarter, quarter)
        sums.append(
            relay_sum(t, part_s.at[place], red_s.at[place], scratch[5 * q : 5 * q + 5])
        )
    scratch = scratch[20:]
    top = 4 * columns
    if count == 8:
        ends = [(PLACE[2], 0, width), (PLACE[3], width, width)]
        plane_b = square_reduce(p, gbp, grads, ends, scratch[0:5])
        ends = [(PLACE[0], 0, 3 * columns), (PLACE[1], 3 * columns, columns)]
        plane_a = square_reduce(p, gap, grads, ends, scratch[5:10])
    else:
        plane_b = plane_sum(count, p, gbp, grads.at[pl.ds(top, 2 * width)], scratch[0:5])
        plane_a = plane_sum(count, p, gap, grads.at[pl.ds(0, top)], scratch[5:10])
    vector = vector_sum("dp", count, p, vecp, vec, scratch[10:13])
    vecp[...] = jnp.zeros_like(vecp)
    lane = lax.broadcasted_iota(jnp.int32, (1, columns), 1)

    def in_head(index):
        return (lane // HD) == index

    def rows_of(h):
        return pl.ds(h * half, half)

    def quarter_of(q):
        return pl.ds(q * quarter, quarter)

    def over_rows(q, body, init=0):
        def step(i, carry):
            first = q * quarter + i * ROW_STEP
            return body(pl.ds(pl.multiple_of(first, ROW_STEP), ROW_STEP), carry)

        return lax.fori_loop(0, quarter // ROW_STEP, step, init)

    def fold(values):
        return values.reshape(ROW_STEP // 8, 8, values.shape[1]).sum(axis=0)

    def add_vec(row, folded):
        vecp[row : row + 1, 0 : folded.shape[1]] += jnp.sum(folded, axis=0, keepdims=True)

    def narrow(index, source, target):
        loads[index].wait()
        if len(source.shape) == 3:
            for i in range(source.shape[0]):
                target[i] = source[i].astype(BF)
        else:
            target[...] = source[...].astype(BF)

    def attention(h):
        r = rows_of(h)
        xb = x[r]
        q = (dot_t(xb, wq[0]) + hb[0:1]).astype(BF)
        k = dot_t(xb, wq[1]).astype(BF)
        v = (dot_t(xb, wq[2]) + hb[1:2]).astype(BF)
        q_s[r], k_s[r], v_s[r] = q, k, v
        down = jnp.broadcast_to(seg[h : h + 1].astype(F32), (half, half))
        same = down == down.T
        context = jnp.zeros((half, columns), F32)
        for index in range(heads):
            mine = jnp.where(in_head(index), q, jnp.zeros_like(q))
            scores = jnp.where(same, dot_t(mine, k) * scale, -1e30)
            expo = jnp.exp(scores - jnp.max(scores, axis=-1, keepdims=True))
            probs = expo / jnp.sum(expo, axis=-1, keepdims=True)
            p_s[h * heads + index] = probs
            context = jnp.where(in_head(index), dot(probs.astype(BF), v), context)
        low = context.astype(BF)
        ctx_s[r] = low
        part_s[r] = dot(low, wo[...]).astype(BF)

    def up(q):
        def norm(r, carry):
            z = x[r].astype(F32) + red_s[r].astype(F32) + rp[0:1]
            center = z - jnp.mean(z, axis=-1, keepdims=True)
            inverse = lax.rsqrt(jnp.mean(center * center, axis=-1, keepdims=True) + EPS_NORM)
            normed = center * inverse
            n1_s[r] = normed
            inv1_s[r] = jnp.broadcast_to(inverse, (ROW_STEP, 128))
            h1l_s[r] = (normed * rp[2:3] + rp[3:4]).astype(BF)
            return carry

        over_rows(q, norm)
        u_s[quarter_of(q)] = dot(h1l_s[quarter_of(q)], wu[...])

        def gelu(r, carry):
            u = u_s[r] + fb[...].reshape(1, width)
            cdf = 0.5 * (1.0 + lax.erf(u * (1.0 / math.sqrt(2.0))))
            act_s[r] = (u * cdf).astype(BF)
            slope_s[r] = cdf + u * jnp.exp(-0.5 * u * u) * (1.0 / math.sqrt(2.0 * math.pi))
            return carry

        over_rows(q, gelu)

    def down(q):
        r = quarter_of(q)
        part_s[r] = dot(act_s[r], wd[...]).astype(BF)

    def out_back(q):
        def norm(r, carry):
            s_dz2, s_dyn, s_dy = carry
            h1 = n1_s[r] * rp[2:3] + rp[3:4]
            z = h1 + red_s[r].astype(F32) + rp[1:2]
            center = z - jnp.mean(z, axis=-1, keepdims=True)
            inverse = lax.rsqrt(jnp.mean(center * center, axis=-1, keepdims=True) + EPS_NORM)
            normed = center * inverse
            y[r] = (normed * rp[4:5] + rp[5:6]).astype(BF)
            dy = cot[r].astype(F32)
            scaled = dy * rp[4:5]
            first = jnp.mean(scaled, axis=-1, keepdims=True)
            second = jnp.mean(scaled * normed, axis=-1, keepdims=True)
            dz2 = inverse * (scaled - first - normed * second)
            dz2_s[r] = dz2
            dm_s[r] = dz2.astype(BF)
            return s_dz2 + fold(dz2), s_dyn + fold(dy * normed), s_dy + fold(dy)

        zero = jnp.zeros((8, width), F32)
        for row, total in zip((1, 4, 5), over_rows(q, norm, (zero, zero, zero))):
            add_vec(row, total)
        u_s[quarter_of(q)] = dot_t(dm_s[quarter_of(q)], wd[...])

        def slope(r, carry):
            du = (u_s[r] * slope_s[r]).astype(BF)
            du_s[r] = du
            return carry + fold(du.astype(F32))

        add_vec(6, over_rows(q, slope, zero))

    def up_back(q):
        r = quarter_of(q)
        part_s[r] = dot_t(du_s[r], wu[...]).astype(BF)

    def grads_b():
        gbp[0:width] = tdot(h1l_s[...], du_s[...]).astype(BF)
        gbp[width : 2 * width] = tdot(act_s[...], dm_s[...]).astype(BF)

    def norm_back(q):
        def norm(r, carry):
            s_dz1, s_dhn, s_dh = carry
            dh1 = red_s[r].astype(F32) + dz2_s[r]
            normed = n1_s[r]
            scaled = dh1 * rp[2:3]
            first = jnp.mean(scaled, axis=-1, keepdims=True)
            second = jnp.mean(scaled * normed, axis=-1, keepdims=True)
            grad = inv1_s[r][:, 0:1] * (scaled - first - normed * second)
            dz1[r] = grad
            da_s[r] = grad.astype(BF)
            return s_dz1 + fold(grad), s_dhn + fold(dh1 * normed), s_dh + fold(dh1)

        zero = jnp.zeros((8, width), F32)
        for row, total in zip((0, 2, 3), over_rows(q, norm, (zero, zero, zero))):
            add_vec(row, total)

    def attention_back(h):
        r = rows_of(h)
        dc = dot_t(da_s[r], wo[...]).astype(BF)
        q, k, v = q_s[r], k_s[r], v_s[r]
        dq = dk = dv = jnp.zeros((half, columns), F32)
        for index in range(heads):
            probs = p_s[h * heads + index]
            mine = jnp.where(in_head(index), dc, jnp.zeros_like(dc))
            dp = dot_t(mine, v)
            ds = (probs * (dp - jnp.sum(probs * dp, axis=-1, keepdims=True))).astype(BF)
            dv = jnp.where(in_head(index), tdot(probs.astype(BF), dc), dv)
            dq = jnp.where(in_head(index), dot(ds, k), dq)
            dk = jnp.where(in_head(index), tdot(ds, q), dk)
        dq = (dq * scale).astype(BF)
        dk = (dk * scale).astype(BF)
        dv = dv.astype(BF)
        dq_s[r], dk_s[r], dv_s[r] = dq, dk, dv
        add_vec(7, jnp.sum(dq.astype(F32), axis=0, keepdims=True))
        add_vec(8, jnp.sum(dv.astype(F32), axis=0, keepdims=True))

    def grads_a():
        for i, source in enumerate((dq_s, dk_s, dv_s)):
            gap[i * columns : (i + 1) * columns] = tdot(source[...], x[...]).astype(BF)
        gap[3 * columns : 4 * columns] = tdot(ctx_s[...], da_s[...]).astype(BF)

    def back_terms(h):
        r = rows_of(h)
        total = dot(dq_s[r], wq[0]) + dot(dk_s[r], wq[1]) + dot(dv_s[r], wq[2])
        bt[r] = total.astype(BF)

    start, mix, settle, pass_on, end = (
        (lambda q, place=place: sums[q][place]()) for place in range(5)
    )

    def round_trip(first, second):
        end(0), first(0), pass_on(1), second(0), settle(2), mix(3), start(0)
        end(1), first(1), pass_on(2), settle(3), second(1), mix(0), start(1)
        end(2), first(2), pass_on(3), second(2), settle(0), mix(1), start(2)
        end(3), first(3), pass_on(0), second(3), settle(1), mix(2), start(3)

    loads[4].wait()
    narrow(0, wq_f, wq)
    narrow(1, wo_f, wo)
    attention(0)
    start(0), start(1)
    attention(1)
    mix(0), start(2), mix(1), settle(0), start(3)
    narrow(2, wu_f, wu)
    mix(2), settle(1), pass_on(0)
    narrow(3, wd_f, wd)
    loads[5].wait()
    round_trip(up, down)
    round_trip(out_back, up_back)
    grads_b()
    plane_b[0]()
    end(0), norm_back(0), pass_on(1), settle(2), mix(3)
    plane_b[1]()
    end(1), norm_back(1), pass_on(2), settle(3)
    attention_back(0)
    end(2), norm_back(2), pass_on(3)
    if count == 8:
        plane_b[2]()
    end(3), norm_back(3)
    attention_back(1)
    grads_a()
    plane_a[0]()
    vector[0]()
    if count != 8:
        plane_b[2]()
    plane_a[1]()
    back_terms(0)
    back_terms(1)
    plane_b[3]()
    plane_a[2]()
    vector[1]()
    moved = 0.5 * mh[...] + vec[7:9, 0:columns]
    squares[0:2] = jnp.broadcast_to(jnp.sum(moved * moved, axis=1, keepdims=True), (2, 128))
    moved = 0.5 * mf[...].reshape(1, width) + vec[6:7]
    squares[2:3] = jnp.broadcast_to(jnp.sum(moved * moved, axis=1, keepdims=True), (1, 128))
    squares[3:8] = jnp.zeros((5, 128), F32)
    plane_a[3]()
    plane_b[4]()
    plane_a[4]()


def layer(count, tokens, cotangent, segments, small, weights, collective_id):
    rows, width = tokens.shape
    w_qkv, w_out, w_up, w_down = weights
    columns = w_qkv.shape[1]
    heads = columns // HD
    half = rows // 2
    grads = width if count == 8 else 4 * columns + 2 * width

    def low(*shape):
        return pltpu.VMEM(shape, BF)

    def full(*shape):
        return pltpu.VMEM(shape, F32)

    def out(shape, dtype):
        return jax.ShapeDtypeStruct(shape, dtype)

    scratch = (
        [low(rows, width)] * 2
        + [full(*weight.shape) for weight in weights]
        + [low(*weight.shape) for weight in weights]
        + [low(rows, columns)] * 4
        + [full(2 * heads, half, half), full(rows, width), full(rows, 128), low(rows, width)]
        + [full(rows, width), low(rows, width), full(rows, width), full(rows, width)]
        + [low(rows, width)] * 3
        + [low(rows, columns)] * 3
        + [low(rows, width)] * 2
        + [low(4 * columns, width), low(2 * width, width), full(16, width)]
        + [pltpu.SemaphoreType.DMA((6,))]
        + relay_scratch(rows // 4, width, BF) * 4
        + (reduce_scratch(2 * width, width) if count == 8 else plane_scratch(count, 2 * width, width))
        + (
            reduce_scratch(4 * columns, width)
            if count == 8
            else plane_scratch(count, 4 * columns, width)
        )
        + vector_scratch(count, (16, width))
    )
    return pl.pallas_call(
        functools.partial(layer_kernel, count),
        out_shape=(
            out((rows, width), BF),
            out((rows, width), F32),
            out((rows, width), BF),
            out((grads, width), BF),
            out((16, width), F32),
            out((8, 128), F32),
        ),
        in_specs=[IN_VMEM] * 6 + [IN_HBM] * 6,
        out_specs=(IN_VMEM,) * 6,
        scratch_shapes=scratch,
        compiler_params=params(collective_id, 56),
        name="layer",
    )(segments, *small, tokens, cotangent, *weights)


def cut(values):
    high = values.astype(BF)
    return high, (values - high.astype(F32)).astype(BF)


def dot3(lh, ll, rh, rl, dims=(((1,), (0,)), ((), ()))):
    def dot(left, right):
        return lax.dot_general(left, right, dims, preferred_element_type=F32)

    return dot(lh, rh) + (dot(lh, rl) + dot(ll, rh))


def muon_kernel(
    count, sizes,
    mq, mo, mu, md, grads, vs, bx, dz1,
    xo, gall, vt, bo,
    zf, gf, zh, zl, gx, go, gp, af, ah, al, dh, dl, sf, sh, sl, xf, bs, lsem, psem, *scratch,
):
    p = lax.axis_index("dp")
    t = lax.axis_index("tensor")
    width = zf.shape[1]
    group = count // 4
    which = p // group
    core = p % 2
    mate = {"dp": p + 1 - 2 * core}
    share = xf.shape[0]
    tile = width // 3
    greet(z_peers(t) + [{"dp": (p + k) % count} for k in range(1, count)])
    vector = vector_sum("tensor", 4, t, vs, vt, scratch[12:15])
    back = line_sum(t, bx, bs, scratch[6:12])
    vector[0]()
    firsts = [sum(sizes[:index]) for index in range(4)]
    for index, moment in enumerate((mq, mo, mu, md)):
        rows = sizes[index]
        first = 0 if count == 8 else firsts[index]

        @pl.when(which == PLACE[index])
        def _(index=index, moment=moment, first=first, rows=rows):
            one = pltpu.make_async_copy(moment, sf.at[pl.ds(0, rows)], lsem.at[0])
            two = pltpu.make_async_copy(
                grads.at[pl.ds(first, rows)], gf.at[pl.ds(0, rows)], lsem.at[1]
            )
            one.start()
            two.start()
            one.wait()
            two.wait()
            for i in range(3):
                spot = pl.ds(i * (rows // 3), rows // 3)
                z = 0.5 * sf[spot] + gf[spot].astype(F32)
                if index == 2:
                    z = z.T
                    spot = (pl.ds(0, width), spot)
                zf[spot] = z
                zh[spot], zl[spot] = cut(z)
            if rows < width:
                spot = pl.ds(rows, width - rows)
                zf[spot] = jnp.zeros((width - rows, width), F32)
                zh[spot] = jnp.zeros((width - rows, width), BF)
                zl[spot] = jnp.zeros((width - rows, width), BF)

    if count == 8:

        def own_gradient(index, part):
            if index == 2:
                across = pl.ds(pl.multiple_of(core * (width // 2), width // 2), width // 2)
                return gf[pl.ds(part * (width // 2), width // 2), across]
            quarter = sizes[index] // 4
            first = pl.multiple_of((2 * core + part) * quarter, quarter)
            return gf[pl.ds(first, quarter)]

        def own_step(index, part):
            if index == 2:
                return xf[:, pl.ds(part * (width // 2), width // 2)].T.astype(BF)
            quarter = sizes[index] // 4
            return xf[pl.ds(part * quarter, quarter)].astype(BF)

        spread = square_gather(p, sizes, gall, own_gradient, scratch[15:17])
        spread[0]()

    def cols(index):
        return pl.ds(pl.multiple_of(index * tile, tile), tile)

    over_rows = (((0,), (0,)), ((), ()))
    for j, (row, col) in enumerate(((core, core), (core, core + 1), (2 * core, 2))):
        gx[:, pl.ds(j * tile, tile)] = dot3(
            zh[:, cols(row)], zl[:, cols(row)], zh[:, cols(col)], zl[:, cols(col)], over_rows
        )
    for step in line_sum(t, gx, go, scratch[:6]):
        step()
    swap = remote(go, gp, psem.at[0], psem.at[1], mate)
    swap.start()
    back[0]()
    swap.wait()
    diagonal = lax.broadcasted_iota(jnp.int32, (tile, tile), 0) == lax.broadcasted_iota(
        jnp.int32, (tile, tile), 1
    )

    def upper(first, second):
        trace = jnp.float32(0.0)
        for block in (first[:, 0:tile], second[:, 0:tile], second[:, 2 * tile :]):
            trace = trace + jnp.sum(jnp.where(diagonal, block, 0.0))
        inverse = 1.0 / (jnp.sqrt(jnp.full((1, 1), trace, F32)) + 1e-07)
        scale = inverse * inverse
        blocks = (
            (0, 0, first, 0), (0, 1, first, 1), (0, 2, first, 2),
            (1, 1, second, 0), (1, 2, second, 1), (2, 2, second, 2),
        )
        for row, col, source, j in blocks:
            block = source[:, j * tile : (j + 1) * tile] * scale
            for r, c, value in ((row, col, block),) + (((col, row, block.T),) if row != col else ()):
                spot = (pl.ds(r * tile, tile), pl.ds(c * tile, tile))
                af[spot] = value
                ah[spot], al[spot] = cut(value)
        if group == 2:
            for index, rows in enumerate(sizes):

                @pl.when(which == PLACE[index])
                def _(half=rows // 2):
                    xf[0:half] = zf[pl.ds(pl.multiple_of(core * half, half), half)] * inverse
                    if half < share:
                        xf[half:share] = jnp.zeros((share - half, width), F32)

        else:
            rank = p % group
            xf[...] = zf[pl.ds(pl.multiple_of(rank * share, share), share)] * inverse

    @pl.when(core == 0)
    def _():
        upper(go, gp)

    @pl.when(core == 1)
    def _():
        upper(gp, go)

    vector[1]()

    def product(left, right, base, base_scale, scale, targets):
        (lh, ll), (rh, rl) = left, right
        for i in range(3):
            rows = pl.ds(i * tile, tile)
            for j in range(i, 3):
                columns = pl.ds(j * tile, tile)
                value = base_scale * base[rows, columns] + scale * dot3(
                    lh[rows], ll[rows], rh[:, columns], rl[:, columns]
                )
                for target, part in zip(targets, (*cut(value), value)):
                    target[rows, columns] = part
                    if i != j:
                        target[columns, rows] = part.T

    def make_d():
        product((ah, al), (ah, al), af, coef_b, coef_c, (dh, dl))

    def move_x():
        xh, xl = cut(xf[...])
        xf[...] = coef_a * xf[...] + dot3(xh, xl, dh[...], dl[...])

    def sweep(k, carry):
        make_d()
        move_x()
        product((ah, al), (dh, dl), af, coef_a, 1.0, (sh, sl, sf))
        product((sh, sl), (dh, dl), sf, coef_a, 1.0, (ah, al, af))
        for i in range(1, 4):
            pl.when(k == i - 1)(back[i])
            if count == 8 and i < 3:
                pl.when(k == i - 1)(spread[i])
        return carry

    lax.fori_loop(0, 4, sweep, 0)
    make_d()
    move_x()
    back[4]()
    bo[...] = (bs[...].astype(F32) + dz1[...]).astype(BF)
    if count == 8:
        spread[3]()
        for step in square_gather(p, sizes, xo, own_step, scratch[17:19]):
            step()
    else:
        gall[...] = jnp.zeros_like(gall)
        gather_any(p, core, count // 2, mate, xf, xo, scratch[15], scratch[16])


def gather_any(p, core, pairs, mate, xf, xo, asem_s, asem_r):
    pair = p // 2
    share = xf.shape[0]

    def rows_of(device):
        return xo.at[pl.ds(pl.multiple_of(device * share, share), share)]

    def after(k):
        return 2 * ((pair + k) % pairs) + core

    def before(k):
        return 2 * ((pair + pairs - k) % pairs) + core

    def send(k):
        return remote(rows_of(p), rows_of(p), asem_s.at[0, k], asem_r.at[0, k], {"dp": after(k)})

    def hand(k):
        spot = rows_of(before(k))
        return remote(spot, spot, asem_s.at[1, k], asem_r.at[1, k], mate)

    xo[pl.ds(pl.multiple_of(p * share, share), share)] = xf[...].astype(BF)
    for k in range(1, pairs):
        send(k).start()
    hand(0).start()
    for k in range(1, pairs):
        spot = rows_of(before(k))
        remote(spot, spot, asem_s.at[0, k], asem_r.at[0, k], mate).wait_recv()
        hand(k).start()
    for k in range(pairs):
        spot = rows_of(before(k) + 1 - 2 * core)
        remote(spot, spot, asem_s.at[1, k], asem_r.at[1, k], mate).wait_recv()
    for k in range(1, pairs):
        send(k).wait_send()
    for k in range(pairs):
        hand(k).wait_send()


def muon(count, moments, grads, squares, back, grad_first, collective_id):
    width = grads.shape[1]
    tile = width // 3
    share = width // (count // 4)
    sizes = tuple(moment.shape[0] for moment in moments)
    square = count == 8

    def vmem(dtype, rows=width, columns=width):
        return pltpu.VMEM((rows, columns), dtype)

    def out(shape, dtype):
        return jax.ShapeDtypeStruct(shape, dtype)

    pair_sems = [pltpu.SemaphoreType.DMA((2, count // 2))] * 2
    scratch = (
        [vmem(F32), vmem(BF), vmem(BF), vmem(BF)]
        + [vmem(F32, tile)] * 3
        + [vmem(F32), vmem(BF), vmem(BF), vmem(BF), vmem(BF), vmem(F32), vmem(BF), vmem(BF)]
        + [vmem(F32, share), vmem(BF, back.shape[0])]
        + [pltpu.SemaphoreType.DMA((2,)), pltpu.SemaphoreType.DMA((2,))]
        + line_scratch(tile, width, F32)
        + line_scratch(*back.shape, BF)
        + vector_scratch(4, squares.shape)
        + (gather_scratch() * 2 if square else pair_sems)
    )
    return pl.pallas_call(
        functools.partial(muon_kernel, count, sizes),
        out_shape=(
            out((sum(sizes) if square else 4 * width, width), BF),
            out((sum(sizes), width) if square else (16, width), BF),
            out(squares.shape, F32),
            out(back.shape, BF),
        ),
        in_specs=[IN_HBM] * 5 + [IN_VMEM] * 3,
        out_specs=(IN_VMEM,) * 4,
        scratch_shapes=scratch,
        compiler_params=params(collective_id, 44),
        name="muon",
    )(*moments, grads, squares, back, grad_first)


def apply_kernel(factors, *refs):
    ins, outs = refs[:26], refs[26:]
    small_in, small_out = ins[18:], outs[14:]
    for index, factor in enumerate(factors):
        weight, moment, grad, step = (ins[4 * index + i] for i in range(4))
        new_moment, new, low = (outs[3 * index + i] for i in range(3))
        new_moment[...] = 0.5 * moment[...] + grad[...].astype(F32)
        value = weight[...] - factor * step[...].astype(F32)
        new[...] = value
        low[...] = value.astype(BF)
    for source, target in zip(ins[16:18], outs[12:14]):
        target[...] = source[...]

    @pl.when(pl.program_id(0) == 0)
    def _():
        vec, totals, heads, ff, rows, mom_heads, mom_ff, mom_rows = small_in
        columns = heads.shape[1]
        wide = ff.shape[0]
        moment = 0.5 * mom_heads[...] + vec[7:9, 0:columns]
        small_out[0][...] = moment
        scale = lax.rsqrt(totals[0:2, 0:1] * (1.0 / (4 * columns)) + 1e-06)
        small_out[1][...] = heads[...] - 0.1 * moment * scale
        moment = 0.5 * mom_ff[...].reshape(1, wide) + vec[6:7]
        small_out[2][...] = moment.reshape(wide)
        scale = lax.rsqrt(totals[2:3, 0:1] * (1.0 / (4 * wide)) + 1e-06)
        value = ff[...].reshape(1, wide) - 0.1 * moment * scale
        small_out[3][...] = value.reshape(wide)
        moment = 0.5 * mom_rows[...] + vec[0:6]
        small_out[4][...] = moment
        mean = jnp.mean(moment * moment, axis=-1, keepdims=True)
        small_out[5][...] = rows[...] - 0.1 * moment * lax.rsqrt(mean + 1e-06)


APPLY_STEPS = 4


def apply(sizes, factors, weights, moments, grads, steps, passed, small):
    width = grads.shape[1]
    in_specs, operands, out_specs, out_shape = [], [], [], []

    def block(rows, first=0):
        share = rows // APPLY_STEPS
        return pl.BlockSpec((share, width), lambda i, skip=first // share: (skip + i, 0))

    def whole(array):
        return pl.BlockSpec(array.shape, lambda i, n=array.ndim: (0,) * n)

    first = 0
    for rows, weight, moment in zip(sizes, weights, moments):
        in_specs += [block(rows), block(rows), block(rows, first), block(rows, first)]
        operands += [weight, moment, grads, steps]
        out_specs += [block(rows)] * 3
        out_shape += [jax.ShapeDtypeStruct((rows, width), kind) for kind in (F32, F32, BF)]
        first += rows
    for array in passed:
        in_specs.append(block(array.shape[0]))
        operands.append(array)
        out_specs.append(block(array.shape[0]))
        out_shape.append(jax.ShapeDtypeStruct(array.shape, array.dtype))
    for array in small:
        in_specs.append(whole(array))
        operands.append(array)
    for array in small[2:5]:
        for _ in range(2):
            out_specs.append(whole(array))
            out_shape.append(jax.ShapeDtypeStruct(array.shape, F32))
    return pl.pallas_call(
        functools.partial(apply_kernel, factors),
        grid=(APPLY_STEPS,),
        out_shape=tuple(out_shape),
        in_specs=in_specs,
        out_specs=tuple(out_specs),
        compiler_params=pltpu.CompilerParams(vmem_limit_bytes=40 * 1024 * 1024),
        name="apply",
    )(*operands)


def vector_step(param, moment, mean_sq):
    return param - 0.1 * moment * lax.rsqrt(mean_sq + 1e-06)


def local(
    tokens, segments, cotangent,
    w_qkv, w_out, w_up, w_down, head_bias, ff_bias, row_params,
    mom_qkv, mom_out, mom_up, mom_down, mom_heads, mom_ff, mom_params,
):
    width = tokens.shape[1]
    columns = w_qkv.shape[2]
    ff_cols = w_up.shape[1]
    tensor_size = lax.axis_size("tensor")
    count = lax.axis_size("dp")
    qkv_rows = 3 * columns
    wq_rows = w_qkv.transpose(0, 2, 1)
    output_rows, grad_first, back_terms, grads, vector_total, squares = layer(
        count, tokens, cotangent, segments,
        (row_params, head_bias, ff_bias, mom_heads, mom_ff),
        (wq_rows, w_out, w_up, w_down), 1,
    )
    moments = (mom_qkv.transpose(0, 2, 1).reshape(qkv_rows, width), mom_out, mom_up, mom_down)
    steps, gathered, totals, grad_inputs = muon(
        count, moments, grads, squares, back_terms, grad_first, 2
    )
    wide = math.sqrt(ff_cols * tensor_size / width)
    if count == 8:
        sizes = (qkv_rows, columns, width, ff_cols)
        factors = (0.8 * math.sqrt(3.0), 0.8, 0.8 * wide, 0.8 * wide)
        done = apply(
            sizes, factors, (wq_rows.reshape(qkv_rows, width), w_out, w_up, w_down), moments,
            gathered, steps, (output_rows, grad_inputs),
            (
                vector_total, totals, head_bias, ff_bias, row_params,
                mom_heads, mom_ff, mom_params,
            ),
        )
        qkv_new = [rows.reshape(3, columns, width).transpose(0, 2, 1) for rows in done[0:3]]
        return (
            *done[12:14], *qkv_new, *done[3:12], *done[14:20],
        )

    def to_qkv(rows):
        return rows.reshape(3, columns, width).transpose(0, 2, 1)

    bounds = (0, qkv_rows, qkv_rows + columns, qkv_rows + columns + width)

    def grad_of(index, rows):
        return grads[bounds[index] : bounds[index] + rows].astype(F32)

    def step_of(index, rows):
        first = PLACE[index] * width
        part = steps[first : first + rows].astype(F32)
        return part.T if index == 2 else part

    new_mom_heads = 0.5 * mom_heads + vector_total[7:9, :columns]
    new_mom_ff = 0.5 * mom_ff + vector_total[6]
    new_mom_params = 0.5 * mom_params + vector_total[0:6]
    new_mom_qkv = 0.5 * mom_qkv + to_qkv(grad_of(0, qkv_rows))
    new_mom_out = 0.5 * mom_out + grad_of(1, columns)
    new_mom_up = 0.5 * mom_up + grad_of(2, width)
    new_mom_down = 0.5 * mom_down + grad_of(3, ff_cols)
    new_qkv = w_qkv - 0.8 * math.sqrt(3.0) * to_qkv(step_of(0, qkv_rows))
    new_out = w_out - 0.8 * step_of(1, columns)
    new_up = w_up - 0.8 * wide * step_of(2, width)
    new_down = w_down - 0.8 * wide * step_of(3, ff_cols)
    new_heads = vector_step(head_bias, new_mom_heads, totals[0:2, 0:1] / (columns * tensor_size))
    new_ff = vector_step(ff_bias, new_mom_ff, totals[2, 0] / (ff_cols * tensor_size))
    new_params = vector_step(
        row_params,
        new_mom_params,
        jnp.mean(new_mom_params * new_mom_params, axis=-1, keepdims=True),
    )
    return (
        output_rows,
        grad_inputs,
        new_mom_qkv, new_qkv, new_qkv.astype(BF),
        new_mom_out, new_out, new_out.astype(BF),
        new_mom_up, new_up, new_up.astype(BF),
        new_mom_down, new_down, new_down.astype(BF),
        new_mom_heads, new_heads,
        new_mom_ff, new_ff,
        new_mom_params, new_params,
    )


def solution(mesh):
    placed = (
        P("dp", None), P("dp", None), P("dp", None),
        P(None, None, "tensor"), P("tensor", None), P(None, "tensor"), P("tensor", None),
        P(None, "tensor"), P("tensor"), P(),
        P(None, None, "tensor"), P("tensor", None), P(None, "tensor"), P("tensor", None),
        P(None, "tensor"), P("tensor"), P(),
    )
    triple = ((P(None, None, "tensor"),) * 3, (P("tensor", None),) * 3, (P(None, "tensor"),) * 3)
    return jax.shard_map(
        local,
        mesh=mesh,
        in_specs=placed,
        out_specs=(
            (P("dp", None), P("dp", None))
            + triple[0] + triple[1] + triple[2] + triple[1]
            + (P(None, "tensor"), P(None, "tensor"), P("tensor"), P("tensor"), P(), P())
        ),
        check_vma=False,
    )
```

```python
import functools
import math

import jax
import jax.numpy as jnp
from jax import lax
from jax.experimental import pallas as pl
from jax.experimental.pallas import tpu as pltpu
from jax.sharding import PartitionSpec as P

HD = 64
EPS_NORM = 1e-05
coef_a = 3.4445
coef_b = -4.775
coef_c = 2.0315
BF = jnp.bfloat16
F32 = jnp.float32
MESH = pl.DeviceIdType.MESH
SUBS = 2
PLACE = (1, 2, 0, 3)
CUTS = 3


def remote(src, dst, send_sem, recv_sem, device):
    return pltpu.make_async_remote_copy(
        src_ref=src,
        dst_ref=dst,
        send_sem=send_sem,
        recv_sem=recv_sem,
        device_id=device,
        device_id_type=MESH,
    )


def greet(devices):
    barrier = pltpu.get_barrier_semaphore()
    for device in devices:
        pl.semaphore_signal(barrier, inc=1, device_id=device, device_id_type=MESH)
    pl.semaphore_wait(barrier, len(devices))


def z_peers(t):
    return [{"tensor": (t + k) % 4} for k in range(1, 4)]


def line_scratch(rows, width, dtype):
    part = rows // 4
    return [
        pltpu.VMEM((part, width), dtype),
        pltpu.VMEM((part, width), dtype),
        pltpu.VMEM((2 * part, width), dtype),
        pltpu.VMEM((2 * part, width), dtype),
        pltpu.SemaphoreType.DMA((8 * SUBS,)),
        pltpu.SemaphoreType.DMA((8 * SUBS,)),
    ]


def line_sum(t, x, o, scratch):
    raw, cmb, fwd, mix, ssem, rsem = scratch
    part = raw.shape[0]
    half = part // SUBS
    subs = range(SUBS)
    mate = t + 1 - 2 * (t % 2)
    outer = (t % 3) == 0
    inner = (t % 3) != 0

    def at(ref, chunk, s):
        return ref.at[pl.ds(pl.multiple_of(chunk * part + s * half, half), half)]

    def to(index, src, dst, recv, device):
        return remote(src, dst, ssem.at[index], rsem.at[recv], {"tensor": device})

    def ag_sem(chunk, s):
        return (4 + chunk) * SUBS + s

    def o_far(s):
        return to(s, at(x, 3 - t, s), at(fwd, 0, s), 2 * SUBS + s, mate)

    def o_near(s):
        return to(SUBS + s, at(x, 3 - mate, s), at(fwd, 1, s), 3 * SUBS + s, mate)

    def o_raw(s):
        return to(2 * SUBS + s, at(x, mate, s), at(raw, 0, s), s, mate)

    def o_own(s):
        return to(3 * SUBS + s, at(o, t, s), at(o, t, s), ag_sem(t, s), mate)

    def i_raw(s):
        return to(s, at(x, mate, s), at(raw, 0, s), s, mate)

    def i_far(s):
        return to(SUBS + s, at(mix, 0, s), at(cmb, 0, s), SUBS + s, 3 - mate)

    def i_near(s):
        return to(2 * SUBS + s, at(mix, 1, s), at(cmb, 0, s), SUBS + s, 3 - t)

    def i_ag(place, chunk, s, device):
        return to(place * SUBS + s, at(o, chunk, s), at(o, chunk, s), ag_sem(chunk, s), device)

    def got(dst, recv):
        remote(dst, dst, ssem.at[0], rsem.at[recv], {"tensor": mate}).wait_recv()

    def add(dst, *terms):
        total = terms[0][...].astype(F32)
        for term in terms[1:]:
            total = total + term[...].astype(F32)
        dst[...] = total.astype(dst.dtype)

    def start():
        @pl.when(outer)
        def _():
            for build in (o_far, o_near, o_raw):
                for s in subs:
                    build(s).start()

        @pl.when(inner)
        def _():
            for s in subs:
                i_raw(s).start()

    def combine():
        @pl.when(inner)
        def _():
            for slot, chunk, build in ((0, 3 - mate, i_far), (1, 3 - t, i_near)):
                for s in subs:
                    got(at(fwd, slot, s), (2 + slot) * SUBS + s)
                    add(at(mix, slot, s), at(fwd, slot, s), at(x, chunk, s))
                    build(s).start()

    def settle():
        for s in subs:
            got(at(raw, 0, s), s)
            got(at(cmb, 0, s), SUBS + s)
            add(at(o, t, s), at(x, t, s), at(raw, 0, s), at(cmb, 0, s))

            @pl.when(outer)
            def _(s=s):
                o_own(s).start()

            @pl.when(inner)
            def _(s=s):
                i_ag(3, t, s, 3 - t).start()
                i_ag(4, t, s, mate).start()

    def pass_on():
        @pl.when(inner)
        def _():
            for s in subs:
                got(at(o, mate, s), ag_sem(mate, s))
                i_ag(5, mate, s, 3 - t).start()
            for s in subs:
                got(at(o, 3 - t, s), ag_sem(3 - t, s))
                i_ag(6, 3 - t, s, mate).start()
            for s in subs:
                got(at(o, 3 - mate, s), ag_sem(3 - mate, s))
                i_ag(7, 3 - mate, s, mate).start()

    def finish():
        @pl.when(outer)
        def _():
            for chunk in (mate, 3 - mate, 3 - t):
                for s in subs:
                    got(at(o, chunk, s), ag_sem(chunk, s))
            for build in (o_far, o_near, o_raw, o_own):
                for s in subs:
                    build(s).wait_send()

        @pl.when(inner)
        def _():
            for s in subs:
                for build in (i_raw, i_far, i_near):
                    build(s).wait_send()
                i_ag(3, t, s, 3 - t).wait_send()
                i_ag(4, t, s, mate).wait_send()
                i_ag(5, mate, s, 3 - t).wait_send()
                i_ag(6, 3 - t, s, mate).wait_send()
                i_ag(7, 3 - mate, s, mate).wait_send()

    return [start, combine, settle, pass_on, finish]


def relay_scratch(rows, width, dtype):
    part = rows // 2
    return [
        pltpu.VMEM((2 * part, width), dtype),
        pltpu.VMEM((part, width), dtype),
        pltpu.VMEM((part, width), dtype),
        pltpu.SemaphoreType.DMA((5 * SUBS,)),
        pltpu.SemaphoreType.DMA((5 * SUBS,)),
    ]


def relay_sum(t, x, o, scratch):
    taken, mixed, mix, ssem, rsem = scratch
    part = mixed.shape[0]
    piece = part // SUBS
    subs = range(SUBS)
    mate = t + 1 - 2 * (t % 2)
    facing = 3 - t
    outer = (t % 3) == 0
    inner = (t % 3) != 0
    near = t // 2
    far = 1 - near

    def at(ref, chunk, s):
        return ref.at[pl.ds(pl.multiple_of(chunk * part + s * piece, piece), piece)]

    def to(index, src, dst, recv, device):
        return remote(
            src, dst, ssem.at[index], rsem.at[recv], {"tensor": device}
        )

    def give_far(s):
        return to(s, at(x, far, s), at(taken, 0, s), s, mate)

    def give_near(s):
        return to(SUBS + s, at(x, near, s), at(taken, 1, s), SUBS + s, mate)

    def cross(s):
        return to(s, at(mix, 0, s), at(mixed, 0, s), 2 * SUBS + s, facing)

    def own_across(s):
        return to(SUBS + s, at(o, near, s), at(o, near, s), (3 + near) * SUBS + s, facing)

    def own_out(s):
        return to(2 * SUBS + s, at(o, near, s), at(o, near, s), (3 + near) * SUBS + s, mate)

    def far_out(s):
        return to(3 * SUBS + s, at(o, far, s), at(o, far, s), (3 + far) * SUBS + s, mate)

    def got(dst, recv):
        remote(dst, dst, ssem.at[0], rsem.at[recv], {"tensor": mate}).wait_recv()

    def add(dst, *terms):
        total = terms[0][...].astype(F32)
        for term in terms[1:]:
            total = total + term[...].astype(F32)
        dst[...] = total.astype(dst.dtype)

    def start():
        @pl.when(outer)
        def _():
            for build in (give_far, give_near):
                for s in subs:
                    build(s).start()

    def combine():
        @pl.when(inner)
        def _():
            for s in subs:
                got(at(taken, 0, s), s)
                add(at(mix, 0, s), at(taken, 0, s), at(x, far, s))
                cross(s).start()

    def settle():
        @pl.when(inner)
        def _():
            for s in subs:
                got(at(taken, 1, s), SUBS + s)
                got(at(mixed, 0, s), 2 * SUBS + s)
                add(at(o, near, s), at(x, near, s), at(taken, 1, s), at(mixed, 0, s))
                own_across(s).start()
                own_out(s).start()

    def pass_on():
        @pl.when(inner)
        def _():
            for s in subs:
                got(at(o, far, s), (3 + far) * SUBS + s)
                far_out(s).start()

    def finish():
        @pl.when(outer)
        def _():
            for chunk in (near, far):
                for s in subs:
                    got(at(o, chunk, s), (3 + chunk) * SUBS + s)
            for build in (give_far, give_near):
                for s in subs:
                    build(s).wait_send()

        @pl.when(inner)
        def _():
            for build in (cross, own_across, own_out, far_out):
                for s in subs:
                    build(s).wait_send()

    return [start, combine, settle, pass_on, finish]


def params(collective_id, mebibytes):
    return pltpu.CompilerParams(
        collective_id=collective_id,
        has_side_effects=True,
        vmem_limit_bytes=mebibytes * 1024 * 1024,
    )


IN_VMEM = pl.BlockSpec(memory_space=pltpu.VMEM)
IN_HBM = pl.BlockSpec(memory_space=pltpu.HBM)


def plane_scratch(count, rows, width):
    pairs = count // 2
    side = width // 2
    block = rows // pairs
    return [
        pltpu.VMEM((rows, side), BF),
        pltpu.VMEM((rows, side), BF),
        pltpu.VMEM((pairs, block, side), BF),
        pltpu.SemaphoreType.DMA((5, pairs)),
        pltpu.SemaphoreType.DMA((4, pairs)),
    ]


def plane_sum(count, p, x, o, scratch):
    from_mate, paired, slots, ssem, rsem = scratch
    pairs = count // 2
    side = from_mate.shape[1]
    block = slots.shape[1]
    pair = p // 2
    core = p % 2
    mate = {"dp": p + 1 - 2 * core}

    def rows_of(index):
        return pl.ds(pl.multiple_of(index * block, block), block)

    def cols_of(which):
        return pl.ds(pl.multiple_of(which * side, side), side)

    def after(k):
        return (pair + k) % pairs

    def before(k):
        return (pair + pairs - k) % pairs

    def give(k):
        spot = rows_of(after(k))
        return remote(
            x.at[spot, cols_of(1 - core)], from_mate.at[spot], ssem.at[0, k % pairs], rsem.at[0, k % pairs], mate
        )

    def hand(k):
        spot = rows_of(after(k))
        return remote(
            paired.at[spot], slots.at[k], ssem.at[1, k], rsem.at[1, k], {"dp": 2 * after(k) + core}
        )

    def spread(k):
        spot = o.at[rows_of(pair), cols_of(core)]
        return remote(spot, spot, ssem.at[2, k], rsem.at[2, k], {"dp": 2 * after(k) + core})

    def share(k):
        spot = o.at[rows_of(before(k)), cols_of(core)]
        return remote(spot, spot, ssem.at[3, k], rsem.at[3, k], mate)

    def start():
        for k in range(1, pairs + 1):
            give(k).start()

    def pair_up():
        for k in range(1, pairs + 1):
            spot = rows_of(after(k))
            give(k).wait_recv()
            total = x[spot, cols_of(core)].astype(F32) + from_mate[spot].astype(F32)
            paired[spot] = total.astype(BF)
            if k < pairs:
                hand(k).start()

    def settle():
        spot = rows_of(pair)
        total = paired[spot].astype(F32)
        for k in range(1, pairs):
            hand(k).wait_recv()
            total = total + slots[k].astype(F32)
        o[spot, cols_of(core)] = total.astype(BF)
        for k in range(1, pairs):
            spread(k).start()
        share(0).start()

    def pass_on():
        for k in range(1, pairs):
            spot = o.at[rows_of(before(k)), cols_of(core)]
            remote(spot, spot, ssem.at[2, k], rsem.at[2, k], mate).wait_recv()
            share(k).start()

    def finish():
        for k in range(pairs):
            spot = o.at[rows_of(before(k)), cols_of(1 - core)]
            remote(spot, spot, ssem.at[3, k], rsem.at[3, k], mate).wait_recv()
        for k in range(1, pairs + 1):
            give(k).wait_send()
        for k in range(1, pairs):
            hand(k).wait_send()
            spread(k).wait_send()
        for k in range(pairs):
            share(k).wait_send()

    return [start, pair_up, settle, pass_on, finish]


def reduce_scratch(rows, width):
    side = width // 2
    return [
        pltpu.VMEM((rows, side), BF),
        pltpu.VMEM((rows, side), BF),
        pltpu.VMEM((2 * rows, side), BF),
        pltpu.SemaphoreType.DMA((2, 8)),
        pltpu.SemaphoreType.DMA((2, 8)),
    ]


def square_reduce(p, x, kept, matrices, scratch):
    from_mate, paired, taken, ssem, rsem = scratch
    side = from_mate.shape[1]
    pair = p // 2
    core = p % 2
    mate = {"dp": p + 1 - 2 * core}

    def away_from(place, away):
        return {"dp": 2 * (place ^ away) + core}

    def cols_of(which):
        return pl.ds(pl.multiple_of(which * side, side), side)

    def give(m):
        _, first, rows = matrices[m]
        spot = pl.ds(first, rows)
        return remote(x.at[spot, cols_of(1 - core)], from_mate.at[spot], ssem.at[m, 0], rsem.at[m, 0], mate)

    def part_of(m, part):
        _, first, rows = matrices[m]
        return pl.ds(first + part * (rows // 2), rows // 2)

    def slot(m, near, part):
        _, first, rows = matrices[m]
        return pl.ds(2 * first + near * rows + part * (rows // 2), rows // 2)

    def opposite_send(m, part):
        place = matrices[m][0]
        return remote(
            paired.at[part_of(m, part)], taken.at[slot(m, 0, part)],
            ssem.at[m, 1 + part], rsem.at[m, 1], away_from(place, 1 + part),
        )

    def near_raw(m, near):
        part = 1 - near
        return remote(
            paired.at[part_of(m, part)], taken.at[slot(m, near, part)],
            ssem.at[m, 1], rsem.at[m, 2 + 2 * near], away_from(matrices[m][0], 0),
        )

    def near_mixed(m, near):
        part = near
        return remote(
            paired.at[part_of(m, part)], taken.at[slot(m, near, part)],
            ssem.at[m, 2], rsem.at[m, 3 + 2 * near], away_from(matrices[m][0], 0),
        )

    def swap(m):
        spot = kept.at[pl.ds(0, matrices[m][2]), cols_of(core)]
        return remote(spot, spot, ssem.at[m, 6], rsem.at[m, 6], mate)

    def arrived(ref, m, index):
        remote(ref, ref, ssem.at[m, 0], rsem.at[m, index], mate).wait_recv()

    def role(m, away):
        return pl.when(pair == (matrices[m][0] ^ away))

    every = range(len(matrices))

    def start():
        for m in every:
            give(m).start()

    def pair_up():
        for m in every:
            _, first, rows = matrices[m]
            spot = pl.ds(first, rows)
            give(m).wait_recv()
            total = x[spot, cols_of(core)].astype(F32) + from_mate[spot].astype(F32)
            paired[spot] = total.astype(BF)

            @role(m, 3)
            def _(m=m):
                for part in range(2):
                    opposite_send(m, part).start()

            for near in range(2):

                @role(m, 1 + near)
                def _(m=m, near=near):
                    near_raw(m, near).start()

    def mix():
        for m in every:
            for near in range(2):

                @role(m, 1 + near)
                def _(m=m, near=near):
                    piece = slot(m, 0, near)
                    arrived(taken.at[piece], m, 1)
                    spot = part_of(m, near)
                    total = paired[spot].astype(F32) + taken[piece].astype(F32)
                    paired[spot] = total.astype(BF)
                    near_mixed(m, near).start()

    def settle():
        for m in every:

            @role(m, 0)
            def _(m=m):
                _, first, rows = matrices[m]
                for near in range(2):
                    arrived(taken.at[slot(m, near, 1 - near)], m, 2 + 2 * near)
                    arrived(taken.at[slot(m, near, near)], m, 3 + 2 * near)
                spot = pl.ds(first, rows)
                total = x[spot, cols_of(core)].astype(F32) + from_mate[spot].astype(F32)
                for near in range(2):
                    total = total + taken[pl.ds(2 * first + near * rows, rows)].astype(F32)
                kept[pl.ds(0, rows), cols_of(core)] = total.astype(BF)
                swap(m).start()

    def finish():
        for m in every:
            rows = matrices[m][2]
            give(m).wait_send()

            @role(m, 0)
            def _(m=m, rows=rows):
                arrived(kept.at[pl.ds(0, rows), cols_of(1 - core)], m, 6)
                swap(m).wait_send()

            @role(m, 3)
            def _(m=m):
                for part in range(2):
                    opposite_send(m, part).wait_send()

            for near in range(2):

                @role(m, 1 + near)
                def _(m=m, near=near):
                    near_raw(m, near).wait_send()
                    near_mixed(m, near).wait_send()

    return [start, pair_up, mix, settle, finish]


def gather_scratch():
    return [pltpu.SemaphoreType.DMA((4, 2 * CUTS, 4))] * 2


def square_gather(p, sizes, out, own, scratch):
    ssem, rsem = scratch
    width = out.shape[1]
    pair = p // 2
    core = p % 2
    mate = {"dp": p + 1 - 2 * core}
    firsts = [sum(sizes[:index]) for index in range(4)]

    def piece(index, side, part):
        rows = sizes[index]
        if index == 2:
            across = pl.ds(pl.multiple_of(side * (width // 2), width // 2), width // 2)
            share = rows // (2 * CUTS)
            return out.at[pl.ds(firsts[index] + part * share, share), across]
        share = rows // (4 * CUTS)
        first = firsts[index] + side * (rows // 2) + part * share
        return out.at[pl.ds(pl.multiple_of(first, share), share)]

    def copy(index, part, route, device):
        spot = piece(index, core, part)
        return remote(spot, spot, ssem.at[index, part, route], rsem.at[index, part, route], device)

    def other(away):
        return {"dp": 2 * (pair + away * (1 - 2 * ((pair // away) % 2))) + core}

    def role(index, away):
        return pl.when(pair == (PLACE[index] ^ away))

    def wait_in(index, part, route, side):
        spot = piece(index, side, part)
        remote(spot, spot, ssem.at[index, part, route], rsem.at[index, part, route], mate).wait_recv()

    ways = ((1, 0, 2), (2, 1, 1))
    parts = 2 * CUTS

    def half(which):
        return range(which * CUTS, (which + 1) * CUTS)

    def start():
        for index in range(4):

            @role(index, 0)
            def _(index=index):
                for part in range(parts):
                    piece(index, core, part)[...] = own(index, part)
                for part in range(parts):
                    copy(index, part, 0, other(1)).start()
                    copy(index, (part + CUTS) % parts, 1, other(2)).start()
                for part in range(parts):
                    copy(index, part, 3, mate).start()

    def pass_on(indices=range(4)):
        for index in indices:
            for away, route, onward in ways:

                @role(index, away)
                def _(index=index, away=away, route=route, onward=onward):
                    for part in half(away - 1):
                        wait_in(index, part, route, core)
                        copy(index, part, 2, other(onward)).start()
                        copy(index, part, 3, mate).start()

    def rest():
        for index in range(4):
            for away, route, _ in ways:

                @role(index, away)
                def _(index=index, away=away, route=route):
                    for part in half(2 - away):
                        wait_in(index, part, route, core)
                        copy(index, part, 3, mate).start()

            @role(index, 3)
            def _(index=index):
                for part in [part // 2 + CUTS * (part % 2) for part in range(parts)]:
                    wait_in(index, part, 2, core)
                    copy(index, part, 3, mate).start()

    def finish():
        for index in range(4):
            for part in range(parts):
                wait_in(index, part, 3, 1 - core)
                copy(index, part, 3, mate).wait_send()

            @role(index, 0)
            def _(index=index):
                for part in range(parts):
                    copy(index, part, 0, other(1)).wait_send()
                    copy(index, part, 1, other(2)).wait_send()

            for away, _, onward in ways:

                @role(index, away)
                def _(index=index, away=away, onward=onward):
                    for part in half(away - 1):
                        copy(index, part, 2, other(onward)).wait_send()

    return [start, pass_on, rest, finish]


def vector_scratch(count, shape):
    return [
        pltpu.VMEM((count,) + shape, F32),
        pltpu.SemaphoreType.DMA((count,)),
        pltpu.SemaphoreType.DMA((count,)),
    ]


def vector_sum(axis, count, p, v, o, scratch):
    slots, ssem, rsem = scratch

    def send(k):
        return remote(v, slots.at[p], ssem.at[k], rsem.at[k], {axis: (p + k) % count})

    def start():
        slots[p] = v[...]
        for k in range(1, count):
            send(k).start()

    def finish():
        for k in range(1, count):
            spot = slots.at[(p + count - k) % count]
            remote(v, spot, ssem.at[k], rsem.at[k], {axis: (p + k) % count}).wait_recv()
        total = slots[0]
        for k in range(1, count):
            total = total + slots[k]
        o[...] = total
        for k in range(1, count):
            send(k).wait_send()

    return [start, finish]


ROW_STEP = 32


def tdot(left, right):
    return lax.dot_general(left, right, (((0,), (0,)), ((), ())), preferred_element_type=F32)


def dot(left, right):
    return jnp.dot(left, right, preferred_element_type=F32)


def dot_t(left, right):
    return lax.dot_general(left, right, (((1,), (1,)), ((), ())), preferred_element_type=F32)


def cut(values):
    high = values.astype(BF)
    return high, (values - high.astype(F32)).astype(BF)


def dot3(lh, ll, rh, rl, dims=(((1,), (0,)), ((), ()))):
    def dot(left, right):
        return lax.dot_general(left, right, dims, preferred_element_type=F32)

    return dot(lh, rh) + (dot(lh, rl) + dot(ll, rh))


def step_kernel(
    count, sizes,
    seg, rp, hb, fb, mh, mf, x_hbm, cot_hbm, wq_hbm, wo_hbm, wu_hbm, wd_hbm, mq, mo, mu, md,
    y_hbm, gt_hbm, xo_hbm, gall_hbm, vec, totals,
    y, gt, xo, gall, x, cot, f1, f2, f3, f4, wo_f, gx, go, gp, dz1, b1, b2, b3, b4, b5, b6, b7, b8, bt, red_s, kept,
    gap, gbp, wq, wo, q_s, k_s, v_s, ctx_s, dq_s, dk_s, dv_s, p_s, inv1_s, vecp, squares,
    wsem, lsem, psem, osem, *scratch,
):
    p = lax.axis_index("dp")
    t = lax.axis_index("tensor")
    tokens, width = x.shape
    half = tokens // 2
    quarter = tokens // 4
    columns = q_s.shape[1]
    heads = columns // HD
    tile = width // 3
    scale = 1.0 / math.sqrt(HD)
    square = count == 8
    group = count // 4
    share = width // group
    which = p // group
    core = p % 2
    mate = {"dp": p + 1 - 2 * core}
    firsts = [sum(sizes[:index]) for index in range(4)]
    n1_s, slope_s, dz2_s, u_s = (ref.at[pl.ds(0, tokens)] for ref in (f3, f1, f2, f4))
    h1l_s, act_s, du_s, dm_s, da_s, part_s = (
        ref.at[pl.ds(0, tokens)] for ref in (b3, b4, b5, b6, b7, b8)
    )
    wu, wd = b1, b2
    zf, af, sf, xf = f3, f1, f2, f4.at[pl.ds(0, share)]
    ah, al, zh, zl, dh, dl, sh, sl = b1, b2, b3, b4, b5, b6, b7, b8
    gf = kept if square else gall
    loads = [
        pltpu.make_async_copy(source, target, wsem.at[i])
        for i, (source, target) in enumerate(
            (
                (wq_hbm, f4), (wo_hbm, wo_f), (wu_hbm, f1), (wd_hbm, f2),
                (x_hbm, x), (cot_hbm, cot),
            )
        )
    ]
    for place in (0, 4, 1, 2, 3, 5):
        loads[place].start()
    greet(z_peers(t) + [{"dp": (p + k) % count} for k in range(1, count)])
    sums, back = [], []
    for q in range(4):
        place = pl.ds(q * quarter, quarter)
        pieces = scratch[5 * q : 5 * q + 5]
        sums.append(relay_sum(t, part_s.at[place], red_s.at[place], pieces))
        back.append(relay_sum(t, bt.at[place], red_s.at[place], pieces))
    top = 4 * columns
    if square:
        ends = [(PLACE[2], 0, width), (PLACE[3], width, width)]
        plane_b = square_reduce(p, gbp, kept, ends, scratch[20:25])
        ends = [(PLACE[0], 0, 3 * columns), (PLACE[1], 3 * columns, columns)]
        plane_a = square_reduce(p, gap, kept, ends, scratch[25:30])
    else:
        plane_b = plane_sum(count, p, gbp, gall.at[pl.ds(top, 2 * width)], scratch[20:25])
        plane_a = plane_sum(count, p, gap, gall.at[pl.ds(0, top)], scratch[25:30])
    vector = vector_sum("dp", count, p, vecp, vec, scratch[30:33])
    along = vector_sum("tensor", 4, t, squares, totals, scratch[33:36])
    line = line_sum(t, gx, go, scratch[36:42])
    vecp[...] = jnp.zeros_like(vecp)
    lane = lax.broadcasted_iota(jnp.int32, (1, columns), 1)

    def in_head(index):
        return (lane // HD) == index

    def rows_of(h):
        return pl.ds(h * half, half)

    def quarter_of(q):
        return pl.ds(q * quarter, quarter)

    def over_rows(q, body, init=0):
        def step(i, carry):
            first = q * quarter + i * ROW_STEP
            return body(pl.ds(pl.multiple_of(first, ROW_STEP), ROW_STEP), carry)

        return lax.fori_loop(0, quarter // ROW_STEP, step, init)

    def fold(values):
        return values.reshape(ROW_STEP // 8, 8, values.shape[1]).sum(axis=0)

    def add_vec(row, folded):
        vecp[row : row + 1, 0 : folded.shape[1]] += jnp.sum(folded, axis=0, keepdims=True)

    def narrow(index, source, target):
        loads[index].wait()
        target[...] = source[...].astype(BF)

    def attention(h):
        r = rows_of(h)
        xb = x[r]
        q = (dot_t(xb, wq[0 * columns : 1 * columns]) + hb[0:1]).astype(BF)
        k = dot_t(xb, wq[1 * columns : 2 * columns]).astype(BF)
        v = (dot_t(xb, wq[2 * columns : 3 * columns]) + hb[1:2]).astype(BF)
        q_s[r], k_s[r], v_s[r] = q, k, v
        down = jnp.broadcast_to(seg[h : h + 1].astype(F32), (half, half))
        same = down == down.T
        context = jnp.zeros((half, columns), F32)
        for index in range(heads):
            mine = jnp.where(in_head(index), q, jnp.zeros_like(q))
            scores = jnp.where(same, dot_t(mine, k) * scale, -1e30)
            expo = jnp.exp(scores - jnp.max(scores, axis=-1, keepdims=True))
            probs = expo / jnp.sum(expo, axis=-1, keepdims=True)
            p_s[h * heads + index] = probs
            context = jnp.where(in_head(index), dot(probs.astype(BF), v), context)
        low = context.astype(BF)
        ctx_s[r] = low
        part_s[r] = dot(low, wo[...]).astype(BF)

    def up(q):
        def norm(r, carry):
            z = x[r].astype(F32) + red_s[r].astype(F32) + rp[0:1]
            center = z - jnp.mean(z, axis=-1, keepdims=True)
            inverse = lax.rsqrt(jnp.mean(center * center, axis=-1, keepdims=True) + EPS_NORM)
            normed = center * inverse
            n1_s[r] = normed
            inv1_s[r] = jnp.broadcast_to(inverse, (ROW_STEP, 128))
            h1l_s[r] = (normed * rp[2:3] + rp[3:4]).astype(BF)
            return carry

        over_rows(q, norm)
        u_s[quarter_of(q)] = dot(h1l_s[quarter_of(q)], wu[...])

        def gelu(r, carry):
            u = u_s[r] + fb[...].reshape(1, width)
            cdf = 0.5 * (1.0 + lax.erf(u * (1.0 / math.sqrt(2.0))))
            act_s[r] = (u * cdf).astype(BF)
            slope_s[r] = cdf + u * jnp.exp(-0.5 * u * u) * (1.0 / math.sqrt(2.0 * math.pi))
            return carry

        over_rows(q, gelu)

    def down(q):
        r = quarter_of(q)
        part_s[r] = dot(act_s[r], wd[...]).astype(BF)

    def out_back(q):
        def norm(r, carry):
            s_dz2, s_dyn, s_dy = carry
            h1 = n1_s[r] * rp[2:3] + rp[3:4]
            z = h1 + red_s[r].astype(F32) + rp[1:2]
            center = z - jnp.mean(z, axis=-1, keepdims=True)
            inverse = lax.rsqrt(jnp.mean(center * center, axis=-1, keepdims=True) + EPS_NORM)
            normed = center * inverse
            y[r] = (normed * rp[4:5] + rp[5:6]).astype(BF)
            dy = cot[r].astype(F32)
            scaled = dy * rp[4:5]
            first = jnp.mean(scaled, axis=-1, keepdims=True)
            second = jnp.mean(scaled * normed, axis=-1, keepdims=True)
            dz2 = inverse * (scaled - first - normed * second)
            dz2_s[r] = dz2
            dm_s[r] = dz2.astype(BF)
            return s_dz2 + fold(dz2), s_dyn + fold(dy * normed), s_dy + fold(dy)

        zero = jnp.zeros((8, width), F32)
        for row, total in zip((1, 4, 5), over_rows(q, norm, (zero, zero, zero))):
            add_vec(row, total)
        u_s[quarter_of(q)] = dot_t(dm_s[quarter_of(q)], wd[...])

        def slope(r, carry):
            du = (u_s[r] * slope_s[r]).astype(BF)
            du_s[r] = du
            return carry + fold(du.astype(F32))

        add_vec(6, over_rows(q, slope, zero))

    def up_back(q):
        r = quarter_of(q)
        part_s[r] = dot_t(du_s[r], wu[...]).astype(BF)

    def grads_b():
        gbp[0:width] = tdot(h1l_s[...], du_s[...]).astype(BF)
        gbp[width : 2 * width] = tdot(act_s[...], dm_s[...]).astype(BF)

    def norm_back(q):
        def norm(r, carry):
            s_dz1, s_dhn, s_dh = carry
            dh1 = red_s[r].astype(F32) + dz2_s[r]
            normed = n1_s[r]
            scaled = dh1 * rp[2:3]
            first = jnp.mean(scaled, axis=-1, keepdims=True)
            second = jnp.mean(scaled * normed, axis=-1, keepdims=True)
            grad = inv1_s[r][:, 0:1] * (scaled - first - normed * second)
            dz1[r] = grad
            da_s[r] = grad.astype(BF)
            return s_dz1 + fold(grad), s_dhn + fold(dh1 * normed), s_dh + fold(dh1)

        zero = jnp.zeros((8, width), F32)
        for row, total in zip((0, 2, 3), over_rows(q, norm, (zero, zero, zero))):
            add_vec(row, total)

    def attention_back(h):
        r = rows_of(h)
        dc = dot_t(da_s[r], wo[...]).astype(BF)
        q, k, v = q_s[r], k_s[r], v_s[r]
        dq = dk = dv = jnp.zeros((half, columns), F32)
        for index in range(heads):
            probs = p_s[h * heads + index]
            mine = jnp.where(in_head(index), dc, jnp.zeros_like(dc))
            dp = dot_t(mine, v)
            ds = (probs * (dp - jnp.sum(probs * dp, axis=-1, keepdims=True))).astype(BF)
            dv = jnp.where(in_head(index), tdot(probs.astype(BF), dc), dv)
            dq = jnp.where(in_head(index), dot(ds, k), dq)
            dk = jnp.where(in_head(index), tdot(ds, q), dk)
        dq = (dq * scale).astype(BF)
        dk = (dk * scale).astype(BF)
        dv = dv.astype(BF)
        dq_s[r], dk_s[r], dv_s[r] = dq, dk, dv
        add_vec(7, jnp.sum(dq.astype(F32), axis=0, keepdims=True))
        add_vec(8, jnp.sum(dv.astype(F32), axis=0, keepdims=True))

    def grads_a():
        for i, source in enumerate((dq_s, dk_s, dv_s)):
            gap[i * columns : (i + 1) * columns] = tdot(source[...], x[...]).astype(BF)
        gap[3 * columns : 4 * columns] = tdot(ctx_s[...], da_s[...]).astype(BF)

    def back_terms(h):
        r = rows_of(h)
        total = dot(dq_s[r], wq[0 * columns : 1 * columns]) + dot(dk_s[r], wq[1 * columns : 2 * columns]) + dot(dv_s[r], wq[2 * columns : 3 * columns])
        bt[r] = total.astype(BF)

    def moment_copy(index):
        moment = (mq, mo, mu, md)[index]
        return pltpu.make_async_copy(moment, f1.at[pl.ds(0, sizes[index])], lsem.at[0])

    def fetch_moment():
        for index in range(4):
            pl.when(which == PLACE[index])(moment_copy(index).start)

    def cols(index):
        return pl.ds(pl.multiple_of(index * tile, tile), tile)

    def gram(indices):
        for index in indices:
            rows = sizes[index]
            first = 0 if square else firsts[index]

            @pl.when(which == PLACE[index])
            def _(index=index, first=first, rows=rows):
                moment_copy(index).wait()
                for i in range(3):
                    spot = pl.ds(i * (rows // 3), rows // 3)
                    z = 0.5 * f1[spot] + gf[pl.ds(first + i * (rows // 3), rows // 3)].astype(F32)
                    if index == 2:
                        z = z.T
                        spot = (pl.ds(0, width), spot)
                    zf[spot] = z
                    zh[spot], zl[spot] = cut(z)
                if rows < width:
                    spot = pl.ds(rows, width - rows)
                    zf[spot] = jnp.zeros((width - rows, width), F32)
                    zh[spot] = jnp.zeros((width - rows, width), BF)
                    zl[spot] = jnp.zeros((width - rows, width), BF)

        over = (((0,), (0,)), ((), ()))
        for j, (row, col) in enumerate(((core, core), (core, core + 1), (2 * core, 2))):
            gx[:, pl.ds(j * tile, tile)] = dot3(
                zh[:, cols(row)], zl[:, cols(row)], zh[:, cols(col)], zl[:, cols(col)], over
            )

    diagonal = lax.broadcasted_iota(jnp.int32, (tile, tile), 0) == lax.broadcasted_iota(
        jnp.int32, (tile, tile), 1
    )

    def upper(first, second):
        trace = jnp.float32(0.0)
        for block in (first[:, 0:tile], second[:, 0:tile], second[:, 2 * tile :]):
            trace = trace + jnp.sum(jnp.where(diagonal, block, 0.0))
        inverse = 1.0 / (jnp.sqrt(jnp.full((1, 1), trace, F32)) + 1e-07)
        shrink = inverse * inverse
        blocks = (
            (0, 0, first, 0), (0, 1, first, 1), (0, 2, first, 2),
            (1, 1, second, 0), (1, 2, second, 1), (2, 2, second, 2),
        )
        for row, col, source, j in blocks:
            block = source[:, j * tile : (j + 1) * tile] * shrink
            for r, c, value in ((row, col, block),) + (((col, row, block.T),) if row != col else ()):
                spot = (pl.ds(r * tile, tile), pl.ds(c * tile, tile))
                af[spot] = value
                ah[spot], al[spot] = cut(value)
        if square:
            for index, rows in enumerate(sizes):

                @pl.when(which == PLACE[index])
                def _(half_rows=rows // 2):
                    mine = pl.ds(pl.multiple_of(core * half_rows, half_rows), half_rows)
                    xf[0:half_rows] = zf[mine] * inverse
                    if half_rows < share:
                        xf[half_rows:share] = jnp.zeros((share - half_rows, width), F32)

        else:
            rank = p % group
            xf[...] = zf[pl.ds(pl.multiple_of(rank * share, share), share)] * inverse

    def product(left, right, base, base_scale, factor, targets, times):
        (lh, ll), (rh, rl) = left, right
        for i in range(3):
            rows = pl.ds(i * tile, tile)
            for j in range(i, 3):
                across = pl.ds(j * tile, tile)
                value = base_scale * base[rows, across] + factor * times(
                    lh[rows], ll[rows], rh[:, across], rl[:, across]
                )
                parts = (*cut(value), value)
                for target, part in zip(targets, parts):
                    target[rows, across] = part
                if i != j and len(targets) == 2:
                    for target, part in zip(targets, parts):
                        target[across, rows] = part.T
                elif i != j:
                    mirrored = value.T
                    for target, part in zip(targets, (*cut(mirrored), mirrored)):
                        target[across, rows] = part

    def make_d(times=dot3):
        product((ah, al), (ah, al), af, coef_b, coef_c, (dh, dl), times)

    def move_x(times=dot3):
        xh, xl = cut(xf[...])
        xf[...] = coef_a * xf[...] + times(xh, xl, dh[...], dl[...])

    def own_gradient(index, part):
        if index == 2:
            across = pl.ds(pl.multiple_of(core * (width // 2), width // 2), width // 2)
            piece = sizes[index] // (2 * CUTS)
            return gf[pl.ds(part * piece, piece), across]
        piece = sizes[index] // (4 * CUTS)
        first = pl.multiple_of(core * (sizes[index] // 2) + part * piece, piece)
        return gf[pl.ds(first, piece)]

    def own_step(index, part):
        if index == 2:
            piece = sizes[index] // (2 * CUTS)
            return xf[:, pl.ds(part * piece, piece)].T.astype(BF)
        piece = sizes[index] // (4 * CUTS)
        return xf[pl.ds(part * piece, piece)].astype(BF)

    if square:
        spread = square_gather(p, sizes, gall, own_gradient, scratch[42:44])
        collect = square_gather(p, sizes, xo, own_step, scratch[44:46])
        early = (which == PLACE[2]) | (which == PLACE[3])
        late = (which == PLACE[0]) | (which == PLACE[1])

    start, mix, settle, pass_on, end = (
        (lambda q, place=place: sums[q][place]()) for place in range(5)
    )

    def round_trip(first, second):
        end(0), first(0), pass_on(1), second(0), settle(2), mix(3), start(0)
        end(1), first(1), pass_on(2), settle(3), second(1), mix(0), start(1)
        end(2), first(2), pass_on(3), second(2), settle(0), mix(1), start(2)
        end(3), first(3), pass_on(0), second(3), settle(1), mix(2), start(3)

    loads[4].wait()
    narrow(0, f4, wq)
    narrow(1, wo_f, wo)
    attention(0)
    start(0), start(1)
    attention(1)
    mix(0), start(2), mix(1), settle(0), start(3)
    narrow(2, f1, wu)
    mix(2), settle(1), pass_on(0)
    narrow(3, f2, wd)
    loads[5].wait()
    outs = [
        pltpu.make_async_copy(source, target, osem.at[i])
        for i, (source, target) in enumerate(((y, y_hbm), (gt, gt_hbm), (gall, gall_hbm)))
    ]
    round_trip(up, down)
    round_trip(out_back, up_back)
    outs[0].start()
    fetch_moment()
    grads_b()
    plane_b[0]()
    end(0), norm_back(0), pass_on(1), settle(2), mix(3)
    plane_b[1]()
    end(1), norm_back(1), pass_on(2), settle(3)
    attention_back(0)
    end(2), norm_back(2), pass_on(3)
    if square:
        plane_b[2]()
    end(3), norm_back(3)
    attention_back(1)
    grads_a()
    plane_a[0]()
    vector[0]()
    if square:
        plane_b[3]()
        plane_a[1]()

        @pl.when(early)
        def _():
            plane_b[4]()
            gram((2, 3))
            line[0]()

        plane_a[2]()
        back_terms(0)
        back_terms(1)

        @pl.when(late)
        def _():
            plane_a[3]()
            plane_b[4]()
            plane_a[4]()
            gram((0, 1))
            line[0]()
            spread[0]()

    else:
        plane_b[2]()
        plane_a[1]()
        back_terms(0)
        back_terms(1)
        plane_b[3]()
        plane_a[2]()
        plane_b[4]()
        plane_a[3]()
        plane_a[4]()
        gram(range(4))
        line[0]()
    vector[1]()
    moved = 0.5 * mh[...] + vec[7:9, 0:columns]
    squares[0:2] = jnp.broadcast_to(jnp.sum(moved * moved, axis=1, keepdims=True), (2, 128))
    moved = 0.5 * mf[...].reshape(1, width) + vec[6:7]
    squares[2:3] = jnp.broadcast_to(jnp.sum(moved * moved, axis=1, keepdims=True), (1, 128))
    squares[3:8] = jnp.zeros((5, 128), F32)
    along[0]()
    if square:
        pl.when(early)(spread[0])
    for place in range(1, 5):
        line[place]()
        if square and place == 2:
            spread[1]()
    swap = remote(go, gp, psem.at[0], psem.at[1], mate)
    swap.start()
    for q in range(2):
        back[q][0]()
    swap.wait()

    @pl.when(core == 0)
    def _():
        upper(go, gp)

    @pl.when(core == 1)
    def _():
        upper(gp, go)

    def one_pass(lh, ll, rh, rl):
        return dot(lh, rh)

    plan = {
        (0, 1): ((1, 0),),
        (0, 2): ((1, 1), (0, 2)),
        (1, 0): ((2, 0), (0, 3)),
        (1, 1): ((2, 1), (1, 2)),
        (1, 2): ((3, 0), (1, 3)),
        (2, 1): ((3, 1), (2, 2)),
        (2, 2): ((2, 3),),
        (3, 0): ((3, 2),),
        (3, 1): ((3, 3),),
    }

    def between(k, place):
        for action, q in plan.get((k, place), ()):
            back[q][action]()
        if square and (k, place) == (1, 2):
            spread[2]()

    def advance(k, times, x_times):
        make_d(times)
        move_x(x_times)
        between(k, 0)
        product((ah, al), (dh, dl), af, coef_a, 1.0, (sh, sl, sf), times)
        between(k, 1)
        product((sh, sl), (dh, dl), sf, coef_a, 1.0, (ah, al, af), times)
        between(k, 2)

    advance(0, dot3, one_pass)
    advance(1, dot3, one_pass)
    advance(2, one_pass, one_pass)
    advance(3, dot3, dot3)
    if square:
        collect[1]((2, 3))
    make_d()
    move_x()
    for q in range(4):
        back[q][4]()
    gt[...] = (red_s[...].astype(F32) + dz1[...]).astype(BF)
    outs[1].start()
    along[1]()
    if square:

        @pl.when(early)
        def _():
            plane_a[4]()

        collect[0]()
        collect[1]((0, 1))
        spread[3]()
        outs[2].start()
        collect[2]()
        collect[3]()
    else:
        outs[2].start()
        gather_any(p, core, count // 2, mate, xf, xo, scratch[42], scratch[43])
    last = pltpu.make_async_copy(xo, xo_hbm, osem.at[3])
    last.start()
    for moving in (*outs, last):
        moving.wait()


def gather_any(p, core, pairs, mate, xf, xo, asem_s, asem_r):
    pair = p // 2
    share = xf.shape[0]

    def rows_of(device):
        return xo.at[pl.ds(pl.multiple_of(device * share, share), share)]

    def after(k):
        return 2 * ((pair + k) % pairs) + core

    def before(k):
        return 2 * ((pair + pairs - k) % pairs) + core

    def send(k):
        return remote(rows_of(p), rows_of(p), asem_s.at[0, k], asem_r.at[0, k], {"dp": after(k)})

    def hand(k):
        spot = rows_of(before(k))
        return remote(spot, spot, asem_s.at[1, k], asem_r.at[1, k], mate)

    xo[pl.ds(pl.multiple_of(p * share, share), share)] = xf[...].astype(BF)
    for k in range(1, pairs):
        send(k).start()
    hand(0).start()
    for k in range(1, pairs):
        spot = rows_of(before(k))
        remote(spot, spot, asem_s.at[0, k], asem_r.at[0, k], mate).wait_recv()
        hand(k).start()
    for k in range(pairs):
        spot = rows_of(before(k) + 1 - 2 * core)
        remote(spot, spot, asem_s.at[1, k], asem_r.at[1, k], mate).wait_recv()
    for k in range(1, pairs):
        send(k).wait_send()
    for k in range(pairs):
        hand(k).wait_send()


def step(count, tokens, cotangent, segments, small, weights, moments, collective_id):
    rows, width = tokens.shape
    sizes = tuple(moment.shape[0] for moment in moments)
    columns = sizes[1]
    heads = columns // HD
    half = rows // 2
    tile = width // 3
    square = count == 8

    def low(*shape):
        return pltpu.VMEM(shape, BF)

    def full(*shape):
        return pltpu.VMEM(shape, F32)

    def out(shape, dtype):
        return jax.ShapeDtypeStruct(shape, dtype)

    plane = reduce_scratch if square else functools.partial(plane_scratch, count)
    pair_sems = [pltpu.SemaphoreType.DMA((2, count // 2))] * 2
    steps_rows = sum(sizes) if square else 4 * width
    scratch = (
        [low(rows, width)] * 2
        + [low(steps_rows, width), low(sum(sizes), width)]
        + [low(rows, width)] * 2
        + [full(width, width)] * 3
        + [full(3 * columns, width), full(columns, width)]
        + [full(tile, width)] * 3
        + [full(rows, width)]
        + [low(width, width)] * 8
        + [low(rows, width)] * 2
        + [low(width, width) if square else low(16, width)]
        + [low(4 * columns, width), low(2 * width, width)]
        + [low(3 * columns, width), low(columns, width)]
        + [low(rows, columns)] * 7
        + [full(2 * heads, half, half), full(rows, 128), full(16, width), full(8, 128)]
        + [pltpu.SemaphoreType.DMA((n,)) for n in (6, 2, 2, 4)]
        + relay_scratch(rows // 4, width, BF) * 4
        + plane(2 * width, width)
        + plane(4 * columns, width)
        + vector_scratch(count, (16, width))
        + vector_scratch(4, (8, 128))
        + line_scratch(tile, width, F32)
        + (gather_scratch() * 2 if square else pair_sems)
    )
    return pl.pallas_call(
        functools.partial(step_kernel, count, sizes),
        out_shape=(
            out((rows, width), BF),
            out((rows, width), BF),
            out((steps_rows, width), BF),
            out((sum(sizes), width), BF),
            out((16, width), F32),
            out((8, 128), F32),
        ),
        in_specs=[IN_VMEM] * 6 + [IN_HBM] * 10,
        out_specs=(IN_HBM,) * 4 + (IN_VMEM,) * 2,
        scratch_shapes=scratch,
        compiler_params=params(collective_id, 61),
        name="step",
    )(segments, *small, tokens, cotangent, *weights, *moments)


def apply_kernel(factors, *refs):
    ins, outs = refs[:26], refs[26:]
    small_in, small_out = ins[18:], outs[14:]
    for index, factor in enumerate(factors):
        weight, moment, grad, step = (ins[4 * index + i] for i in range(4))
        new_moment, new, low = (outs[3 * index + i] for i in range(3))
        new_moment[...] = 0.5 * moment[...] + grad[...].astype(F32)
        value = weight[...] - factor * step[...].astype(F32)
        new[...] = value
        low[...] = value.astype(BF)
    for source, target in zip(ins[16:18], outs[12:14]):
        target[...] = source[...]

    @pl.when(pl.program_id(0) == 0)
    def _():
        vec, totals, heads, ff, rows, mom_heads, mom_ff, mom_rows = small_in
        columns = heads.shape[1]
        wide = ff.shape[0]
        moment = 0.5 * mom_heads[...] + vec[7:9, 0:columns]
        small_out[0][...] = moment
        scale = lax.rsqrt(totals[0:2, 0:1] * (1.0 / (4 * columns)) + 1e-06)
        small_out[1][...] = heads[...] - 0.1 * moment * scale
        moment = 0.5 * mom_ff[...].reshape(1, wide) + vec[6:7]
        small_out[2][...] = moment.reshape(wide)
        scale = lax.rsqrt(totals[2:3, 0:1] * (1.0 / (4 * wide)) + 1e-06)
        value = ff[...].reshape(1, wide) - 0.1 * moment * scale
        small_out[3][...] = value.reshape(wide)
        moment = 0.5 * mom_rows[...] + vec[0:6]
        small_out[4][...] = moment
        mean = jnp.mean(moment * moment, axis=-1, keepdims=True)
        small_out[5][...] = rows[...] - 0.1 * moment * lax.rsqrt(mean + 1e-06)


APPLY_STEPS = 4


def apply(sizes, factors, weights, moments, grads, steps, passed, small):
    width = grads.shape[1]
    in_specs, operands, out_specs, out_shape = [], [], [], []

    def block(rows, first=0):
        share = rows // APPLY_STEPS
        return pl.BlockSpec((share, width), lambda i, skip=first // share: (skip + i, 0))

    def whole(array):
        return pl.BlockSpec(array.shape, lambda i, n=array.ndim: (0,) * n)

    first = 0
    for rows, weight, moment in zip(sizes, weights, moments):
        in_specs += [block(rows), block(rows), block(rows, first), block(rows, first)]
        operands += [weight, moment, grads, steps]
        out_specs += [block(rows)] * 3
        out_shape += [jax.ShapeDtypeStruct((rows, width), kind) for kind in (F32, F32, BF)]
        first += rows
    for array in passed:
        turn = pl.BlockSpec((array.shape[0] // 4, width), lambda i: (i // (APPLY_STEPS // 4), 0))
        in_specs.append(turn)
        operands.append(array)
        out_specs.append(turn)
        out_shape.append(jax.ShapeDtypeStruct(array.shape, array.dtype))
    for array in small:
        in_specs.append(whole(array))
        operands.append(array)
    for array in small[2:5]:
        for _ in range(2):
            out_specs.append(whole(array))
            out_shape.append(jax.ShapeDtypeStruct(array.shape, F32))
    return pl.pallas_call(
        functools.partial(apply_kernel, factors),
        grid=(APPLY_STEPS,),
        out_shape=tuple(out_shape),
        in_specs=in_specs,
        out_specs=tuple(out_specs),
        compiler_params=pltpu.CompilerParams(vmem_limit_bytes=61 * 1024 * 1024),
        name="apply",
    )(*operands)


def vector_step(param, moment, mean_sq):
    return param - 0.1 * moment * lax.rsqrt(mean_sq + 1e-06)


def local(
    tokens, segments, cotangent,
    w_qkv, w_out, w_up, w_down, head_bias, ff_bias, row_params,
    mom_qkv, mom_out, mom_up, mom_down, mom_heads, mom_ff, mom_params,
):
    width = tokens.shape[1]
    columns = w_qkv.shape[2]
    ff_cols = w_up.shape[1]
    tensor_size = lax.axis_size("tensor")
    count = lax.axis_size("dp")
    qkv_rows = 3 * columns
    wq_rows = w_qkv.transpose(0, 2, 1).reshape(qkv_rows, width)
    moments = (mom_qkv.transpose(0, 2, 1).reshape(qkv_rows, width), mom_out, mom_up, mom_down)
    output_rows, grad_inputs, steps, grads, vector_total, totals = step(
        count, tokens, cotangent, segments, (row_params, head_bias, ff_bias, mom_heads, mom_ff),
        (wq_rows, w_out, w_up, w_down), moments, 1,
    )

    def to_qkv(rows):
        return rows.reshape(3, columns, width).transpose(0, 2, 1)

    bounds = (0, qkv_rows, qkv_rows + columns, qkv_rows + columns + width)

    def grad_of(index, rows):
        return grads[bounds[index] : bounds[index] + rows].astype(F32)

    def step_of(index, rows):
        first = PLACE[index] * width
        part = steps[first : first + rows].astype(F32)
        return part.T if index == 2 else part

    wide = math.sqrt(ff_cols * tensor_size / width)
    if count == 8:
        sizes = (qkv_rows, columns, width, ff_cols)
        factors = (0.8 * math.sqrt(3.0), 0.8, 0.8 * wide, 0.8 * wide)
        done = apply(
            sizes, factors, (wq_rows, w_out, w_up, w_down), moments, grads, steps, (output_rows, grad_inputs),
            (
                vector_total, totals, head_bias, ff_bias, row_params,
                mom_heads, mom_ff, mom_params,
            ),
        )
        qkv_new = [rows.reshape(3, columns, width).transpose(0, 2, 1) for rows in done[0:3]]
        return (
            *done[12:14], *qkv_new, *done[3:12], *done[14:20],
        )

    new_mom_heads = 0.5 * mom_heads + vector_total[7:9, :columns]
    new_mom_ff = 0.5 * mom_ff + vector_total[6]
    new_mom_params = 0.5 * mom_params + vector_total[0:6]
    new_mom_qkv = 0.5 * mom_qkv + to_qkv(grad_of(0, qkv_rows))
    new_mom_out = 0.5 * mom_out + grad_of(1, columns)
    new_mom_up = 0.5 * mom_up + grad_of(2, width)
    new_mom_down = 0.5 * mom_down + grad_of(3, ff_cols)
    new_qkv = w_qkv - 0.8 * math.sqrt(3.0) * to_qkv(step_of(0, qkv_rows))
    new_out = w_out - 0.8 * step_of(1, columns)
    new_up = w_up - 0.8 * wide * step_of(2, width)
    new_down = w_down - 0.8 * wide * step_of(3, ff_cols)
    new_heads = vector_step(head_bias, new_mom_heads, totals[0:2, 0:1] / (columns * tensor_size))
    new_ff = vector_step(ff_bias, new_mom_ff, totals[2, 0] / (ff_cols * tensor_size))
    new_params = vector_step(
        row_params,
        new_mom_params,
        jnp.mean(new_mom_params * new_mom_params, axis=-1, keepdims=True),
    )
    return (
        output_rows,
        grad_inputs,
        new_mom_qkv, new_qkv, new_qkv.astype(BF),
        new_mom_out, new_out, new_out.astype(BF),
        new_mom_up, new_up, new_up.astype(BF),
        new_mom_down, new_down, new_down.astype(BF),
        new_mom_heads, new_heads,
        new_mom_ff, new_ff,
        new_mom_params, new_params,
    )


def solution(mesh):
    placed = (
        P("dp", None), P("dp", None), P("dp", None),
        P(None, None, "tensor"), P("tensor", None), P(None, "tensor"), P("tensor", None),
        P(None, "tensor"), P("tensor"), P(),
        P(None, None, "tensor"), P("tensor", None), P(None, "tensor"), P("tensor", None),
        P(None, "tensor"), P("tensor"), P(),
    )
    triple = ((P(None, None, "tensor"),) * 3, (P("tensor", None),) * 3, (P(None, "tensor"),) * 3)
    return jax.shard_map(
        local,
        mesh=mesh,
        in_specs=placed,
        out_specs=(
            (P("dp", None), P("dp", None))
            + triple[0] + triple[1] + triple[2] + triple[1]
            + (P(None, "tensor"), P(None, "tensor"), P("tensor"), P("tensor"), P(), P())
        ),
        check_vma=False,
    )
```

```python
import functools
import math

import jax
import jax.numpy as jnp
from jax import lax
from jax.experimental import pallas as pl
from jax.experimental.pallas import tpu as pltpu
from jax.sharding import PartitionSpec as P

HD = 64
EPS_NORM = 1e-05
coef_a = 3.4445
coef_b = -4.775
coef_c = 2.0315
BF = jnp.bfloat16
F32 = jnp.float32
MESH = pl.DeviceIdType.MESH
SUBS = 2
PLACE = (1, 2, 0, 3)
CUTS = 3


def remote(src, dst, send_sem, recv_sem, device):
    return pltpu.make_async_remote_copy(
        src_ref=src,
        dst_ref=dst,
        send_sem=send_sem,
        recv_sem=recv_sem,
        device_id=device,
        device_id_type=MESH,
    )


def greet(devices):
    barrier = pltpu.get_barrier_semaphore()
    for device in devices:
        pl.semaphore_signal(barrier, inc=1, device_id=device, device_id_type=MESH)
    pl.semaphore_wait(barrier, len(devices))


def z_peers(t):
    return [{"tensor": (t + k) % 4} for k in range(1, 4)]


def line_scratch(rows, width, dtype):
    part = rows // 4
    return [
        pltpu.VMEM((part, width), dtype),
        pltpu.VMEM((part, width), dtype),
        pltpu.VMEM((2 * part, width), dtype),
        pltpu.VMEM((2 * part, width), dtype),
        pltpu.SemaphoreType.DMA((8 * SUBS,)),
        pltpu.SemaphoreType.DMA((8 * SUBS,)),
    ]


def line_sum(t, x, o, scratch):
    raw, cmb, fwd, mix, ssem, rsem = scratch
    part = raw.shape[0]
    half = part // SUBS
    subs = range(SUBS)
    mate = t + 1 - 2 * (t % 2)
    outer = (t % 3) == 0
    inner = (t % 3) != 0

    def at(ref, chunk, s):
        return ref.at[pl.ds(pl.multiple_of(chunk * part + s * half, half), half)]

    def to(index, src, dst, recv, device):
        return remote(src, dst, ssem.at[index], rsem.at[recv], {"tensor": device})

    def ag_sem(chunk, s):
        return (4 + chunk) * SUBS + s

    def o_far(s):
        return to(s, at(x, 3 - t, s), at(fwd, 0, s), 2 * SUBS + s, mate)

    def o_near(s):
        return to(SUBS + s, at(x, 3 - mate, s), at(fwd, 1, s), 3 * SUBS + s, mate)

    def o_raw(s):
        return to(2 * SUBS + s, at(x, mate, s), at(raw, 0, s), s, mate)

    def o_own(s):
        return to(3 * SUBS + s, at(o, t, s), at(o, t, s), ag_sem(t, s), mate)

    def i_raw(s):
        return to(s, at(x, mate, s), at(raw, 0, s), s, mate)

    def i_far(s):
        return to(SUBS + s, at(mix, 0, s), at(cmb, 0, s), SUBS + s, 3 - mate)

    def i_near(s):
        return to(2 * SUBS + s, at(mix, 1, s), at(cmb, 0, s), SUBS + s, 3 - t)

    def i_ag(place, chunk, s, device):
        return to(place * SUBS + s, at(o, chunk, s), at(o, chunk, s), ag_sem(chunk, s), device)

    def got(dst, recv):
        remote(dst, dst, ssem.at[0], rsem.at[recv], {"tensor": mate}).wait_recv()

    def add(dst, *terms):
        total = terms[0][...].astype(F32)
        for term in terms[1:]:
            total = total + term[...].astype(F32)
        dst[...] = total.astype(dst.dtype)

    def start():
        @pl.when(outer)
        def _():
            for build in (o_far, o_near, o_raw):
                for s in subs:
                    build(s).start()

        @pl.when(inner)
        def _():
            for s in subs:
                i_raw(s).start()

    def combine():
        @pl.when(inner)
        def _():
            for slot, chunk, build in ((0, 3 - mate, i_far), (1, 3 - t, i_near)):
                for s in subs:
                    got(at(fwd, slot, s), (2 + slot) * SUBS + s)
                    add(at(mix, slot, s), at(fwd, slot, s), at(x, chunk, s))
                    build(s).start()

    def settle():
        for s in subs:
            got(at(raw, 0, s), s)
            got(at(cmb, 0, s), SUBS + s)
            add(at(o, t, s), at(x, t, s), at(raw, 0, s), at(cmb, 0, s))

            @pl.when(outer)
            def _(s=s):
                o_own(s).start()

            @pl.when(inner)
            def _(s=s):
                i_ag(3, t, s, 3 - t).start()
                i_ag(4, t, s, mate).start()

    def pass_on():
        @pl.when(inner)
        def _():
            for s in subs:
                got(at(o, mate, s), ag_sem(mate, s))
                i_ag(5, mate, s, 3 - t).start()
            for s in subs:
                got(at(o, 3 - t, s), ag_sem(3 - t, s))
                i_ag(6, 3 - t, s, mate).start()
            for s in subs:
                got(at(o, 3 - mate, s), ag_sem(3 - mate, s))
                i_ag(7, 3 - mate, s, mate).start()

    def finish():
        @pl.when(outer)
        def _():
            for chunk in (mate, 3 - mate, 3 - t):
                for s in subs:
                    got(at(o, chunk, s), ag_sem(chunk, s))
            for build in (o_far, o_near, o_raw, o_own):
                for s in subs:
                    build(s).wait_send()

        @pl.when(inner)
        def _():
            for s in subs:
                for build in (i_raw, i_far, i_near):
                    build(s).wait_send()
                i_ag(3, t, s, 3 - t).wait_send()
                i_ag(4, t, s, mate).wait_send()
                i_ag(5, mate, s, 3 - t).wait_send()
                i_ag(6, 3 - t, s, mate).wait_send()
                i_ag(7, 3 - mate, s, mate).wait_send()

    return [start, combine, settle, pass_on, finish]


def relay_scratch(rows, width, dtype):
    part = rows // 2
    return [
        pltpu.VMEM((2 * part, width), dtype),
        pltpu.VMEM((part, width), dtype),
        pltpu.VMEM((part, width), dtype),
        pltpu.SemaphoreType.DMA((5 * SUBS,)),
        pltpu.SemaphoreType.DMA((5 * SUBS,)),
    ]


def relay_sum(t, x, o, scratch):
    taken, mixed, mix, ssem, rsem = scratch
    part = mixed.shape[0]
    piece = part // SUBS
    subs = range(SUBS)
    mate = t + 1 - 2 * (t % 2)
    facing = 3 - t
    outer = (t % 3) == 0
    inner = (t % 3) != 0
    near = t // 2
    far = 1 - near

    def at(ref, chunk, s):
        return ref.at[pl.ds(pl.multiple_of(chunk * part + s * piece, piece), piece)]

    def to(index, src, dst, recv, device):
        return remote(
            src, dst, ssem.at[index], rsem.at[recv], {"tensor": device}
        )

    def give_far(s):
        return to(s, at(x, far, s), at(taken, 0, s), s, mate)

    def give_near(s):
        return to(SUBS + s, at(x, near, s), at(taken, 1, s), SUBS + s, mate)

    def cross(s):
        return to(s, at(mix, 0, s), at(mixed, 0, s), 2 * SUBS + s, facing)

    def own_across(s):
        return to(SUBS + s, at(o, near, s), at(o, near, s), (3 + near) * SUBS + s, facing)

    def own_out(s):
        return to(2 * SUBS + s, at(o, near, s), at(o, near, s), (3 + near) * SUBS + s, mate)

    def far_out(s):
        return to(3 * SUBS + s, at(o, far, s), at(o, far, s), (3 + far) * SUBS + s, mate)

    def got(dst, recv):
        remote(dst, dst, ssem.at[0], rsem.at[recv], {"tensor": mate}).wait_recv()

    def add(dst, *terms):
        total = terms[0][...].astype(F32)
        for term in terms[1:]:
            total = total + term[...].astype(F32)
        dst[...] = total.astype(dst.dtype)

    def start():
        @pl.when(outer)
        def _():
            for build in (give_far, give_near):
                for s in subs:
                    build(s).start()

    def combine():
        @pl.when(inner)
        def _():
            for s in subs:
                got(at(taken, 0, s), s)
                add(at(mix, 0, s), at(taken, 0, s), at(x, far, s))
                cross(s).start()

    def settle():
        @pl.when(inner)
        def _():
            for s in subs:
                got(at(taken, 1, s), SUBS + s)
                got(at(mixed, 0, s), 2 * SUBS + s)
                add(at(o, near, s), at(x, near, s), at(taken, 1, s), at(mixed, 0, s))
                own_across(s).start()
                own_out(s).start()

    def pass_on():
        @pl.when(inner)
        def _():
            for s in subs:
                got(at(o, far, s), (3 + far) * SUBS + s)
                far_out(s).start()

    def finish():
        @pl.when(outer)
        def _():
            for chunk in (near, far):
                for s in subs:
                    got(at(o, chunk, s), (3 + chunk) * SUBS + s)
            for build in (give_far, give_near):
                for s in subs:
                    build(s).wait_send()

        @pl.when(inner)
        def _():
            for build in (cross, own_across, own_out, far_out):
                for s in subs:
                    build(s).wait_send()

    return [start, combine, settle, pass_on, finish]


def params(collective_id, mebibytes):
    return pltpu.CompilerParams(
        collective_id=collective_id,
        has_side_effects=True,
        vmem_limit_bytes=mebibytes * 1024 * 1024,
    )


IN_VMEM = pl.BlockSpec(memory_space=pltpu.VMEM)
IN_HBM = pl.BlockSpec(memory_space=pltpu.HBM)


def plane_scratch(count, rows, width):
    pairs = count // 2
    side = width // 2
    block = rows // pairs
    return [
        pltpu.VMEM((rows, side), BF),
        pltpu.VMEM((rows, side), BF),
        pltpu.VMEM((pairs, block, side), BF),
        pltpu.SemaphoreType.DMA((5, pairs)),
        pltpu.SemaphoreType.DMA((4, pairs)),
    ]


def plane_sum(count, p, x, o, scratch):
    from_mate, paired, slots, ssem, rsem = scratch
    pairs = count // 2
    side = from_mate.shape[1]
    block = slots.shape[1]
    pair = p // 2
    core = p % 2
    mate = {"dp": p + 1 - 2 * core}

    def rows_of(index):
        return pl.ds(pl.multiple_of(index * block, block), block)

    def cols_of(which):
        return pl.ds(pl.multiple_of(which * side, side), side)

    def after(k):
        return (pair + k) % pairs

    def before(k):
        return (pair + pairs - k) % pairs

    def give(k):
        spot = rows_of(after(k))
        return remote(
            x.at[spot, cols_of(1 - core)], from_mate.at[spot], ssem.at[0, k % pairs], rsem.at[0, k % pairs], mate
        )

    def hand(k):
        spot = rows_of(after(k))
        return remote(
            paired.at[spot], slots.at[k], ssem.at[1, k], rsem.at[1, k], {"dp": 2 * after(k) + core}
        )

    def spread(k):
        spot = o.at[rows_of(pair), cols_of(core)]
        return remote(spot, spot, ssem.at[2, k], rsem.at[2, k], {"dp": 2 * after(k) + core})

    def share(k):
        spot = o.at[rows_of(before(k)), cols_of(core)]
        return remote(spot, spot, ssem.at[3, k], rsem.at[3, k], mate)

    def start():
        for k in range(1, pairs + 1):
            give(k).start()

    def pair_up():
        for k in range(1, pairs + 1):
            spot = rows_of(after(k))
            give(k).wait_recv()
            total = x[spot, cols_of(core)].astype(F32) + from_mate[spot].astype(F32)
            paired[spot] = total.astype(BF)
            if k < pairs:
                hand(k).start()

    def settle():
        spot = rows_of(pair)
        total = paired[spot].astype(F32)
        for k in range(1, pairs):
            hand(k).wait_recv()
            total = total + slots[k].astype(F32)
        o[spot, cols_of(core)] = total.astype(BF)
        for k in range(1, pairs):
            spread(k).start()
        share(0).start()

    def pass_on():
        for k in range(1, pairs):
            spot = o.at[rows_of(before(k)), cols_of(core)]
            remote(spot, spot, ssem.at[2, k], rsem.at[2, k], mate).wait_recv()
            share(k).start()

    def finish():
        for k in range(pairs):
            spot = o.at[rows_of(before(k)), cols_of(1 - core)]
            remote(spot, spot, ssem.at[3, k], rsem.at[3, k], mate).wait_recv()
        for k in range(1, pairs + 1):
            give(k).wait_send()
        for k in range(1, pairs):
            hand(k).wait_send()
            spread(k).wait_send()
        for k in range(pairs):
            share(k).wait_send()

    return [start, pair_up, settle, pass_on, finish]


def reduce_scratch(rows, width):
    side = width // 2
    return [
        pltpu.VMEM((rows, side), BF),
        pltpu.VMEM((rows, side), BF),
        pltpu.VMEM((2 * rows, side), BF),
        pltpu.SemaphoreType.DMA((2, 8)),
        pltpu.SemaphoreType.DMA((2, 8)),
    ]


def square_reduce(p, x, kept, matrices, scratch):
    from_mate, paired, taken, ssem, rsem = scratch
    side = from_mate.shape[1]
    pair = p // 2
    core = p % 2
    mate = {"dp": p + 1 - 2 * core}

    def away_from(place, away):
        return {"dp": 2 * (place ^ away) + core}

    def cols_of(which):
        return pl.ds(pl.multiple_of(which * side, side), side)

    def give(m):
        _, first, rows = matrices[m]
        spot = pl.ds(first, rows)
        return remote(x.at[spot, cols_of(1 - core)], from_mate.at[spot], ssem.at[m, 0], rsem.at[m, 0], mate)

    def part_of(m, part):
        _, first, rows = matrices[m]
        return pl.ds(first + part * (rows // 2), rows // 2)

    def slot(m, near, part):
        _, first, rows = matrices[m]
        return pl.ds(2 * first + near * rows + part * (rows // 2), rows // 2)

    def opposite_send(m, part):
        place = matrices[m][0]
        return remote(
            paired.at[part_of(m, part)], taken.at[slot(m, 0, part)],
            ssem.at[m, 1 + part], rsem.at[m, 1], away_from(place, 1 + part),
        )

    def near_raw(m, near):
        part = 1 - near
        return remote(
            paired.at[part_of(m, part)], taken.at[slot(m, near, part)],
            ssem.at[m, 1], rsem.at[m, 2 + 2 * near], away_from(matrices[m][0], 0),
        )

    def near_mixed(m, near):
        part = near
        return remote(
            paired.at[part_of(m, part)], taken.at[slot(m, near, part)],
            ssem.at[m, 2], rsem.at[m, 3 + 2 * near], away_from(matrices[m][0], 0),
        )

    def swap(m):
        spot = kept.at[pl.ds(0, matrices[m][2]), cols_of(core)]
        return remote(spot, spot, ssem.at[m, 6], rsem.at[m, 6], mate)

    def arrived(ref, m, index):
        remote(ref, ref, ssem.at[m, 0], rsem.at[m, index], mate).wait_recv()

    def role(m, away):
        return pl.when(pair == (matrices[m][0] ^ away))

    every = range(len(matrices))

    def start():
        for m in every:
            give(m).start()

    def pair_up():
        for m in every:
            _, first, rows = matrices[m]
            spot = pl.ds(first, rows)
            give(m).wait_recv()
            total = x[spot, cols_of(core)].astype(F32) + from_mate[spot].astype(F32)
            paired[spot] = total.astype(BF)

            @role(m, 3)
            def _(m=m):
                for part in range(2):
                    opposite_send(m, part).start()

            for near in range(2):

                @role(m, 1 + near)
                def _(m=m, near=near):
                    near_raw(m, near).start()

    def mix():
        for m in every:
            for near in range(2):

                @role(m, 1 + near)
                def _(m=m, near=near):
                    piece = slot(m, 0, near)
                    arrived(taken.at[piece], m, 1)
                    spot = part_of(m, near)
                    total = paired[spot].astype(F32) + taken[piece].astype(F32)
                    paired[spot] = total.astype(BF)
                    near_mixed(m, near).start()

    def settle():
        for m in every:

            @role(m, 0)
            def _(m=m):
                _, first, rows = matrices[m]
                for near in range(2):
                    arrived(taken.at[slot(m, near, 1 - near)], m, 2 + 2 * near)
                    arrived(taken.at[slot(m, near, near)], m, 3 + 2 * near)
                spot = pl.ds(first, rows)
                total = x[spot, cols_of(core)].astype(F32) + from_mate[spot].astype(F32)
                for near in range(2):
                    total = total + taken[pl.ds(2 * first + near * rows, rows)].astype(F32)
                kept[pl.ds(0, rows), cols_of(core)] = total.astype(BF)
                swap(m).start()

    def finish():
        for m in every:
            rows = matrices[m][2]
            give(m).wait_send()

            @role(m, 0)
            def _(m=m, rows=rows):
                arrived(kept.at[pl.ds(0, rows), cols_of(1 - core)], m, 6)
                swap(m).wait_send()

            @role(m, 3)
            def _(m=m):
                for part in range(2):
                    opposite_send(m, part).wait_send()

            for near in range(2):

                @role(m, 1 + near)
                def _(m=m, near=near):
                    near_raw(m, near).wait_send()
                    near_mixed(m, near).wait_send()

    return [start, pair_up, mix, settle, finish]


def gather_scratch():
    return [pltpu.SemaphoreType.DMA((4, 2 * CUTS, 4))] * 2


def square_gather(p, sizes, out, own, cuts, scratch):
    ssem, rsem = scratch
    width = out.shape[1]
    pair = p // 2
    core = p % 2
    mate = {"dp": p + 1 - 2 * core}
    firsts = [sum(sizes[:index]) for index in range(4)]

    def piece(index, side, part):
        rows = sizes[index]
        if index == 2:
            across = pl.ds(pl.multiple_of(side * (width // 2), width // 2), width // 2)
            share = rows // (2 * cuts)
            return out.at[pl.ds(firsts[index] + part * share, share), across]
        share = rows // (4 * cuts)
        first = firsts[index] + side * (rows // 2) + part * share
        return out.at[pl.ds(pl.multiple_of(first, share), share)]

    def copy(index, part, route, device):
        spot = piece(index, core, part)
        return remote(spot, spot, ssem.at[index, part, route], rsem.at[index, part, route], device)

    def other(away):
        return {"dp": 2 * (pair + away * (1 - 2 * ((pair // away) % 2))) + core}

    def role(index, away):
        return pl.when(pair == (PLACE[index] ^ away))

    def wait_in(index, part, route, side):
        spot = piece(index, side, part)
        remote(spot, spot, ssem.at[index, part, route], rsem.at[index, part, route], mate).wait_recv()

    ways = ((1, 0, 2), (2, 1, 1))
    parts = 2 * cuts

    def half(which):
        return range(which * cuts, (which + 1) * cuts)

    def start():
        for index in range(4):

            @role(index, 0)
            def _(index=index):
                for part in range(parts):
                    piece(index, core, part)[...] = own(index, part)
                for part in range(parts):
                    copy(index, part, 0, other(1)).start()
                    copy(index, (part + cuts) % parts, 1, other(2)).start()
                for part in range(parts):
                    copy(index, part, 3, mate).start()

    def pass_on(indices=range(4)):
        for index in indices:
            for away, route, onward in ways:

                @role(index, away)
                def _(index=index, away=away, route=route, onward=onward):
                    for part in half(away - 1):
                        wait_in(index, part, route, core)
                        copy(index, part, 2, other(onward)).start()
                        copy(index, part, 3, mate).start()

    def rest():
        for index in range(4):
            for away, route, _ in ways:

                @role(index, away)
                def _(index=index, away=away, route=route):
                    for part in half(2 - away):
                        wait_in(index, part, route, core)
                        copy(index, part, 3, mate).start()

            @role(index, 3)
            def _(index=index):
                for part in [part // 2 + cuts * (part % 2) for part in range(parts)]:
                    wait_in(index, part, 2, core)
                    copy(index, part, 3, mate).start()

    def finish():
        for index in range(4):
            for part in range(parts):
                wait_in(index, part, 3, 1 - core)
                copy(index, part, 3, mate).wait_send()

            @role(index, 0)
            def _(index=index):
                for part in range(parts):
                    copy(index, part, 0, other(1)).wait_send()
                    copy(index, part, 1, other(2)).wait_send()

            for away, _, onward in ways:

                @role(index, away)
                def _(index=index, away=away, onward=onward):
                    for part in half(away - 1):
                        copy(index, part, 2, other(onward)).wait_send()

    return [start, pass_on, rest, finish]


def vector_scratch(count, shape):
    return [
        pltpu.VMEM((count,) + shape, F32),
        pltpu.SemaphoreType.DMA((count,)),
        pltpu.SemaphoreType.DMA((count,)),
    ]


def vector_sum(axis, count, p, v, o, scratch):
    slots, ssem, rsem = scratch

    def send(k):
        return remote(v, slots.at[p], ssem.at[k], rsem.at[k], {axis: (p + k) % count})

    def start():
        slots[p] = v[...]
        for k in range(1, count):
            send(k).start()

    def finish():
        for k in range(1, count):
            spot = slots.at[(p + count - k) % count]
            remote(v, spot, ssem.at[k], rsem.at[k], {axis: (p + k) % count}).wait_recv()
        total = slots[0]
        for k in range(1, count):
            total = total + slots[k]
        o[...] = total
        for k in range(1, count):
            send(k).wait_send()

    return [start, finish]


ROW_STEP = 32


def tdot(left, right):
    return lax.dot_general(left, right, (((0,), (0,)), ((), ())), preferred_element_type=F32)


def dot(left, right):
    return jnp.dot(left, right, preferred_element_type=F32)


def dot_t(left, right):
    return lax.dot_general(left, right, (((1,), (1,)), ((), ())), preferred_element_type=F32)


def cut(values):
    high = values.astype(BF)
    return high, (values - high.astype(F32)).astype(BF)


def dot3(lh, ll, rh, rl, dims=(((1,), (0,)), ((), ()))):
    def dot(left, right):
        return lax.dot_general(left, right, dims, preferred_element_type=F32)

    return dot(lh, rh) + (dot(lh, rl) + dot(ll, rh))


def step_kernel(
    count, sizes,
    seg, rp, hb, fb, mh, mf, x_hbm, cot_hbm, wq_hbm, wo_hbm, wu_hbm, wd_hbm, mq, mo, mu, md,
    y_hbm, gt_hbm, xo_hbm, gall_hbm, vec, totals,
    y, gt, xo, gall, x, cot, f1, f2, f3, f4, wo_f, gx, go, gp, dz1, b1, b2, b3, b4, b5, b6, b7, b8, bt, red_s, kept,
    gap, gbp, wq, wo, q_s, k_s, v_s, ctx_s, dq_s, dk_s, dv_s, p_s, inv1_s, vecp, squares,
    wsem, lsem, psem, osem, *scratch,
):
    p = lax.axis_index("dp")
    t = lax.axis_index("tensor")
    tokens, width = x.shape
    half = tokens // 2
    quarter = tokens // 4
    columns = q_s.shape[1]
    heads = columns // HD
    tile = width // 3
    scale = 1.0 / math.sqrt(HD)
    square = count == 8
    group = count // 4
    share = width // group
    which = p // group
    core = p % 2
    mate = {"dp": p + 1 - 2 * core}
    firsts = [sum(sizes[:index]) for index in range(4)]
    n1_s, slope_s, dz2_s, u_s = (ref.at[pl.ds(0, tokens)] for ref in (f3, f1, f2, f4))
    h1l_s, act_s, du_s, dm_s, da_s, part_s = (
        ref.at[pl.ds(0, tokens)] for ref in (b3, b4, b5, b6, b7, b8)
    )
    wu, wd = b1, b2
    zf, af, sf, xf = f3, f1, f2, f4.at[pl.ds(0, share)]
    ah, al, zh, zl, dh, dl, sh, sl = b1, b2, b3, b4, b5, b6, b7, b8
    gf = kept if square else gall
    loads = [
        pltpu.make_async_copy(source, target, wsem.at[i])
        for i, (source, target) in enumerate(
            (
                (wq_hbm, f4), (wo_hbm, wo_f), (wu_hbm, f1), (wd_hbm, f2),
                (x_hbm, x), (cot_hbm, cot),
            )
        )
    ]
    for place in (0, 4, 1, 2, 3, 5):
        loads[place].start()
    greet(z_peers(t) + [{"dp": (p + k) % count} for k in range(1, count)])
    sums, back = [], []
    for q in range(4):
        place = pl.ds(q * quarter, quarter)
        pieces = scratch[5 * q : 5 * q + 5]
        sums.append(relay_sum(t, part_s.at[place], red_s.at[place], pieces))
        back.append(relay_sum(t, bt.at[place], red_s.at[place], pieces))
    top = 4 * columns
    if square:
        ends = [(PLACE[2], 0, width), (PLACE[3], width, width)]
        plane_b = square_reduce(p, gbp, kept, ends, scratch[20:25])
        ends = [(PLACE[0], 0, 3 * columns), (PLACE[1], 3 * columns, columns)]
        plane_a = square_reduce(p, gap, kept, ends, scratch[25:30])
    else:
        plane_b = plane_sum(count, p, gbp, gall.at[pl.ds(top, 2 * width)], scratch[20:25])
        plane_a = plane_sum(count, p, gap, gall.at[pl.ds(0, top)], scratch[25:30])
    vector = vector_sum("dp", count, p, vecp, vec, scratch[30:33])
    along = vector_sum("tensor", 4, t, squares, totals, scratch[33:36])
    line = line_sum(t, gx, go, scratch[36:42])
    vecp[...] = jnp.zeros_like(vecp)
    lane = lax.broadcasted_iota(jnp.int32, (1, columns), 1)

    def in_head(index):
        return (lane // HD) == index

    def rows_of(h):
        return pl.ds(h * half, half)

    def quarter_of(q):
        return pl.ds(q * quarter, quarter)

    def over_rows(q, body, init=0):
        def step(i, carry):
            first = q * quarter + i * ROW_STEP
            return body(pl.ds(pl.multiple_of(first, ROW_STEP), ROW_STEP), carry)

        return lax.fori_loop(0, quarter // ROW_STEP, step, init)

    def fold(values):
        return values.reshape(ROW_STEP // 8, 8, values.shape[1]).sum(axis=0)

    def add_vec(row, folded):
        vecp[row : row + 1, 0 : folded.shape[1]] += jnp.sum(folded, axis=0, keepdims=True)

    def narrow(index, source, target):
        loads[index].wait()
        target[...] = source[...].astype(BF)

    def attention(h):
        r = rows_of(h)
        xb = x[r]
        q = (dot_t(xb, wq[0 * columns : 1 * columns]) + hb[0:1]).astype(BF)
        k = dot_t(xb, wq[1 * columns : 2 * columns]).astype(BF)
        v = (dot_t(xb, wq[2 * columns : 3 * columns]) + hb[1:2]).astype(BF)
        q_s[r], k_s[r], v_s[r] = q, k, v
        down = jnp.broadcast_to(seg[h : h + 1].astype(F32), (half, half))
        same = down == down.T

        def one_head(index, context):
            mine = jnp.where(in_head(index), q, jnp.zeros_like(q))
            scores = jnp.where(same, dot_t(mine, k) * scale, -1e30)
            expo = jnp.exp(scores - jnp.max(scores, axis=-1, keepdims=True))
            probs = expo / jnp.sum(expo, axis=-1, keepdims=True)
            p_s[h * heads + index] = probs
            return jnp.where(in_head(index), dot(probs.astype(BF), v), context)

        context = lax.fori_loop(0, heads, one_head, jnp.zeros((half, columns), F32))
        low = context.astype(BF)
        ctx_s[r] = low
        part_s[r] = dot(low, wo[...]).astype(BF)

    def up(q):
        def norm(r, carry):
            z = x[r].astype(F32) + red_s[r].astype(F32) + rp[0:1]
            center = z - jnp.mean(z, axis=-1, keepdims=True)
            inverse = lax.rsqrt(jnp.mean(center * center, axis=-1, keepdims=True) + EPS_NORM)
            normed = center * inverse
            n1_s[r] = normed
            inv1_s[r] = jnp.broadcast_to(inverse, (ROW_STEP, 128))
            h1l_s[r] = (normed * rp[2:3] + rp[3:4]).astype(BF)
            return carry

        over_rows(q, norm)
        u_s[quarter_of(q)] = dot(h1l_s[quarter_of(q)], wu[...])

        def gelu(r, carry):
            u = u_s[r] + fb[...].reshape(1, width)
            cdf = 0.5 * (1.0 + lax.erf(u * (1.0 / math.sqrt(2.0))))
            act_s[r] = (u * cdf).astype(BF)
            slope_s[r] = cdf + u * jnp.exp(-0.5 * u * u) * (1.0 / math.sqrt(2.0 * math.pi))
            return carry

        over_rows(q, gelu)

    def down(q):
        r = quarter_of(q)
        part_s[r] = dot(act_s[r], wd[...]).astype(BF)

    def out_back(q):
        def norm(r, carry):
            s_dz2, s_dyn, s_dy = carry
            h1 = n1_s[r] * rp[2:3] + rp[3:4]
            z = h1 + red_s[r].astype(F32) + rp[1:2]
            center = z - jnp.mean(z, axis=-1, keepdims=True)
            inverse = lax.rsqrt(jnp.mean(center * center, axis=-1, keepdims=True) + EPS_NORM)
            normed = center * inverse
            y[r] = (normed * rp[4:5] + rp[5:6]).astype(BF)
            dy = cot[r].astype(F32)
            scaled = dy * rp[4:5]
            first = jnp.mean(scaled, axis=-1, keepdims=True)
            second = jnp.mean(scaled * normed, axis=-1, keepdims=True)
            dz2 = inverse * (scaled - first - normed * second)
            dz2_s[r] = dz2
            dm_s[r] = dz2.astype(BF)
            return s_dz2 + fold(dz2), s_dyn + fold(dy * normed), s_dy + fold(dy)

        zero = jnp.zeros((8, width), F32)
        for row, total in zip((1, 4, 5), over_rows(q, norm, (zero, zero, zero))):
            add_vec(row, total)
        u_s[quarter_of(q)] = dot_t(dm_s[quarter_of(q)], wd[...])

        def slope(r, carry):
            du = (u_s[r] * slope_s[r]).astype(BF)
            du_s[r] = du
            return carry + fold(du.astype(F32))

        add_vec(6, over_rows(q, slope, zero))

    def up_back(q):
        r = quarter_of(q)
        part_s[r] = dot_t(du_s[r], wu[...]).astype(BF)

    def grads_b():
        gbp[0:width] = tdot(h1l_s[...], du_s[...]).astype(BF)
        gbp[width : 2 * width] = tdot(act_s[...], dm_s[...]).astype(BF)

    def norm_back(q):
        def norm(r, carry):
            s_dz1, s_dhn, s_dh = carry
            dh1 = red_s[r].astype(F32) + dz2_s[r]
            normed = n1_s[r]
            scaled = dh1 * rp[2:3]
            first = jnp.mean(scaled, axis=-1, keepdims=True)
            second = jnp.mean(scaled * normed, axis=-1, keepdims=True)
            grad = inv1_s[r][:, 0:1] * (scaled - first - normed * second)
            dz1[r] = grad
            da_s[r] = grad.astype(BF)
            return s_dz1 + fold(grad), s_dhn + fold(dh1 * normed), s_dh + fold(dh1)

        zero = jnp.zeros((8, width), F32)
        for row, total in zip((0, 2, 3), over_rows(q, norm, (zero, zero, zero))):
            add_vec(row, total)

    def attention_back(h):
        r = rows_of(h)
        dc = dot_t(da_s[r], wo[...]).astype(BF)
        q, k, v = q_s[r], k_s[r], v_s[r]

        def one_head(index, carry):
            dq, dk, dv = carry
            probs = p_s[h * heads + index]
            mine = jnp.where(in_head(index), dc, jnp.zeros_like(dc))
            dp = dot_t(mine, v)
            ds = (probs * (dp - jnp.sum(probs * dp, axis=-1, keepdims=True))).astype(BF)
            dv = jnp.where(in_head(index), tdot(probs.astype(BF), dc), dv)
            dq = jnp.where(in_head(index), dot(ds, k), dq)
            dk = jnp.where(in_head(index), tdot(ds, q), dk)
            return dq, dk, dv

        dq, dk, dv = lax.fori_loop(0, heads, one_head, (jnp.zeros((half, columns), F32),) * 3)
        dq = (dq * scale).astype(BF)
        dk = (dk * scale).astype(BF)
        dv = dv.astype(BF)
        dq_s[r], dk_s[r], dv_s[r] = dq, dk, dv
        add_vec(7, jnp.sum(dq.astype(F32), axis=0, keepdims=True))
        add_vec(8, jnp.sum(dv.astype(F32), axis=0, keepdims=True))

    def grads_a():
        for i, source in enumerate((dq_s, dk_s, dv_s)):
            gap[i * columns : (i + 1) * columns] = tdot(source[...], x[...]).astype(BF)
        gap[3 * columns : 4 * columns] = tdot(ctx_s[...], da_s[...]).astype(BF)

    def back_terms(h):
        r = rows_of(h)
        total = dot(dq_s[r], wq[0 * columns : 1 * columns]) + dot(dk_s[r], wq[1 * columns : 2 * columns]) + dot(dv_s[r], wq[2 * columns : 3 * columns])
        bt[r] = total.astype(BF)

    def moment_copy(index):
        moment = (mq, mo, mu, md)[index]
        return pltpu.make_async_copy(moment, f1.at[pl.ds(0, sizes[index])], lsem.at[0])

    def fetch_moment():
        for index in range(4):
            pl.when(which == PLACE[index])(moment_copy(index).start)

    def cols(index):
        return pl.ds(pl.multiple_of(index * tile, tile), tile)

    def place_of(side, j):
        return side * (1 + j // 2), j + side * (1 - j // 2)

    def gram(indices):
        for index in indices:
            rows = sizes[index]
            first = 0 if square else firsts[index]

            @pl.when(which == PLACE[index])
            def _(index=index, first=first, rows=rows):
                moment_copy(index).wait()
                for i in range(3):
                    spot = pl.ds(i * (rows // 3), rows // 3)
                    z = 0.5 * f1[spot] + gf[pl.ds(first + i * (rows // 3), rows // 3)].astype(F32)
                    if index == 2:
                        z = z.T
                        spot = (pl.ds(0, width), spot)
                    zf[spot] = z
                    zh[spot], zl[spot] = cut(z)
                if rows < width:
                    spot = pl.ds(rows, width - rows)
                    zf[spot] = jnp.zeros((width - rows, width), F32)
                    zh[spot] = jnp.zeros((width - rows, width), BF)
                    zl[spot] = jnp.zeros((width - rows, width), BF)

        over = (((0,), (0,)), ((), ()))

        @pl.loop(0, 3)
        def _(j):
            row, col = place_of(core, j)
            gx[:, cols(j)] = dot3(
                zh[:, cols(row)], zl[:, cols(row)], zh[:, cols(col)], zl[:, cols(col)], over
            )

    diagonal = lax.broadcasted_iota(jnp.int32, (tile, tile), 0) == lax.broadcasted_iota(
        jnp.int32, (tile, tile), 1
    )

    def upper():
        def trace(block):
            return jnp.sum(jnp.where(diagonal, block, 0.0))

        def write(rows, across, value):
            af[rows, across] = value
            ah[rows, across], al[rows, across] = cut(value)

        last = jnp.where(core == 1, go[:, 2 * tile :], gp[:, 2 * tile :])
        total = trace(go[:, 0:tile]) + trace(gp[:, 0:tile]) + trace(last)
        inverse = 1.0 / (jnp.sqrt(jnp.full((1, 1), total, F32)) + 1e-07)
        shrink = inverse * inverse
        for source, side in ((go, core), (gp, 1 - core)):
            for j in range(3):
                row, col = place_of(side, j)
                block = source[:, j * tile : (j + 1) * tile] * shrink
                write(cols(row), cols(col), block)
                if j > 0:
                    write(cols(col), cols(row), block.T)

        if square:
            for index, rows in enumerate(sizes):

                @pl.when(which == PLACE[index])
                def _(half_rows=rows // 2):
                    mine = pl.ds(pl.multiple_of(core * half_rows, half_rows), half_rows)
                    xf[0:half_rows] = zf[mine] * inverse
                    if half_rows < share:
                        xf[half_rows:share] = jnp.zeros((share - half_rows, width), F32)

        else:
            rank = p % group
            xf[...] = zf[pl.ds(pl.multiple_of(rank * share, share), share)] * inverse

    def product(left, right, base, base_scale, factor, targets, times):
        (lh, ll), (rh, rl) = left, right
        for i in range(3):
            rows = pl.ds(i * tile, tile)
            for j in range(i, 3):
                across = pl.ds(j * tile, tile)
                value = base_scale * base[rows, across] + factor * times(
                    lh[rows], ll[rows], rh[:, across], rl[:, across]
                )
                parts = (*cut(value), value)
                for target, part in zip(targets, parts):
                    target[rows, across] = part
                if i != j and len(targets) == 2:
                    for target, part in zip(targets, parts):
                        target[across, rows] = part.T
                elif i != j:
                    mirrored = value.T
                    for target, part in zip(targets, (*cut(mirrored), mirrored)):
                        target[across, rows] = part

    def make_d(times=dot3):
        product((ah, al), (ah, al), af, coef_b, coef_c, (dh, dl), times)

    def move_x(times=dot3):
        xh, xl = cut(xf[...])
        xf[...] = coef_a * xf[...] + times(xh, xl, dh[...], dl[...])

    def own_gradient(index, part):
        if index == 2:
            across = pl.ds(pl.multiple_of(core * (width // 2), width // 2), width // 2)
            piece = sizes[index] // (2)
            return gf[pl.ds(part * piece, piece), across]
        piece = sizes[index] // (4)
        first = pl.multiple_of(core * (sizes[index] // 2) + part * piece, piece)
        return gf[pl.ds(first, piece)]

    def own_step(index, part):
        if index == 2:
            piece = sizes[index] // (2 * CUTS)
            return xf[:, pl.ds(part * piece, piece)].T.astype(BF)
        piece = sizes[index] // (4 * CUTS)
        return xf[pl.ds(part * piece, piece)].astype(BF)

    if square:
        spread = square_gather(p, sizes, gall, own_gradient, 1, scratch[42:44])
        collect = square_gather(p, sizes, xo, own_step, CUTS, scratch[44:46])
        early = (which == PLACE[2]) | (which == PLACE[3])
        late = (which == PLACE[0]) | (which == PLACE[1])

    start, mix, settle, pass_on, end = (
        (lambda q, place=place: sums[q][place]()) for place in range(5)
    )

    def round_trip(first, second):
        end(0), first(0), pass_on(1), second(0), settle(2), mix(3), start(0)
        end(1), first(1), pass_on(2), settle(3), second(1), mix(0), start(1)
        end(2), first(2), pass_on(3), second(2), settle(0), mix(1), start(2)
        end(3), first(3), pass_on(0), second(3), settle(1), mix(2), start(3)

    loads[4].wait()
    narrow(0, f4, wq)
    narrow(1, wo_f, wo)
    attention(0)
    start(0), start(1)
    attention(1)
    mix(0), start(2), mix(1), settle(0), start(3)
    narrow(2, f1, wu)
    mix(2), settle(1), pass_on(0)
    narrow(3, f2, wd)
    loads[5].wait()
    outs = [
        pltpu.make_async_copy(source, target, osem.at[i])
        for i, (source, target) in enumerate(((y, y_hbm), (gt, gt_hbm), (gall, gall_hbm)))
    ]
    round_trip(up, down)
    round_trip(out_back, up_back)
    outs[0].start()
    fetch_moment()
    grads_b()
    plane_b[0]()
    end(0), norm_back(0), pass_on(1), settle(2), mix(3)
    plane_b[1]()
    end(1), norm_back(1), pass_on(2), settle(3)
    attention_back(0)
    end(2), norm_back(2), pass_on(3)
    if square:
        plane_b[2]()
    end(3), norm_back(3)
    attention_back(1)
    grads_a()
    plane_a[0]()
    vector[0]()
    if square:
        plane_b[3]()
        plane_a[1]()

        @pl.when(early)
        def _():
            plane_b[4]()
            gram((2, 3))
            line[0]()

        plane_a[2]()
        back_terms(0)
        back_terms(1)

        @pl.when(late)
        def _():
            plane_a[3]()
            plane_b[4]()
            plane_a[4]()
            gram((0, 1))
            line[0]()
            spread[0]()

    else:
        plane_b[2]()
        plane_a[1]()
        back_terms(0)
        back_terms(1)
        plane_b[3]()
        plane_a[2]()
        plane_b[4]()
        plane_a[3]()
        plane_a[4]()
        gram(range(4))
        line[0]()
    vector[1]()
    moved = 0.5 * mh[...] + vec[7:9, 0:columns]
    squares[0:2] = jnp.broadcast_to(jnp.sum(moved * moved, axis=1, keepdims=True), (2, 128))
    moved = 0.5 * mf[...].reshape(1, width) + vec[6:7]
    squares[2:3] = jnp.broadcast_to(jnp.sum(moved * moved, axis=1, keepdims=True), (1, 128))
    squares[3:8] = jnp.zeros((5, 128), F32)
    along[0]()
    if square:
        pl.when(early)(spread[0])
    for place in range(1, 5):
        line[place]()
        if square and place == 2:
            spread[1]()
    swap = remote(go, gp, psem.at[0], psem.at[1], mate)
    swap.start()
    for q in range(2):
        back[q][0]()
    swap.wait()

    upper()

    def one_pass(lh, ll, rh, rl):
        return dot(lh, rh)

    plan = {
        (0, 1): ((1, 0),),
        (0, 2): ((1, 1), (0, 2)),
        (1, 0): ((2, 0), (0, 3)),
        (1, 1): ((2, 1), (1, 2)),
        (1, 2): ((3, 0), (1, 3)),
        (2, 1): ((3, 1), (2, 2)),
        (2, 2): ((2, 3),),
        (3, 0): ((3, 2),),
        (3, 1): ((3, 3),),
    }

    def between(k, place):
        for turn in range(4):
            actions = plan.get((turn, place), ())
            if actions:

                @pl.when(k == turn)
                def _(turn=turn, actions=actions):
                    for action, q in actions:
                        back[q][action]()
                    if square and (turn, place) == (1, 2):
                        spread[2]()

    def sweep(k, carry):
        make_d()
        xh, xl = cut(xf[...])
        xf[...] = coef_a * xf[...] + dot(xh, dh[...])

        @pl.when(k == 3)
        def _():
            xf[...] += dot(xh, dl[...]) + dot(xl, dh[...])

        between(k, 0)
        product((ah, al), (dh, dl), af, coef_a, 1.0, (sh, sl, sf), dot3)
        between(k, 1)
        product((sh, sl), (dh, dl), sf, coef_a, 1.0, (ah, al, af), dot3)
        between(k, 2)
        return carry

    lax.fori_loop(0, 4, sweep, 0)
    if square:
        collect[1]((2, 3))
    make_d()
    move_x()
    for q in range(4):
        back[q][4]()
    gt[...] = (red_s[...].astype(F32) + dz1[...]).astype(BF)
    outs[1].start()
    along[1]()
    if square:

        @pl.when(early)
        def _():
            plane_a[4]()

        collect[0]()
        collect[1]((0, 1))
        spread[3]()
        outs[2].start()
        collect[2]()
        collect[3]()
    else:
        outs[2].start()
        gather_any(p, core, count // 2, mate, xf, xo, scratch[42], scratch[43])
    last = pltpu.make_async_copy(xo, xo_hbm, osem.at[3])
    last.start()
    for moving in (*outs, last):
        moving.wait()


def gather_any(p, core, pairs, mate, xf, xo, asem_s, asem_r):
    pair = p // 2
    share = xf.shape[0]

    def rows_of(device):
        return xo.at[pl.ds(pl.multiple_of(device * share, share), share)]

    def after(k):
        return 2 * ((pair + k) % pairs) + core

    def before(k):
        return 2 * ((pair + pairs - k) % pairs) + core

    def send(k):
        return remote(rows_of(p), rows_of(p), asem_s.at[0, k], asem_r.at[0, k], {"dp": after(k)})

    def hand(k):
        spot = rows_of(before(k))
        return remote(spot, spot, asem_s.at[1, k], asem_r.at[1, k], mate)

    xo[pl.ds(pl.multiple_of(p * share, share), share)] = xf[...].astype(BF)
    for k in range(1, pairs):
        send(k).start()
    hand(0).start()
    for k in range(1, pairs):
        spot = rows_of(before(k))
        remote(spot, spot, asem_s.at[0, k], asem_r.at[0, k], mate).wait_recv()
        hand(k).start()
    for k in range(pairs):
        spot = rows_of(before(k) + 1 - 2 * core)
        remote(spot, spot, asem_s.at[1, k], asem_r.at[1, k], mate).wait_recv()
    for k in range(1, pairs):
        send(k).wait_send()
    for k in range(pairs):
        hand(k).wait_send()


def step(count, tokens, cotangent, segments, small, weights, moments, collective_id):
    rows, width = tokens.shape
    sizes = tuple(moment.shape[0] for moment in moments)
    columns = sizes[1]
    heads = columns // HD
    half = rows // 2
    tile = width // 3
    square = count == 8

    def low(*shape):
        return pltpu.VMEM(shape, BF)

    def full(*shape):
        return pltpu.VMEM(shape, F32)

    def out(shape, dtype):
        return jax.ShapeDtypeStruct(shape, dtype)

    plane = reduce_scratch if square else functools.partial(plane_scratch, count)
    pair_sems = [pltpu.SemaphoreType.DMA((2, count // 2))] * 2
    steps_rows = sum(sizes) if square else 4 * width
    scratch = (
        [low(rows, width)] * 2
        + [low(steps_rows, width), low(sum(sizes), width)]
        + [low(rows, width)] * 2
        + [full(width, width)] * 3
        + [full(3 * columns, width), full(columns, width)]
        + [full(tile, width)] * 3
        + [full(rows, width)]
        + [low(width, width)] * 8
        + [low(rows, width)] * 2
        + [low(width, width) if square else low(16, width)]
        + [low(4 * columns, width), low(2 * width, width)]
        + [low(3 * columns, width), low(columns, width)]
        + [low(rows, columns)] * 7
        + [full(2 * heads, half, half), full(rows, 128), full(16, width), full(8, 128)]
        + [pltpu.SemaphoreType.DMA((n,)) for n in (6, 2, 2, 4)]
        + relay_scratch(rows // 4, width, BF) * 4
        + plane(2 * width, width)
        + plane(4 * columns, width)
        + vector_scratch(count, (16, width))
        + vector_scratch(4, (8, 128))
        + line_scratch(tile, width, F32)
        + (gather_scratch() * 2 if square else pair_sems)
    )
    return pl.pallas_call(
        functools.partial(step_kernel, count, sizes),
        out_shape=(
            out((rows, width), BF),
            out((rows, width), BF),
            out((steps_rows, width), BF),
            out((sum(sizes), width), BF),
            out((16, width), F32),
            out((8, 128), F32),
        ),
        in_specs=[IN_VMEM] * 6 + [IN_HBM] * 10,
        out_specs=(IN_HBM,) * 4 + (IN_VMEM,) * 2,
        scratch_shapes=scratch,
        compiler_params=params(collective_id, 61),
        name="step",
    )(segments, *small, tokens, cotangent, *weights, *moments)


def apply_kernel(factors, *refs):
    ins, outs = refs[:26], refs[26:]
    small_in, small_out = ins[18:], outs[14:]
    for index, factor in enumerate(factors):
        weight, moment, grad, step = (ins[4 * index + i] for i in range(4))
        new_moment, new, low = (outs[3 * index + i] for i in range(3))
        new_moment[...] = 0.5 * moment[...] + grad[...].astype(F32)
        value = weight[...] - factor * step[...].astype(F32)
        new[...] = value
        low[...] = value.astype(BF)
    for source, target in zip(ins[16:18], outs[12:14]):
        target[...] = source[...]

    @pl.when(pl.program_id(0) == 0)
    def _():
        vec, totals, heads, ff, rows, mom_heads, mom_ff, mom_rows = small_in
        columns = heads.shape[1]
        wide = ff.shape[0]
        moment = 0.5 * mom_heads[...] + vec[7:9, 0:columns]
        small_out[0][...] = moment
        scale = lax.rsqrt(totals[0:2, 0:1] * (1.0 / (4 * columns)) + 1e-06)
        small_out[1][...] = heads[...] - 0.1 * moment * scale
        moment = 0.5 * mom_ff[...].reshape(1, wide) + vec[6:7]
        small_out[2][...] = moment.reshape(wide)
        scale = lax.rsqrt(totals[2:3, 0:1] * (1.0 / (4 * wide)) + 1e-06)
        value = ff[...].reshape(1, wide) - 0.1 * moment * scale
        small_out[3][...] = value.reshape(wide)
        moment = 0.5 * mom_rows[...] + vec[0:6]
        small_out[4][...] = moment
        mean = jnp.mean(moment * moment, axis=-1, keepdims=True)
        small_out[5][...] = rows[...] - 0.1 * moment * lax.rsqrt(mean + 1e-06)


APPLY_STEPS = 4


def apply(sizes, factors, weights, moments, grads, steps, passed, small):
    width = grads.shape[1]
    in_specs, operands, out_specs, out_shape = [], [], [], []

    def block(rows, first=0):
        share = rows // APPLY_STEPS
        return pl.BlockSpec((share, width), lambda i, skip=first // share: (skip + i, 0))

    def whole(array):
        return pl.BlockSpec(array.shape, lambda i, n=array.ndim: (0,) * n)

    first = 0
    for rows, weight, moment in zip(sizes, weights, moments):
        in_specs += [block(rows), block(rows), block(rows, first), block(rows, first)]
        operands += [weight, moment, grads, steps]
        out_specs += [block(rows)] * 3
        out_shape += [jax.ShapeDtypeStruct((rows, width), kind) for kind in (F32, F32, BF)]
        first += rows
    for array in passed:
        turn = pl.BlockSpec((array.shape[0] // 4, width), lambda i: (i // (APPLY_STEPS // 4), 0))
        in_specs.append(turn)
        operands.append(array)
        out_specs.append(turn)
        out_shape.append(jax.ShapeDtypeStruct(array.shape, array.dtype))
    for array in small:
        in_specs.append(whole(array))
        operands.append(array)
    for array in small[2:5]:
        for _ in range(2):
            out_specs.append(whole(array))
            out_shape.append(jax.ShapeDtypeStruct(array.shape, F32))
    return pl.pallas_call(
        functools.partial(apply_kernel, factors),
        grid=(APPLY_STEPS,),
        out_shape=tuple(out_shape),
        in_specs=in_specs,
        out_specs=tuple(out_specs),
        compiler_params=pltpu.CompilerParams(vmem_limit_bytes=61 * 1024 * 1024),
        name="apply",
    )(*operands)


def vector_step(param, moment, mean_sq):
    return param - 0.1 * moment * lax.rsqrt(mean_sq + 1e-06)


def local(
    tokens, segments, cotangent,
    w_qkv, w_out, w_up, w_down, head_bias, ff_bias, row_params,
    mom_qkv, mom_out, mom_up, mom_down, mom_heads, mom_ff, mom_params,
):
    width = tokens.shape[1]
    columns = w_qkv.shape[2]
    ff_cols = w_up.shape[1]
    tensor_size = lax.axis_size("tensor")
    count = lax.axis_size("dp")
    qkv_rows = 3 * columns
    wq_rows = w_qkv.transpose(0, 2, 1).reshape(qkv_rows, width)
    moments = (mom_qkv.transpose(0, 2, 1).reshape(qkv_rows, width), mom_out, mom_up, mom_down)
    output_rows, grad_inputs, steps, grads, vector_total, totals = step(
        count, tokens, cotangent, segments, (row_params, head_bias, ff_bias, mom_heads, mom_ff),
        (wq_rows, w_out, w_up, w_down), moments, 1,
    )

    def to_qkv(rows):
        return rows.reshape(3, columns, width).transpose(0, 2, 1)

    bounds = (0, qkv_rows, qkv_rows + columns, qkv_rows + columns + width)

    def grad_of(index, rows):
        return grads[bounds[index] : bounds[index] + rows].astype(F32)

    def step_of(index, rows):
        first = PLACE[index] * width
        part = steps[first : first + rows].astype(F32)
        return part.T if index == 2 else part

    wide = math.sqrt(ff_cols * tensor_size / width)
    if count == 8:
        sizes = (qkv_rows, columns, width, ff_cols)
        factors = (0.8 * math.sqrt(3.0), 0.8, 0.8 * wide, 0.8 * wide)
        done = apply(
            sizes, factors, (wq_rows, w_out, w_up, w_down), moments, grads, steps, (output_rows, grad_inputs),
            (
                vector_total, totals, head_bias, ff_bias, row_params,
                mom_heads, mom_ff, mom_params,
            ),
        )
        qkv_new = [rows.reshape(3, columns, width).transpose(0, 2, 1) for rows in done[0:3]]
        return (
            *done[12:14], *qkv_new, *done[3:12], *done[14:20],
        )

    new_mom_heads = 0.5 * mom_heads + vector_total[7:9, :columns]
    new_mom_ff = 0.5 * mom_ff + vector_total[6]
    new_mom_params = 0.5 * mom_params + vector_total[0:6]
    new_mom_qkv = 0.5 * mom_qkv + to_qkv(grad_of(0, qkv_rows))
    new_mom_out = 0.5 * mom_out + grad_of(1, columns)
    new_mom_up = 0.5 * mom_up + grad_of(2, width)
    new_mom_down = 0.5 * mom_down + grad_of(3, ff_cols)
    new_qkv = w_qkv - 0.8 * math.sqrt(3.0) * to_qkv(step_of(0, qkv_rows))
    new_out = w_out - 0.8 * step_of(1, columns)
    new_up = w_up - 0.8 * wide * step_of(2, width)
    new_down = w_down - 0.8 * wide * step_of(3, ff_cols)
    new_heads = vector_step(head_bias, new_mom_heads, totals[0:2, 0:1] / (columns * tensor_size))
    new_ff = vector_step(ff_bias, new_mom_ff, totals[2, 0] / (ff_cols * tensor_size))
    new_params = vector_step(
        row_params,
        new_mom_params,
        jnp.mean(new_mom_params * new_mom_params, axis=-1, keepdims=True),
    )
    return (
        output_rows,
        grad_inputs,
        new_mom_qkv, new_qkv, new_qkv.astype(BF),
        new_mom_out, new_out, new_out.astype(BF),
        new_mom_up, new_up, new_up.astype(BF),
        new_mom_down, new_down, new_down.astype(BF),
        new_mom_heads, new_heads,
        new_mom_ff, new_ff,
        new_mom_params, new_params,
    )


def solution(mesh):
    placed = (
        P("dp", None), P("dp", None), P("dp", None),
        P(None, None, "tensor"), P("tensor", None), P(None, "tensor"), P("tensor", None),
        P(None, "tensor"), P("tensor"), P(),
        P(None, None, "tensor"), P("tensor", None), P(None, "tensor"), P("tensor", None),
        P(None, "tensor"), P("tensor"), P(),
    )
    triple = ((P(None, None, "tensor"),) * 3, (P("tensor", None),) * 3, (P(None, "tensor"),) * 3)
    return jax.shard_map(
        local,
        mesh=mesh,
        in_specs=placed,
        out_specs=(
            (P("dp", None), P("dp", None))
            + triple[0] + triple[1] + triple[2] + triple[1]
            + (P(None, "tensor"), P(None, "tensor"), P("tensor"), P("tensor"), P(), P())
        ),
        check_vma=False,
    )
```

```python
import functools
import math

import jax
import jax.numpy as jnp
from jax import lax
from jax.experimental import pallas as pl
from jax.experimental.pallas import tpu as pltpu
from jax.sharding import PartitionSpec as P

HD = 64
EPS_NORM = 1e-05
coef_a = 3.4445
coef_b = -4.775
coef_c = 2.0315
BF = jnp.bfloat16
F32 = jnp.float32
MESH = pl.DeviceIdType.MESH
SUBS = 2
PLACE = (1, 2, 0, 3)
CUTS = 3
LAST_FIRST = (2, 3, 1, 0)


def remote(src, dst, send_sem, recv_sem, device):
    return pltpu.make_async_remote_copy(
        src_ref=src,
        dst_ref=dst,
        send_sem=send_sem,
        recv_sem=recv_sem,
        device_id=device,
        device_id_type=MESH,
    )


def greet(devices):
    barrier = pltpu.get_barrier_semaphore()
    for device in devices:
        pl.semaphore_signal(barrier, inc=1, device_id=device, device_id_type=MESH)
    pl.semaphore_wait(barrier, len(devices))


def z_peers(t):
    return [{"tensor": (t + k) % 4} for k in range(1, 4)]


def line_scratch(rows, width, dtype):
    part = rows // 4
    return [
        pltpu.VMEM((part, width), dtype),
        pltpu.VMEM((part, width), dtype),
        pltpu.VMEM((2 * part, width), dtype),
        pltpu.VMEM((2 * part, width), dtype),
        pltpu.SemaphoreType.DMA((8 * SUBS,)),
        pltpu.SemaphoreType.DMA((8 * SUBS,)),
    ]


def line_sum(t, x, o, scratch):
    raw, cmb, fwd, mix, ssem, rsem = scratch
    part = raw.shape[0]
    half = part // SUBS
    subs = range(SUBS)
    mate = t + 1 - 2 * (t % 2)
    outer = (t % 3) == 0
    inner = (t % 3) != 0

    def at(ref, chunk, s):
        return ref.at[pl.ds(pl.multiple_of(chunk * part + s * half, half), half)]

    def to(index, src, dst, recv, device):
        return remote(src, dst, ssem.at[index], rsem.at[recv], {"tensor": device})

    def ag_sem(chunk, s):
        return (4 + chunk) * SUBS + s

    def o_far(s):
        return to(s, at(x, 3 - t, s), at(fwd, 0, s), 2 * SUBS + s, mate)

    def o_near(s):
        return to(SUBS + s, at(x, 3 - mate, s), at(fwd, 1, s), 3 * SUBS + s, mate)

    def o_raw(s):
        return to(2 * SUBS + s, at(x, mate, s), at(raw, 0, s), s, mate)

    def o_own(s):
        return to(3 * SUBS + s, at(o, t, s), at(o, t, s), ag_sem(t, s), mate)

    def i_raw(s):
        return to(s, at(x, mate, s), at(raw, 0, s), s, mate)

    def i_far(s):
        return to(SUBS + s, at(mix, 0, s), at(cmb, 0, s), SUBS + s, 3 - mate)

    def i_near(s):
        return to(2 * SUBS + s, at(mix, 1, s), at(cmb, 0, s), SUBS + s, 3 - t)

    def i_ag(place, chunk, s, device):
        return to(place * SUBS + s, at(o, chunk, s), at(o, chunk, s), ag_sem(chunk, s), device)

    def got(dst, recv):
        remote(dst, dst, ssem.at[0], rsem.at[recv], {"tensor": mate}).wait_recv()

    def add(dst, *terms):
        total = terms[0][...].astype(F32)
        for term in terms[1:]:
            total = total + term[...].astype(F32)
        dst[...] = total.astype(dst.dtype)

    def start():
        @pl.when(outer)
        def _():
            for build in (o_far, o_near, o_raw):
                for s in subs:
                    build(s).start()

        @pl.when(inner)
        def _():
            for s in subs:
                i_raw(s).start()

    def combine():
        @pl.when(inner)
        def _():
            for slot, chunk, build in ((0, 3 - mate, i_far), (1, 3 - t, i_near)):
                for s in subs:
                    got(at(fwd, slot, s), (2 + slot) * SUBS + s)
                    add(at(mix, slot, s), at(fwd, slot, s), at(x, chunk, s))
                    build(s).start()

    def settle():
        for s in subs:
            got(at(raw, 0, s), s)
            got(at(cmb, 0, s), SUBS + s)
            add(at(o, t, s), at(x, t, s), at(raw, 0, s), at(cmb, 0, s))

            @pl.when(outer)
            def _(s=s):
                o_own(s).start()

            @pl.when(inner)
            def _(s=s):
                i_ag(3, t, s, 3 - t).start()
                i_ag(4, t, s, mate).start()

    def pass_on():
        @pl.when(inner)
        def _():
            for s in subs:
                got(at(o, mate, s), ag_sem(mate, s))
                i_ag(5, mate, s, 3 - t).start()
            for s in subs:
                got(at(o, 3 - t, s), ag_sem(3 - t, s))
                i_ag(6, 3 - t, s, mate).start()
            for s in subs:
                got(at(o, 3 - mate, s), ag_sem(3 - mate, s))
                i_ag(7, 3 - mate, s, mate).start()

    def finish():
        @pl.when(outer)
        def _():
            for chunk in (mate, 3 - mate, 3 - t):
                for s in subs:
                    got(at(o, chunk, s), ag_sem(chunk, s))
            for build in (o_far, o_near, o_raw, o_own):
                for s in subs:
                    build(s).wait_send()

        @pl.when(inner)
        def _():
            for s in subs:
                for build in (i_raw, i_far, i_near):
                    build(s).wait_send()
                i_ag(3, t, s, 3 - t).wait_send()
                i_ag(4, t, s, mate).wait_send()
                i_ag(5, mate, s, 3 - t).wait_send()
                i_ag(6, 3 - t, s, mate).wait_send()
                i_ag(7, 3 - mate, s, mate).wait_send()

    return [start, combine, settle, pass_on, finish]


def relay_scratch(rows, width, dtype):
    part = rows // 2
    return [
        pltpu.VMEM((2 * part, width), dtype),
        pltpu.VMEM((part, width), dtype),
        pltpu.VMEM((part, width), dtype),
        pltpu.SemaphoreType.DMA((5 * SUBS,)),
        pltpu.SemaphoreType.DMA((5 * SUBS,)),
    ]


def relay_sum(t, x, o, scratch):
    taken, mixed, mix, ssem, rsem = scratch
    part = mixed.shape[0]
    piece = part // SUBS
    subs = range(SUBS)
    mate = t + 1 - 2 * (t % 2)
    facing = 3 - t
    outer = (t % 3) == 0
    inner = (t % 3) != 0
    near = t // 2
    far = 1 - near

    def at(ref, chunk, s):
        return ref.at[pl.ds(pl.multiple_of(chunk * part + s * piece, piece), piece)]

    def to(index, src, dst, recv, device):
        return remote(
            src, dst, ssem.at[index], rsem.at[recv], {"tensor": device}
        )

    def give_far(s):
        return to(s, at(x, far, s), at(taken, 0, s), s, mate)

    def give_near(s):
        return to(SUBS + s, at(x, near, s), at(taken, 1, s), SUBS + s, mate)

    def cross(s):
        return to(s, at(mix, 0, s), at(mixed, 0, s), 2 * SUBS + s, facing)

    def own_across(s):
        return to(SUBS + s, at(o, near, s), at(o, near, s), (3 + near) * SUBS + s, facing)

    def own_out(s):
        return to(2 * SUBS + s, at(o, near, s), at(o, near, s), (3 + near) * SUBS + s, mate)

    def far_out(s):
        return to(3 * SUBS + s, at(o, far, s), at(o, far, s), (3 + far) * SUBS + s, mate)

    def got(dst, recv):
        remote(dst, dst, ssem.at[0], rsem.at[recv], {"tensor": mate}).wait_recv()

    def add(dst, *terms):
        total = terms[0][...].astype(F32)
        for term in terms[1:]:
            total = total + term[...].astype(F32)
        dst[...] = total.astype(dst.dtype)

    def start():
        @pl.when(outer)
        def _():
            for build in (give_far, give_near):
                for s in subs:
                    build(s).start()

    def combine():
        @pl.when(inner)
        def _():
            for s in subs:
                got(at(taken, 0, s), s)
                add(at(mix, 0, s), at(taken, 0, s), at(x, far, s))
                cross(s).start()

    def settle():
        @pl.when(inner)
        def _():
            for s in subs:
                got(at(taken, 1, s), SUBS + s)
                got(at(mixed, 0, s), 2 * SUBS + s)
                add(at(o, near, s), at(x, near, s), at(taken, 1, s), at(mixed, 0, s))
                own_across(s).start()
                own_out(s).start()

    def pass_on():
        @pl.when(inner)
        def _():
            for s in subs:
                got(at(o, far, s), (3 + far) * SUBS + s)
                far_out(s).start()

    def finish():
        @pl.when(outer)
        def _():
            for chunk in (near, far):
                for s in subs:
                    got(at(o, chunk, s), (3 + chunk) * SUBS + s)
            for build in (give_far, give_near):
                for s in subs:
                    build(s).wait_send()

        @pl.when(inner)
        def _():
            for build in (cross, own_across, own_out, far_out):
                for s in subs:
                    build(s).wait_send()

    return [start, combine, settle, pass_on, finish]


def params(collective_id, mebibytes):
    return pltpu.CompilerParams(
        collective_id=collective_id,
        has_side_effects=True,
        vmem_limit_bytes=mebibytes * 1024 * 1024,
    )


IN_VMEM = pl.BlockSpec(memory_space=pltpu.VMEM)
IN_HBM = pl.BlockSpec(memory_space=pltpu.HBM)


def plane_scratch(count, rows, width):
    pairs = count // 2
    side = width // 2
    block = rows // pairs
    return [
        pltpu.VMEM((rows, side), BF),
        pltpu.VMEM((rows, side), BF),
        pltpu.VMEM((pairs, block, side), BF),
        pltpu.SemaphoreType.DMA((5, pairs)),
        pltpu.SemaphoreType.DMA((4, pairs)),
    ]


def plane_sum(count, p, x, o, scratch):
    from_mate, paired, slots, ssem, rsem = scratch
    pairs = count // 2
    side = from_mate.shape[1]
    block = slots.shape[1]
    pair = p // 2
    core = p % 2
    mate = {"dp": p + 1 - 2 * core}

    def rows_of(index):
        return pl.ds(pl.multiple_of(index * block, block), block)

    def cols_of(which):
        return pl.ds(pl.multiple_of(which * side, side), side)

    def after(k):
        return (pair + k) % pairs

    def before(k):
        return (pair + pairs - k) % pairs

    def give(k):
        spot = rows_of(after(k))
        return remote(
            x.at[spot, cols_of(1 - core)], from_mate.at[spot], ssem.at[0, k % pairs], rsem.at[0, k % pairs], mate
        )

    def hand(k):
        spot = rows_of(after(k))
        return remote(
            paired.at[spot], slots.at[k], ssem.at[1, k], rsem.at[1, k], {"dp": 2 * after(k) + core}
        )

    def spread(k):
        spot = o.at[rows_of(pair), cols_of(core)]
        return remote(spot, spot, ssem.at[2, k], rsem.at[2, k], {"dp": 2 * after(k) + core})

    def share(k):
        spot = o.at[rows_of(before(k)), cols_of(core)]
        return remote(spot, spot, ssem.at[3, k], rsem.at[3, k], mate)

    def start():
        for k in range(1, pairs + 1):
            give(k).start()

    def pair_up():
        for k in range(1, pairs + 1):
            spot = rows_of(after(k))
            give(k).wait_recv()
            total = x[spot, cols_of(core)].astype(F32) + from_mate[spot].astype(F32)
            paired[spot] = total.astype(BF)
            if k < pairs:
                hand(k).start()

    def settle():
        spot = rows_of(pair)
        total = paired[spot].astype(F32)
        for k in range(1, pairs):
            hand(k).wait_recv()
            total = total + slots[k].astype(F32)
        o[spot, cols_of(core)] = total.astype(BF)
        for k in range(1, pairs):
            spread(k).start()
        share(0).start()

    def pass_on():
        for k in range(1, pairs):
            spot = o.at[rows_of(before(k)), cols_of(core)]
            remote(spot, spot, ssem.at[2, k], rsem.at[2, k], mate).wait_recv()
            share(k).start()

    def finish():
        for k in range(pairs):
            spot = o.at[rows_of(before(k)), cols_of(1 - core)]
            remote(spot, spot, ssem.at[3, k], rsem.at[3, k], mate).wait_recv()
        for k in range(1, pairs + 1):
            give(k).wait_send()
        for k in range(1, pairs):
            hand(k).wait_send()
            spread(k).wait_send()
        for k in range(pairs):
            share(k).wait_send()

    return [start, pair_up, settle, pass_on, finish]


def reduce_scratch(rows, width):
    side = width // 2
    return [
        pltpu.VMEM((rows, side), BF),
        pltpu.VMEM((rows, side), BF),
        pltpu.VMEM((2 * rows, side), BF),
        pltpu.SemaphoreType.DMA((2, 8)),
        pltpu.SemaphoreType.DMA((2, 8)),
    ]


def square_reduce(p, x, kept, matrices, scratch):
    from_mate, paired, taken, ssem, rsem = scratch
    side = from_mate.shape[1]
    pair = p // 2
    core = p % 2
    mate = {"dp": p + 1 - 2 * core}

    def away_from(place, away):
        return {"dp": 2 * (place ^ away) + core}

    def cols_of(which):
        return pl.ds(pl.multiple_of(which * side, side), side)

    def give(m):
        _, first, rows = matrices[m]
        spot = pl.ds(first, rows)
        return remote(x.at[spot, cols_of(1 - core)], from_mate.at[spot], ssem.at[m, 0], rsem.at[m, 0], mate)

    def part_of(m, part):
        _, first, rows = matrices[m]
        return pl.ds(first + part * (rows // 2), rows // 2)

    def slot(m, near, part):
        _, first, rows = matrices[m]
        return pl.ds(2 * first + near * rows + part * (rows // 2), rows // 2)

    def opposite_send(m, part):
        place = matrices[m][0]
        return remote(
            paired.at[part_of(m, part)], taken.at[slot(m, 0, part)],
            ssem.at[m, 1 + part], rsem.at[m, 1], away_from(place, 1 + part),
        )

    def near_raw(m, near):
        part = 1 - near
        return remote(
            paired.at[part_of(m, part)], taken.at[slot(m, near, part)],
            ssem.at[m, 1], rsem.at[m, 2 + 2 * near], away_from(matrices[m][0], 0),
        )

    def near_mixed(m, near):
        part = near
        return remote(
            paired.at[part_of(m, part)], taken.at[slot(m, near, part)],
            ssem.at[m, 2], rsem.at[m, 3 + 2 * near], away_from(matrices[m][0], 0),
        )

    def swap(m):
        spot = kept.at[pl.ds(0, matrices[m][2]), cols_of(core)]
        return remote(spot, spot, ssem.at[m, 6], rsem.at[m, 6], mate)

    def arrived(ref, m, index):
        remote(ref, ref, ssem.at[m, 0], rsem.at[m, index], mate).wait_recv()

    def role(m, away):
        return pl.when(pair == (matrices[m][0] ^ away))

    every = range(len(matrices))

    def start():
        for m in every:
            give(m).start()

    def pair_up():
        for m in every:
            _, first, rows = matrices[m]
            spot = pl.ds(first, rows)
            give(m).wait_recv()
            total = x[spot, cols_of(core)].astype(F32) + from_mate[spot].astype(F32)
            paired[spot] = total.astype(BF)

            @role(m, 3)
            def _(m=m):
                for part in range(2):
                    opposite_send(m, part).start()

            for near in range(2):

                @role(m, 1 + near)
                def _(m=m, near=near):
                    near_raw(m, near).start()

    def mix():
        for m in every:
            for near in range(2):

                @role(m, 1 + near)
                def _(m=m, near=near):
                    piece = slot(m, 0, near)
                    arrived(taken.at[piece], m, 1)
                    spot = part_of(m, near)
                    total = paired[spot].astype(F32) + taken[piece].astype(F32)
                    paired[spot] = total.astype(BF)
                    near_mixed(m, near).start()

    def settle():
        for m in every:

            @role(m, 0)
            def _(m=m):
                _, first, rows = matrices[m]
                for near in range(2):
                    arrived(taken.at[slot(m, near, 1 - near)], m, 2 + 2 * near)
                    arrived(taken.at[slot(m, near, near)], m, 3 + 2 * near)
                spot = pl.ds(first, rows)
                total = x[spot, cols_of(core)].astype(F32) + from_mate[spot].astype(F32)
                for near in range(2):
                    total = total + taken[pl.ds(2 * first + near * rows, rows)].astype(F32)
                kept[pl.ds(0, rows), cols_of(core)] = total.astype(BF)
                swap(m).start()

    def finish():
        for m in every:
            rows = matrices[m][2]
            give(m).wait_send()

            @role(m, 0)
            def _(m=m, rows=rows):
                arrived(kept.at[pl.ds(0, rows), cols_of(1 - core)], m, 6)
                swap(m).wait_send()

            @role(m, 3)
            def _(m=m):
                for part in range(2):
                    opposite_send(m, part).wait_send()

            for near in range(2):

                @role(m, 1 + near)
                def _(m=m, near=near):
                    near_raw(m, near).wait_send()
                    near_mixed(m, near).wait_send()

    return [start, pair_up, mix, settle, finish]


def gather_scratch():
    return [pltpu.SemaphoreType.DMA((4, 2 * CUTS, 4))] * 2


def square_gather(p, sizes, out, own, cuts, scratch):
    ssem, rsem = scratch
    width = out.shape[1]
    pair = p // 2
    core = p % 2
    mate = {"dp": p + 1 - 2 * core}
    firsts = [sum(sizes[:index]) for index in range(4)]

    def piece(index, side, part):
        rows = sizes[index]
        if index == 2:
            across = pl.ds(pl.multiple_of(side * (width // 2), width // 2), width // 2)
            share = rows // (2 * cuts)
            return out.at[pl.ds(firsts[index] + part * share, share), across]
        share = rows // (4 * cuts)
        first = firsts[index] + side * (rows // 2) + part * share
        return out.at[pl.ds(pl.multiple_of(first, share), share)]

    def copy(index, part, route, device):
        spot = piece(index, core, part)
        return remote(spot, spot, ssem.at[index, part, route], rsem.at[index, part, route], device)

    def other(away):
        return {"dp": 2 * (pair + away * (1 - 2 * ((pair // away) % 2))) + core}

    def role(index, away):
        return pl.when(pair == (PLACE[index] ^ away))

    def wait_in(index, part, route, side):
        spot = piece(index, side, part)
        remote(spot, spot, ssem.at[index, part, route], rsem.at[index, part, route], mate).wait_recv()

    ways = ((1, 0, 2), (2, 1, 1))
    parts = 2 * cuts

    def half(which):
        return range(which * cuts, (which + 1) * cuts)

    def start():
        for index in range(4):

            @role(index, 0)
            def _(index=index):
                for part in range(parts):
                    piece(index, core, part)[...] = own(index, part)
                for part in range(parts):
                    copy(index, part, 0, other(1)).start()
                    copy(index, (part + cuts) % parts, 1, other(2)).start()
                for part in range(parts):
                    copy(index, part, 3, mate).start()

    def pass_on(indices=range(4)):
        for index in indices:
            for away, route, onward in ways:

                @role(index, away)
                def _(index=index, away=away, route=route, onward=onward):
                    for part in half(away - 1):
                        wait_in(index, part, route, core)
                        copy(index, part, 2, other(onward)).start()
                        copy(index, part, 3, mate).start()

    def rest():
        for index in LAST_FIRST:
            for away, route, _ in ways:

                @role(index, away)
                def _(index=index, away=away, route=route):
                    for part in half(2 - away):
                        wait_in(index, part, route, core)
                        copy(index, part, 3, mate).start()

            @role(index, 3)
            def _(index=index):
                for part in [part // 2 + cuts * (part % 2) for part in range(parts)]:
                    wait_in(index, part, 2, core)
                    copy(index, part, 3, mate).start()

    def finish(ready=None):
        for index in LAST_FIRST:
            for part in range(parts):
                wait_in(index, part, 3, 1 - core)
            if index == 1 and ready is not None:
                ready()
        for index in range(4):
            for part in range(parts):
                copy(index, part, 3, mate).wait_send()

            @role(index, 0)
            def _(index=index):
                for part in range(parts):
                    copy(index, part, 0, other(1)).wait_send()
                    copy(index, part, 1, other(2)).wait_send()

            for away, _, onward in ways:

                @role(index, away)
                def _(index=index, away=away, onward=onward):
                    for part in half(away - 1):
                        copy(index, part, 2, other(onward)).wait_send()

    return [start, pass_on, rest, finish]


def vector_scratch(count, shape):
    return [
        pltpu.VMEM((count,) + shape, F32),
        pltpu.SemaphoreType.DMA((count,)),
        pltpu.SemaphoreType.DMA((count,)),
    ]


def vector_sum(axis, count, p, v, o, scratch):
    slots, ssem, rsem = scratch

    def send(k):
        return remote(v, slots.at[p], ssem.at[k], rsem.at[k], {axis: (p + k) % count})

    def start():
        slots[p] = v[...]
        for k in range(1, count):
            send(k).start()

    def finish():
        for k in range(1, count):
            spot = slots.at[(p + count - k) % count]
            remote(v, spot, ssem.at[k], rsem.at[k], {axis: (p + k) % count}).wait_recv()
        total = slots[0]
        for k in range(1, count):
            total = total + slots[k]
        o[...] = total
        for k in range(1, count):
            send(k).wait_send()

    return [start, finish]


ROW_STEP = 32


def tdot(left, right):
    return lax.dot_general(left, right, (((0,), (0,)), ((), ())), preferred_element_type=F32)


def dot(left, right):
    return jnp.dot(left, right, preferred_element_type=F32)


def dot_t(left, right):
    return lax.dot_general(left, right, (((1,), (1,)), ((), ())), preferred_element_type=F32)


def cut(values):
    high = values.astype(BF)
    return high, (values - high.astype(F32)).astype(BF)


def dot3(lh, ll, rh, rl, dims=(((1,), (0,)), ((), ()))):
    def dot(left, right):
        return lax.dot_general(left, right, dims, preferred_element_type=F32)

    return dot(lh, rh) + (dot(lh, rl) + dot(ll, rh))


def step_kernel(
    count, sizes,
    seg, rp, hb, fb, mh, mf, x_hbm, cot_hbm, wq_hbm, wo_hbm, wu_hbm, wd_hbm, mq, mo, mu, md,
    y_hbm, gt_hbm, xo_hbm, gall_hbm, vec, totals,
    y, gt, xo, gall, x, cot, f1, f2, f3, f4, wo_f, gx, go, gp, dz1, b1, b2, b3, b4, b5, b6, b7, b8, bt, red_s, kept,
    gap, gbp, wq, wo, q_s, k_s, v_s, ctx_s, dq_s, dk_s, dv_s, p_s, inv1_s, vecp, squares,
    wsem, lsem, psem, osem, *scratch,
):
    p = lax.axis_index("dp")
    t = lax.axis_index("tensor")
    tokens, width = x.shape
    half = tokens // 2
    quarter = tokens // 4
    columns = q_s.shape[1]
    heads = columns // HD
    tile = width // 3
    scale = 1.0 / math.sqrt(HD)
    square = count == 8
    group = count // 4
    share = width // group
    which = p // group
    core = p % 2
    mate = {"dp": p + 1 - 2 * core}
    firsts = [sum(sizes[:index]) for index in range(4)]
    n1_s, slope_s, dz2_s, u_s = (ref.at[pl.ds(0, tokens)] for ref in (f3, f1, f2, f4))
    h1l_s, act_s, du_s, dm_s, da_s, part_s = (
        ref.at[pl.ds(0, tokens)] for ref in (b3, b4, b5, b6, b7, b8)
    )
    wu, wd = b1, b2
    zf, af, sf, xf = f3, f1, f2, f4.at[pl.ds(0, share)]
    ah, al, zh, zl, dh, dl, sh, sl = b1, b2, b3, b4, b5, b6, b7, b8
    gf = kept if square else gall
    loads = [
        pltpu.make_async_copy(source, target, wsem.at[i])
        for i, (source, target) in enumerate(
            (
                (wq_hbm, f4), (wo_hbm, wo_f), (wu_hbm, f1), (wd_hbm, f2),
                (x_hbm, x), (cot_hbm, cot),
            )
        )
    ]
    for place in (0, 4, 1, 2, 3, 5):
        loads[place].start()
    greet(z_peers(t) + [{"dp": (p + k) % count} for k in range(1, count)])
    sums, back = [], []
    for q in range(4):
        place = pl.ds(q * quarter, quarter)
        pieces = scratch[5 * q : 5 * q + 5]
        sums.append(relay_sum(t, part_s.at[place], red_s.at[place], pieces))
        back.append(relay_sum(t, bt.at[place], red_s.at[place], pieces))
    top = 4 * columns
    if square:
        ends = [(PLACE[2], 0, width), (PLACE[3], width, width)]
        plane_b = square_reduce(p, gbp, kept, ends, scratch[20:25])
        ends = [(PLACE[0], 0, 3 * columns), (PLACE[1], 3 * columns, columns)]
        plane_a = square_reduce(p, gap, kept, ends, scratch[25:30])
    else:
        plane_b = plane_sum(count, p, gbp, gall.at[pl.ds(top, 2 * width)], scratch[20:25])
        plane_a = plane_sum(count, p, gap, gall.at[pl.ds(0, top)], scratch[25:30])
    vector = vector_sum("dp", count, p, vecp, vec, scratch[30:33])
    along = vector_sum("tensor", 4, t, squares, totals, scratch[33:36])
    line = line_sum(t, gx, go, scratch[36:42])
    vecp[...] = jnp.zeros_like(vecp)
    lane = lax.broadcasted_iota(jnp.int32, (1, columns), 1)

    def in_head(index):
        return (lane // HD) == index

    def rows_of(h):
        return pl.ds(h * half, half)

    def quarter_of(q):
        return pl.ds(q * quarter, quarter)

    def over_rows(q, body, init=0):
        def step(i, carry):
            first = q * quarter + i * ROW_STEP
            return body(pl.ds(pl.multiple_of(first, ROW_STEP), ROW_STEP), carry)

        return lax.fori_loop(0, quarter // ROW_STEP, step, init)

    def fold(values):
        return values.reshape(ROW_STEP // 8, 8, values.shape[1]).sum(axis=0)

    def add_vec(row, folded):
        vecp[row : row + 1, 0 : folded.shape[1]] += jnp.sum(folded, axis=0, keepdims=True)

    def narrow(index, source, target):
        loads[index].wait()
        target[...] = source[...].astype(BF)

    def attention(h):
        r = rows_of(h)
        xb = x[r]
        q = (dot_t(xb, wq[0 * columns : 1 * columns]) + hb[0:1]).astype(BF)
        k = dot_t(xb, wq[1 * columns : 2 * columns]).astype(BF)
        v = (dot_t(xb, wq[2 * columns : 3 * columns]) + hb[1:2]).astype(BF)
        q_s[r], k_s[r], v_s[r] = q, k, v
        down = jnp.broadcast_to(seg[h : h + 1].astype(F32), (half, half))
        same = down == down.T

        def one_head(index, context):
            mine = jnp.where(in_head(index), q, jnp.zeros_like(q))
            scores = jnp.where(same, dot_t(mine, k) * scale, -1e30)
            expo = jnp.exp(scores - jnp.max(scores, axis=-1, keepdims=True))
            probs = expo / jnp.sum(expo, axis=-1, keepdims=True)
            p_s[h * heads + index] = probs
            return jnp.where(in_head(index), dot(probs.astype(BF), v), context)

        context = lax.fori_loop(0, heads, one_head, jnp.zeros((half, columns), F32))
        low = context.astype(BF)
        ctx_s[r] = low
        part_s[r] = dot(low, wo[...]).astype(BF)

    def up(q):
        def norm(r, carry):
            z = x[r].astype(F32) + red_s[r].astype(F32) + rp[0:1]
            center = z - jnp.mean(z, axis=-1, keepdims=True)
            inverse = lax.rsqrt(jnp.mean(center * center, axis=-1, keepdims=True) + EPS_NORM)
            normed = center * inverse
            n1_s[r] = normed
            inv1_s[r] = jnp.broadcast_to(inverse, (ROW_STEP, 128))
            h1l_s[r] = (normed * rp[2:3] + rp[3:4]).astype(BF)
            return carry

        over_rows(q, norm)
        u_s[quarter_of(q)] = dot(h1l_s[quarter_of(q)], wu[...])

        def gelu(r, carry):
            u = u_s[r] + fb[...].reshape(1, width)
            cdf = 0.5 * (1.0 + lax.erf(u * (1.0 / math.sqrt(2.0))))
            act_s[r] = (u * cdf).astype(BF)
            slope_s[r] = cdf + u * jnp.exp(-0.5 * u * u) * (1.0 / math.sqrt(2.0 * math.pi))
            return carry

        over_rows(q, gelu)

    def down(q):
        r = quarter_of(q)
        part_s[r] = dot(act_s[r], wd[...]).astype(BF)

    def out_back(q):
        def norm(r, carry):
            s_dz2, s_dyn, s_dy = carry
            h1 = n1_s[r] * rp[2:3] + rp[3:4]
            z = h1 + red_s[r].astype(F32) + rp[1:2]
            center = z - jnp.mean(z, axis=-1, keepdims=True)
            inverse = lax.rsqrt(jnp.mean(center * center, axis=-1, keepdims=True) + EPS_NORM)
            normed = center * inverse
            y[r] = (normed * rp[4:5] + rp[5:6]).astype(BF)
            dy = cot[r].astype(F32)
            scaled = dy * rp[4:5]
            first = jnp.mean(scaled, axis=-1, keepdims=True)
            second = jnp.mean(scaled * normed, axis=-1, keepdims=True)
            dz2 = inverse * (scaled - first - normed * second)
            dz2_s[r] = dz2
            dm_s[r] = dz2.astype(BF)
            return s_dz2 + fold(dz2), s_dyn + fold(dy * normed), s_dy + fold(dy)

        zero = jnp.zeros((8, width), F32)
        for row, total in zip((1, 4, 5), over_rows(q, norm, (zero, zero, zero))):
            add_vec(row, total)
        u_s[quarter_of(q)] = dot_t(dm_s[quarter_of(q)], wd[...])

        def slope(r, carry):
            du = (u_s[r] * slope_s[r]).astype(BF)
            du_s[r] = du
            return carry + fold(du.astype(F32))

        add_vec(6, over_rows(q, slope, zero))

    def up_back(q):
        r = quarter_of(q)
        part_s[r] = dot_t(du_s[r], wu[...]).astype(BF)

    def grads_b():
        gbp[0:width] = tdot(h1l_s[...], du_s[...]).astype(BF)
        gbp[width : 2 * width] = tdot(act_s[...], dm_s[...]).astype(BF)

    def norm_back(q):
        def norm(r, carry):
            s_dz1, s_dhn, s_dh = carry
            dh1 = red_s[r].astype(F32) + dz2_s[r]
            normed = n1_s[r]
            scaled = dh1 * rp[2:3]
            first = jnp.mean(scaled, axis=-1, keepdims=True)
            second = jnp.mean(scaled * normed, axis=-1, keepdims=True)
            grad = inv1_s[r][:, 0:1] * (scaled - first - normed * second)
            dz1[r] = grad
            da_s[r] = grad.astype(BF)
            return s_dz1 + fold(grad), s_dhn + fold(dh1 * normed), s_dh + fold(dh1)

        zero = jnp.zeros((8, width), F32)
        for row, total in zip((0, 2, 3), over_rows(q, norm, (zero, zero, zero))):
            add_vec(row, total)

    def attention_back(h):
        r = rows_of(h)
        dc = dot_t(da_s[r], wo[...]).astype(BF)
        q, k, v = q_s[r], k_s[r], v_s[r]

        def one_head(index, carry):
            dq, dk, dv = carry
            probs = p_s[h * heads + index]
            mine = jnp.where(in_head(index), dc, jnp.zeros_like(dc))
            dp = dot_t(mine, v)
            ds = (probs * (dp - jnp.sum(probs * dp, axis=-1, keepdims=True))).astype(BF)
            dv = jnp.where(in_head(index), tdot(probs.astype(BF), dc), dv)
            dq = jnp.where(in_head(index), dot(ds, k), dq)
            dk = jnp.where(in_head(index), tdot(ds, q), dk)
            return dq, dk, dv

        dq, dk, dv = lax.fori_loop(0, heads, one_head, (jnp.zeros((half, columns), F32),) * 3)
        dq = (dq * scale).astype(BF)
        dk = (dk * scale).astype(BF)
        dv = dv.astype(BF)
        dq_s[r], dk_s[r], dv_s[r] = dq, dk, dv
        add_vec(7, jnp.sum(dq.astype(F32), axis=0, keepdims=True))
        add_vec(8, jnp.sum(dv.astype(F32), axis=0, keepdims=True))

    def grads_a():
        for i, source in enumerate((dq_s, dk_s, dv_s)):
            gap[i * columns : (i + 1) * columns] = tdot(source[...], x[...]).astype(BF)
        gap[3 * columns : 4 * columns] = tdot(ctx_s[...], da_s[...]).astype(BF)

    def back_terms(h):
        r = rows_of(h)
        total = dot(dq_s[r], wq[0 * columns : 1 * columns]) + dot(dk_s[r], wq[1 * columns : 2 * columns]) + dot(dv_s[r], wq[2 * columns : 3 * columns])
        bt[r] = total.astype(BF)

    def moment_copy(index):
        moment = (mq, mo, mu, md)[index]
        return pltpu.make_async_copy(moment, f1.at[pl.ds(0, sizes[index])], lsem.at[0])

    def fetch_moment():
        for index in range(4):
            pl.when(which == PLACE[index])(moment_copy(index).start)

    def cols(index):
        return pl.ds(pl.multiple_of(index * tile, tile), tile)

    def place_of(side, j):
        return side * (1 + j // 2), j + side * (1 - j // 2)

    def gram(indices):
        for index in indices:
            rows = sizes[index]
            first = 0 if square else firsts[index]

            @pl.when(which == PLACE[index])
            def _(index=index, first=first, rows=rows):
                moment_copy(index).wait()
                for i in range(3):
                    spot = pl.ds(i * (rows // 3), rows // 3)
                    z = 0.5 * f1[spot] + gf[pl.ds(first + i * (rows // 3), rows // 3)].astype(F32)
                    if index == 2:
                        z = z.T
                        spot = (pl.ds(0, width), spot)
                    zf[spot] = z
                    zh[spot], zl[spot] = cut(z)
                if rows < width:
                    spot = pl.ds(rows, width - rows)
                    zf[spot] = jnp.zeros((width - rows, width), F32)
                    zh[spot] = jnp.zeros((width - rows, width), BF)
                    zl[spot] = jnp.zeros((width - rows, width), BF)

        over = (((0,), (0,)), ((), ()))

        @pl.loop(0, 3)
        def _(j):
            row, col = place_of(core, j)
            gx[:, cols(j)] = dot3(
                zh[:, cols(row)], zl[:, cols(row)], zh[:, cols(col)], zl[:, cols(col)], over
            )

    diagonal = lax.broadcasted_iota(jnp.int32, (tile, tile), 0) == lax.broadcasted_iota(
        jnp.int32, (tile, tile), 1
    )

    def upper():
        def trace(block):
            return jnp.sum(jnp.where(diagonal, block, 0.0))

        def write(rows, across, value):
            af[rows, across] = value
            ah[rows, across], al[rows, across] = cut(value)

        last = jnp.where(core == 1, go[:, 2 * tile :], gp[:, 2 * tile :])
        total = trace(go[:, 0:tile]) + trace(gp[:, 0:tile]) + trace(last)
        inverse = 1.0 / (jnp.sqrt(jnp.full((1, 1), total, F32)) + 1e-07)
        shrink = inverse * inverse
        for source, side in ((go, core), (gp, 1 - core)):
            for j in range(3):
                row, col = place_of(side, j)
                block = source[:, j * tile : (j + 1) * tile] * shrink
                write(cols(row), cols(col), block)
                if j > 0:
                    write(cols(col), cols(row), block.T)

        if square:
            for index, rows in enumerate(sizes):

                @pl.when(which == PLACE[index])
                def _(half_rows=rows // 2):
                    mine = pl.ds(pl.multiple_of(core * half_rows, half_rows), half_rows)
                    xf[0:half_rows] = zf[mine] * inverse
                    if half_rows < share:
                        xf[half_rows:share] = jnp.zeros((share - half_rows, width), F32)

        else:
            rank = p % group
            xf[...] = zf[pl.ds(pl.multiple_of(rank * share, share), share)] * inverse

    def product(left, right, base, base_scale, factor, targets, times):
        (lh, ll), (rh, rl) = left, right
        for i in range(3):
            rows = pl.ds(i * tile, tile)
            for j in range(i, 3):
                across = pl.ds(j * tile, tile)
                value = base_scale * base[rows, across] + factor * times(
                    lh[rows], ll[rows], rh[:, across], rl[:, across]
                )
                parts = (*cut(value), value)
                for target, part in zip(targets, parts):
                    target[rows, across] = part
                if i != j and len(targets) == 2:
                    for target, part in zip(targets, parts):
                        target[across, rows] = part.T
                elif i != j:
                    mirrored = value.T
                    for target, part in zip(targets, (*cut(mirrored), mirrored)):
                        target[across, rows] = part

    def make_d(times=dot3):
        product((ah, al), (ah, al), af, coef_b, coef_c, (dh, dl), times)

    def move_x(times=dot3):
        xh, xl = cut(xf[...])
        xf[...] = coef_a * xf[...] + times(xh, xl, dh[...], dl[...])

    def own_gradient(index, part):
        if index == 2:
            across = pl.ds(pl.multiple_of(core * (width // 2), width // 2), width // 2)
            piece = sizes[index] // (2)
            return gf[pl.ds(part * piece, piece), across]
        piece = sizes[index] // (4)
        first = pl.multiple_of(core * (sizes[index] // 2) + part * piece, piece)
        return gf[pl.ds(first, piece)]

    def own_step(index, part):
        if index == 2:
            piece = sizes[index] // (2 * CUTS)
            return xf[:, pl.ds(part * piece, piece)].T.astype(BF)
        piece = sizes[index] // (4 * CUTS)
        return xf[pl.ds(part * piece, piece)].astype(BF)

    if square:
        spread = square_gather(p, sizes, gall, own_gradient, 1, scratch[42:44])
        collect = square_gather(p, sizes, xo, own_step, CUTS, scratch[44:46])
        early = (which == PLACE[2]) | (which == PLACE[3])
        late = (which == PLACE[0]) | (which == PLACE[1])

    start, mix, settle, pass_on, end = (
        (lambda q, place=place: sums[q][place]()) for place in range(5)
    )

    def round_trip(first, second):
        end(0), first(0), pass_on(1), second(0), settle(2), mix(3), start(0)
        end(1), first(1), pass_on(2), settle(3), second(1), mix(0), start(1)
        end(2), first(2), pass_on(3), second(2), settle(0), mix(1), start(2)
        end(3), first(3), pass_on(0), second(3), settle(1), mix(2), start(3)

    loads[4].wait()
    narrow(0, f4, wq)
    narrow(1, wo_f, wo)
    attention(0)
    start(0), start(1)
    attention(1)
    mix(0), start(2), mix(1), settle(0), start(3)
    narrow(2, f1, wu)
    mix(2), settle(1), pass_on(0)
    narrow(3, f2, wd)
    loads[5].wait()
    outs = [
        pltpu.make_async_copy(source, target, osem.at[i])
        for i, (source, target) in enumerate(((y, y_hbm), (gt, gt_hbm), (gall, gall_hbm)))
    ]
    round_trip(up, down)
    round_trip(out_back, up_back)
    outs[0].start()
    fetch_moment()
    grads_b()
    plane_b[0]()
    end(0), norm_back(0), pass_on(1), settle(2), mix(3)
    plane_b[1]()
    end(1), norm_back(1), pass_on(2), settle(3)
    attention_back(0)
    end(2), norm_back(2), pass_on(3)
    if square:
        plane_b[2]()
    end(3), norm_back(3)
    attention_back(1)
    grads_a()
    plane_a[0]()
    vector[0]()
    if square:
        plane_b[3]()
        plane_a[1]()

        @pl.when(early)
        def _():
            plane_b[4]()
            gram((2, 3))
            line[0]()

        plane_a[2]()
        back_terms(0)
        back_terms(1)

        @pl.when(late)
        def _():
            plane_a[3]()
            plane_b[4]()
            plane_a[4]()
            gram((0, 1))
            line[0]()
            spread[0]()

    else:
        plane_b[2]()
        plane_a[1]()
        back_terms(0)
        back_terms(1)
        plane_b[3]()
        plane_a[2]()
        plane_b[4]()
        plane_a[3]()
        plane_a[4]()
        gram(range(4))
        line[0]()
    vector[1]()
    moved = 0.5 * mh[...] + vec[7:9, 0:columns]
    squares[0:2] = jnp.broadcast_to(jnp.sum(moved * moved, axis=1, keepdims=True), (2, 128))
    moved = 0.5 * mf[...].reshape(1, width) + vec[6:7]
    squares[2:3] = jnp.broadcast_to(jnp.sum(moved * moved, axis=1, keepdims=True), (1, 128))
    squares[3:8] = jnp.zeros((5, 128), F32)
    along[0]()
    if square:
        pl.when(early)(spread[0])
    for place in range(1, 5):
        line[place]()
        if square and place == 2:
            spread[1]()
    swap = remote(go, gp, psem.at[0], psem.at[1], mate)
    swap.start()
    for q in range(2):
        back[q][0]()
    swap.wait()

    upper()

    def one_pass(lh, ll, rh, rl):
        return dot(lh, rh)

    plan = {
        (0, 1): ((1, 0),),
        (0, 2): ((1, 1), (0, 2)),
        (1, 0): ((2, 0), (0, 3)),
        (1, 1): ((2, 1), (1, 2)),
        (1, 2): ((3, 0), (1, 3)),
        (2, 1): ((3, 1), (2, 2)),
        (2, 2): ((2, 3),),
        (3, 0): ((3, 2),),
        (3, 1): ((3, 3),),
    }

    def between(k, place):
        for turn in range(4):
            actions = plan.get((turn, place), ())
            if actions:

                @pl.when(k == turn)
                def _(turn=turn, actions=actions):
                    for action, q in actions:
                        back[q][action]()
                    if square and (turn, place) == (1, 2):
                        spread[2]()

    def sweep(k, carry):
        make_d()
        xh, xl = cut(xf[...])
        xf[...] = coef_a * xf[...] + dot(xh, dh[...])

        @pl.when(k == 3)
        def _():
            xf[...] += dot(xh, dl[...]) + dot(xl, dh[...])

        between(k, 0)
        product((ah, al), (dh, dl), af, coef_a, 1.0, (sh, sl, sf), dot3)
        between(k, 1)
        product((sh, sl), (dh, dl), sf, coef_a, 1.0, (ah, al, af), dot3)
        between(k, 2)
        return carry

    lax.fori_loop(0, 4, sweep, 0)
    if square:
        collect[1]((2, 3))
    make_d()
    move_x()
    for q in range(4):
        back[q][4]()
    gt[...] = (red_s[...].astype(F32) + dz1[...]).astype(BF)
    outs[1].start()
    along[1]()
    if square:

        @pl.when(early)
        def _():
            plane_a[4]()

        collect[0]()
        collect[1]((1, 0))
        spread[3]()
        outs[2].start()
        collect[2]()
        rest = pl.ds(sizes[0], sum(sizes[1:]))
        most = pltpu.make_async_copy(xo.at[rest], xo_hbm.at[rest], osem.at[4])
        collect[3](most.start)
        first = pl.ds(0, sizes[0])
        last = pltpu.make_async_copy(xo.at[first], xo_hbm.at[first], osem.at[3])
        last.start()
        most.wait()
    else:
        outs[2].start()
        gather_any(p, core, count // 2, mate, xf, xo, scratch[42], scratch[43])
        last = pltpu.make_async_copy(xo, xo_hbm, osem.at[3])
        last.start()
    for moving in (*outs, last):
        moving.wait()


def gather_any(p, core, pairs, mate, xf, xo, asem_s, asem_r):
    pair = p // 2
    share = xf.shape[0]

    def rows_of(device):
        return xo.at[pl.ds(pl.multiple_of(device * share, share), share)]

    def after(k):
        return 2 * ((pair + k) % pairs) + core

    def before(k):
        return 2 * ((pair + pairs - k) % pairs) + core

    def send(k):
        return remote(rows_of(p), rows_of(p), asem_s.at[0, k], asem_r.at[0, k], {"dp": after(k)})

    def hand(k):
        spot = rows_of(before(k))
        return remote(spot, spot, asem_s.at[1, k], asem_r.at[1, k], mate)

    xo[pl.ds(pl.multiple_of(p * share, share), share)] = xf[...].astype(BF)
    for k in range(1, pairs):
        send(k).start()
    hand(0).start()
    for k in range(1, pairs):
        spot = rows_of(before(k))
        remote(spot, spot, asem_s.at[0, k], asem_r.at[0, k], mate).wait_recv()
        hand(k).start()
    for k in range(pairs):
        spot = rows_of(before(k) + 1 - 2 * core)
        remote(spot, spot, asem_s.at[1, k], asem_r.at[1, k], mate).wait_recv()
    for k in range(1, pairs):
        send(k).wait_send()
    for k in range(pairs):
        hand(k).wait_send()


def step(count, tokens, cotangent, segments, small, weights, moments, collective_id):
    rows, width = tokens.shape
    sizes = tuple(moment.shape[0] for moment in moments)
    columns = sizes[1]
    heads = columns // HD
    half = rows // 2
    tile = width // 3
    square = count == 8

    def low(*shape):
        return pltpu.VMEM(shape, BF)

    def full(*shape):
        return pltpu.VMEM(shape, F32)

    def out(shape, dtype):
        return jax.ShapeDtypeStruct(shape, dtype)

    plane = reduce_scratch if square else functools.partial(plane_scratch, count)
    pair_sems = [pltpu.SemaphoreType.DMA((2, count // 2))] * 2
    steps_rows = sum(sizes) if square else 4 * width
    scratch = (
        [low(rows, width)] * 2
        + [low(steps_rows, width), low(sum(sizes), width)]
        + [low(rows, width)] * 2
        + [full(width, width)] * 3
        + [full(3 * columns, width), full(columns, width)]
        + [full(tile, width)] * 3
        + [full(rows, width)]
        + [low(width, width)] * 8
        + [low(rows, width)] * 2
        + [low(width, width) if square else low(16, width)]
        + [low(4 * columns, width), low(2 * width, width)]
        + [low(3 * columns, width), low(columns, width)]
        + [low(rows, columns)] * 7
        + [full(2 * heads, half, half), full(rows, 128), full(16, width), full(8, 128)]
        + [pltpu.SemaphoreType.DMA((n,)) for n in (6, 2, 2, 5)]
        + relay_scratch(rows // 4, width, BF) * 4
        + plane(2 * width, width)
        + plane(4 * columns, width)
        + vector_scratch(count, (16, width))
        + vector_scratch(4, (8, 128))
        + line_scratch(tile, width, F32)
        + (gather_scratch() * 2 if square else pair_sems)
    )
    return pl.pallas_call(
        functools.partial(step_kernel, count, sizes),
        out_shape=(
            out((rows, width), BF),
            out((rows, width), BF),
            out((steps_rows, width), BF),
            out((sum(sizes), width), BF),
            out((16, width), F32),
            out((8, 128), F32),
        ),
        in_specs=[IN_VMEM] * 6 + [IN_HBM] * 10,
        out_specs=(IN_HBM,) * 4 + (IN_VMEM,) * 2,
        scratch_shapes=scratch,
        compiler_params=params(collective_id, 61),
        name="step",
    )(segments, *small, tokens, cotangent, *weights, *moments)


def apply_kernel(factors, *refs):
    ins, outs = refs[:26], refs[26:]
    small_in, small_out = ins[18:], outs[14:]
    for index, factor in enumerate(factors):
        weight, moment, grad, step = (ins[4 * index + i] for i in range(4))
        new_moment, new, low = (outs[3 * index + i] for i in range(3))
        new_moment[...] = 0.5 * moment[...] + grad[...].astype(F32)
        value = weight[...] - factor * step[...].astype(F32)
        new[...] = value
        low[...] = value.astype(BF)
    for source, target in zip(ins[16:18], outs[12:14]):
        target[...] = source[...]

    @pl.when(pl.program_id(0) == 0)
    def _():
        vec, totals, heads, ff, rows, mom_heads, mom_ff, mom_rows = small_in
        columns = heads.shape[1]
        wide = ff.shape[0]
        moment = 0.5 * mom_heads[...] + vec[7:9, 0:columns]
        small_out[0][...] = moment
        scale = lax.rsqrt(totals[0:2, 0:1] * (1.0 / (4 * columns)) + 1e-06)
        small_out[1][...] = heads[...] - 0.1 * moment * scale
        moment = 0.5 * mom_ff[...].reshape(1, wide) + vec[6:7]
        small_out[2][...] = moment.reshape(wide)
        scale = lax.rsqrt(totals[2:3, 0:1] * (1.0 / (4 * wide)) + 1e-06)
        value = ff[...].reshape(1, wide) - 0.1 * moment * scale
        small_out[3][...] = value.reshape(wide)
        moment = 0.5 * mom_rows[...] + vec[0:6]
        small_out[4][...] = moment
        mean = jnp.mean(moment * moment, axis=-1, keepdims=True)
        small_out[5][...] = rows[...] - 0.1 * moment * lax.rsqrt(mean + 1e-06)


APPLY_STEPS = 4


def apply(sizes, factors, weights, moments, grads, steps, passed, small):
    width = grads.shape[1]
    in_specs, operands, out_specs, out_shape = [], [], [], []

    def block(rows, first=0):
        share = rows // APPLY_STEPS
        return pl.BlockSpec((share, width), lambda i, skip=first // share: (skip + i, 0))

    def whole(array):
        return pl.BlockSpec(array.shape, lambda i, n=array.ndim: (0,) * n)

    first = 0
    for rows, weight, moment in zip(sizes, weights, moments):
        in_specs += [block(rows), block(rows), block(rows, first), block(rows, first)]
        operands += [weight, moment, grads, steps]
        out_specs += [block(rows)] * 3
        out_shape += [jax.ShapeDtypeStruct((rows, width), kind) for kind in (F32, F32, BF)]
        first += rows
    for array in passed:
        turn = pl.BlockSpec((array.shape[0] // 4, width), lambda i: (i // (APPLY_STEPS // 4), 0))
        in_specs.append(turn)
        operands.append(array)
        out_specs.append(turn)
        out_shape.append(jax.ShapeDtypeStruct(array.shape, array.dtype))
    for array in small:
        in_specs.append(whole(array))
        operands.append(array)
    for array in small[2:5]:
        for _ in range(2):
            out_specs.append(whole(array))
            out_shape.append(jax.ShapeDtypeStruct(array.shape, F32))
    return pl.pallas_call(
        functools.partial(apply_kernel, factors),
        grid=(APPLY_STEPS,),
        out_shape=tuple(out_shape),
        in_specs=in_specs,
        out_specs=tuple(out_specs),
        compiler_params=pltpu.CompilerParams(vmem_limit_bytes=61 * 1024 * 1024),
        name="apply",
    )(*operands)


def vector_step(param, moment, mean_sq):
    return param - 0.1 * moment * lax.rsqrt(mean_sq + 1e-06)


def local(
    tokens, segments, cotangent,
    w_qkv, w_out, w_up, w_down, head_bias, ff_bias, row_params,
    mom_qkv, mom_out, mom_up, mom_down, mom_heads, mom_ff, mom_params,
):
    width = tokens.shape[1]
    columns = w_qkv.shape[2]
    ff_cols = w_up.shape[1]
    tensor_size = lax.axis_size("tensor")
    count = lax.axis_size("dp")
    qkv_rows = 3 * columns
    wq_rows = w_qkv.transpose(0, 2, 1).reshape(qkv_rows, width)
    moments = (mom_qkv.transpose(0, 2, 1).reshape(qkv_rows, width), mom_out, mom_up, mom_down)
    output_rows, grad_inputs, steps, grads, vector_total, totals = step(
        count, tokens, cotangent, segments, (row_params, head_bias, ff_bias, mom_heads, mom_ff),
        (wq_rows, w_out, w_up, w_down), moments, 1,
    )

    def to_qkv(rows):
        return rows.reshape(3, columns, width).transpose(0, 2, 1)

    bounds = (0, qkv_rows, qkv_rows + columns, qkv_rows + columns + width)

    def grad_of(index, rows):
        return grads[bounds[index] : bounds[index] + rows].astype(F32)

    def step_of(index, rows):
        first = PLACE[index] * width
        part = steps[first : first + rows].astype(F32)
        return part.T if index == 2 else part

    wide = math.sqrt(ff_cols * tensor_size / width)
    if count == 8:
        sizes = (qkv_rows, columns, width, ff_cols)
        factors = (0.8 * math.sqrt(3.0), 0.8, 0.8 * wide, 0.8 * wide)
        done = apply(
            sizes, factors, (wq_rows, w_out, w_up, w_down), moments, grads, steps, (output_rows, grad_inputs),
            (
                vector_total, totals, head_bias, ff_bias, row_params,
                mom_heads, mom_ff, mom_params,
            ),
        )
        qkv_new = [rows.reshape(3, columns, width).transpose(0, 2, 1) for rows in done[0:3]]
        return (
            *done[12:14], *qkv_new, *done[3:12], *done[14:20],
        )

    new_mom_heads = 0.5 * mom_heads + vector_total[7:9, :columns]
    new_mom_ff = 0.5 * mom_ff + vector_total[6]
    new_mom_params = 0.5 * mom_params + vector_total[0:6]
    new_mom_qkv = 0.5 * mom_qkv + to_qkv(grad_of(0, qkv_rows))
    new_mom_out = 0.5 * mom_out + grad_of(1, columns)
    new_mom_up = 0.5 * mom_up + grad_of(2, width)
    new_mom_down = 0.5 * mom_down + grad_of(3, ff_cols)
    new_qkv = w_qkv - 0.8 * math.sqrt(3.0) * to_qkv(step_of(0, qkv_rows))
    new_out = w_out - 0.8 * step_of(1, columns)
    new_up = w_up - 0.8 * wide * step_of(2, width)
    new_down = w_down - 0.8 * wide * step_of(3, ff_cols)
    new_heads = vector_step(head_bias, new_mom_heads, totals[0:2, 0:1] / (columns * tensor_size))
    new_ff = vector_step(ff_bias, new_mom_ff, totals[2, 0] / (ff_cols * tensor_size))
    new_params = vector_step(
        row_params,
        new_mom_params,
        jnp.mean(new_mom_params * new_mom_params, axis=-1, keepdims=True),
    )
    return (
        output_rows,
        grad_inputs,
        new_mom_qkv, new_qkv, new_qkv.astype(BF),
        new_mom_out, new_out, new_out.astype(BF),
        new_mom_up, new_up, new_up.astype(BF),
        new_mom_down, new_down, new_down.astype(BF),
        new_mom_heads, new_heads,
        new_mom_ff, new_ff,
        new_mom_params, new_params,
    )


def solution(mesh):
    placed = (
        P("dp", None), P("dp", None), P("dp", None),
        P(None, None, "tensor"), P("tensor", None), P(None, "tensor"), P("tensor", None),
        P(None, "tensor"), P("tensor"), P(),
        P(None, None, "tensor"), P("tensor", None), P(None, "tensor"), P("tensor", None),
        P(None, "tensor"), P("tensor"), P(),
    )
    triple = ((P(None, None, "tensor"),) * 3, (P("tensor", None),) * 3, (P(None, "tensor"),) * 3)
    return jax.shard_map(
        local,
        mesh=mesh,
        in_specs=placed,
        out_specs=(
            (P("dp", None), P("dp", None))
            + triple[0] + triple[1] + triple[2] + triple[1]
            + (P(None, "tensor"), P(None, "tensor"), P("tensor"), P("tensor"), P(), P())
        ),
        check_vma=False,
    )
```
